32 devices in a mesh: dp: 8 (over z, x), tensor: 4 (over y, core).
Axes of the slice: x: 2, y: 2, z: 4, core: 2. Of those that a mesh axis runs over, the one named last changes fastest.
Arguments:
- tokens: bfloat16 [24576, 768], P('dp'), may hold values from -6 to 6
- token_mask: int32 [24576], P('dp'), may hold values from 0 to 1, as said below
- masked_flags: int32 [24576], P('dp'), may hold values 0 or 1
- doc_lengths: int32 [96], P('dp'), may hold values from 0 to 2048, as said below
- mask_embedding: bfloat16 [768], replicated, may hold values from -6 to 6
- ln1_gain: bfloat16 [768], replicated, may hold values from 0.5 to 1.5
- ln1_bias: bfloat16 [768], replicated, may hold values from -0.625 to 0.625
- w_query: bfloat16 [768, 768], P(None, 'tensor'), may hold values from -0.21875 to 0.21875
- query_bias: bfloat16 [768], P('tensor'), may hold values from -1.75 to 1.75
- w_key: bfloat16 [768, 768], P(None, 'tensor'), may hold values from -0.21875 to 0.21875
- w_value: bfloat16 [768, 768], P(None, 'tensor'), may hold values from -0.21875 to 0.21875
- value_bias: bfloat16 [768], P('tensor'), may hold values from -0.3125 to 0.3125
- w_out: bfloat16 [768, 768], P('tensor'), may hold values from -3.5 to 3.5
- out_bias: bfloat16 [768], replicated, may hold values from -1.25 to 1.25
- ln2_gain: bfloat16 [768], replicated, may hold values from 0.5 to 1.5
- ln2_bias: bfloat16 [768], replicated, may hold values from -0.625 to 0.625
- w_up: bfloat16 [768, 3072], P(None, 'tensor'), may hold values from -0.21875 to 0.21875
- up_bias: bfloat16 [3072], P('tensor'), may hold values from -0.625 to 0.625
- w_down: bfloat16 [3072, 768], P('tensor'), may hold values from -0.21875 to 0.21875
- down_bias: bfloat16 [768], replicated, may hold values from -1.25 to 1.25
- cotangent: bfloat16 [24576, 768], P(('dp', 'tensor')), may hold values from -6 to 6
Outputs:
- layer_output: bfloat16 [24576, 768], P(('dp', 'tensor'))
- input_grad: float32 [24576, 768], P(('dp', 'tensor'))
- grad_mask_embedding: float32 [768], replicated
- grad_ln1_gain: float32 [768], replicated
- grad_ln1_bias: float32 [768], replicated
- grad_w_query: float32 [768, 768], P('dp', 'tensor')
- grad_query_bias: float32 [768], replicated
- grad_w_key: float32 [768, 768], P('dp', 'tensor')
- grad_w_value: float32 [768, 768], P('dp', 'tensor')
- grad_value_bias: float32 [768], replicated
- grad_w_out: float32 [768, 768], P('tensor', 'dp')
- grad_out_bias: float32 [768], replicated
- grad_ln2_gain: float32 [768], replicated
- grad_ln2_bias: float32 [768], replicated
- grad_w_up: float32 [768, 3072], P('dp', 'tensor')
- grad_up_bias: float32 [3072], replicated
- grad_w_down: float32 [3072, 768], P('tensor', 'dp')
- grad_down_bias: float32 [768], replicated
The draws below stay inside these ranges and needn't reach their ends.
Inputs may be any that keep to these rules, and one draw needn't show every extreme that they name: `doc_lengths`: within each index of dp the 12 entries are the lengths of consecutive documents starting at its first token; they sum to 3072; entries after the last document are 0; some document in every draw has exactly 2048 tokens. `token_mask`: within each group of 3072 tokens the real tokens lie in a leading stretch whose length differs from group to group, from about 3/10 of 3072 to all of it; every token after the stretch is padding, and about one token in 20 inside it is padding too.
All inputs are finite; a program needn't handle non-finite values. No bound on the sum of `masked_flags` on one device may be relied on, other than what follows from the above.
Results may differ from the reference program's by a relative error of at most 0.019.
Values may be sent and summed in bfloat16 or wider, within the bound.
A program may use at most 192 MiB of HBM per device.

```python
import math
import jax
import jax.numpy as jnp
from jax import lax

D = 768
H = 12
HD = 64
FF = 3072
TOK_DEV = 3072
MIN_DOC = 256
MAX_DOC = 2048
TOKENS = 24576
SLOTS = 12


def draw_doc_lengths(key, part):
    key = jax.random.fold_in(key, 7)
    group_count = TOKENS // TOK_DEV
    length_key, pick_key = jax.random.split(key)
    drawn_lengths = jax.random.randint(length_key, (group_count, SLOTS), MIN_DOC, MAX_DOC + 1)
    chosen = jax.random.randint(pick_key, (), 0, group_count)
    first_slot = jnp.arange(SLOTS)[None, :] == 0
    chosen_group = jnp.arange(group_count)[:, None] == chosen
    drawn_lengths = jnp.where(first_slot & chosen_group, MAX_DOC, drawn_lengths).astype(jnp.int32)
    starts = jnp.cumsum(drawn_lengths, axis=1).astype(jnp.int32) - drawn_lengths
    lengths = jnp.clip(TOK_DEV - starts, 0, drawn_lengths)
    return lengths.reshape(-1).astype(jnp.int32)


def draw_token_mask(key, part):
    key = jax.random.fold_in(key, 11)
    group_count = TOKENS // TOK_DEV
    count_key, coin_key = jax.random.split(key)
    least_live = 3 * TOK_DEV // 10
    live_counts = jax.random.randint(count_key, (group_count, 1), least_live, TOK_DEV + 1)
    coins = jax.random.randint(coin_key, (group_count, TOK_DEV), 0, 20)
    positions = jnp.arange(TOK_DEV, dtype=jnp.int32)[None, :]
    live = (positions < live_counts) & (coins != 0)
    return live.astype(jnp.int32).reshape(-1)


def touch_ends(result, rng, low, largest):
    place = [jax.random.randint(jax.random.fold_in(rng, axis), (), 0, length) for axis, length in enumerate(result.shape)]
    main_axis = result.shape.index(max(result.shape))
    neighbour = place[:main_axis] + [(place[main_axis] + 1) % result.shape[main_axis]] + place[main_axis + 1:]
    return result.at[tuple(place)].set(low).at[tuple(neighbour)].set(largest)


def block_levels(own_key, shape, cuts, low, high):
    loudness, own = 1.0, jax.random.fold_in(own_key, 6)
    for dim, parts in cuts:
        heights = jnp.exp(jax.random.uniform(jax.random.fold_in(own, dim), (parts,), jnp.float32, low / len(cuts), high / len(cuts)))
        loudness = loudness * jnp.repeat(heights, shape[dim] // parts).reshape([-1 if axis == dim else 1 for axis in range(len(shape))])
    return loudness


def gaussian(key, shape, scale, bound, cuts=(), kind=jnp.bfloat16):
    drawn = scale * jax.random.normal(key, shape, jnp.float32)
    if cuts:
        drawn = drawn * block_levels(key, shape, cuts, -0.22, 0.18)
    return jnp.clip(drawn, -bound, bound).astype(kind)


def setup_inputs(seed: int = 0) -> dict:
    key_of = jax.random.split(jax.random.key(seed), 22)
    tokens = gaussian(key_of[0], (TOKENS, D), 1.0, 6.0, ((0, 8),))
    token_mask = draw_token_mask(jax.random.fold_in(key_of[21], 71), 0)
    masked_flags = touch_ends((jax.random.randint(key_of[2], (TOKENS,), 0, 20) < 3).astype(jnp.int32), jax.random.fold_in(key_of[2], 1), 0, 1)
    doc_lengths = draw_doc_lengths(jax.random.fold_in(key_of[21], 71), 0)
    mask_embedding = gaussian(key_of[4], (D,), 1.0, 6.0)
    ln1_gain = jnp.clip(1.0 + 0.1 * jax.random.normal(key_of[5], (D,), jnp.float32), 0.5, 1.5).astype(jnp.bfloat16)
    ln1_bias = gaussian(key_of[6], (D,), 0.1, 0.625)
    w_query = gaussian(key_of[7], (D, D), D ** -0.5, 0.21875, ((1, 4),))
    query_bias = gaussian(key_of[8], (D,), 0.3, 1.75, ((0, 4),))
    w_key = gaussian(key_of[9], (D, D), D ** -0.5, 0.21875, ((1, 4),))
    w_value = gaussian(key_of[10], (D, D), D ** -0.5, 0.21875, ((1, 4),))
    value_bias = gaussian(key_of[11], (D,), 0.05, 0.3125, ((0, 4),))
    w_out = gaussian(key_of[12], (D, D), (max(2, D // 256)) ** -0.5, 3.5, ((0, 4),))
    out_bias = gaussian(key_of[13], (D,), 0.2, 1.25)
    ln2_gain = jnp.clip(1.0 + 0.1 * jax.random.normal(key_of[14], (D,), jnp.float32), 0.5, 1.5).astype(jnp.bfloat16)
    ln2_bias = gaussian(key_of[15], (D,), 0.1, 0.625)
    w_up = gaussian(key_of[16], (D, FF), D ** -0.5, 0.21875, ((1, 4),))
    up_bias = gaussian(key_of[17], (FF,), 0.1, 0.625, ((0, 4),))
    w_down = gaussian(key_of[18], (FF, D), (FF // 4) ** -0.5, 0.21875, ((0, 4),))
    down_bias = gaussian(key_of[19], (D,), 0.2, 1.25)
    cotangent = gaussian(key_of[20], (TOKENS, D), 1.0, 6.0, ((0, 32),))
    return {"tokens": tokens, "token_mask": token_mask, "masked_flags": masked_flags, "doc_lengths": doc_lengths, "mask_embedding": mask_embedding, "ln1_gain": ln1_gain, "ln1_bias": ln1_bias, "w_query": w_query, "query_bias": query_bias, "w_key": w_key, "w_value": w_value, "value_bias": value_bias, "w_out": w_out, "out_bias": out_bias, "ln2_gain": ln2_gain, "ln2_bias": ln2_bias, "w_up": w_up, "up_bias": up_bias, "w_down": w_down, "down_bias": down_bias, "cotangent": cotangent}


@jax.custom_vjp
def low(v):
    return lax.optimization_barrier(v.astype(jnp.bfloat16)).astype(jnp.float32)

@jax.custom_vjp
def low_back(v):
    return v

def low_keep(v):
    return (low(v), None)

def low_pass(kept, grad):
    return (grad,)

def back_keep(v):
    return (v, None)

def back_low(kept, grad):
    return (low(grad),)
low.defvjp(low_keep, low_pass)
low_back.defvjp(back_keep, back_low)
highest = lax.Precision.HIGHEST
epsilon = 1e-05
negative_fill = -1e+30

def matmul_high(first_operand, second_operand):
    return jnp.dot(first_operand, second_operand, precision=highest)

def norm_rows(values, gain_row, shift_row):
    average = lax.optimization_barrier(jnp.mean(values, axis=-1, keepdims=True))
    centred = values - average
    spread = lax.optimization_barrier(jnp.mean(centred * centred, axis=-1, keepdims=True))
    return centred * lax.rsqrt(spread + epsilon) * gain_row + shift_row

def doc_index(doc_lengths, row_total):
    doc_ends = jnp.cumsum(doc_lengths).astype(jnp.int32)
    places = jnp.arange(row_total, dtype=jnp.int32)
    return lax.optimization_barrier(jnp.sum((places[:, None] >= doc_ends[None, :]).astype(jnp.int32), axis=1)).astype(jnp.int32)

def layer_group(tokens_in, live_mask, flag_rows, lengths, weights):
    mask_embedding, ln1_gain, ln1_bias, w_query, query_bias, w_key, w_value, value_bias, w_out, out_bias, ln2_gain, ln2_bias, w_up, up_bias, w_down, down_bias = weights
    row_total = tokens_in.shape[0]
    layer_in = jnp.where(flag_rows[:, None] == 1, mask_embedding[None, :], tokens_in)
    first_norm = low(norm_rows(layer_in, ln1_gain, ln1_bias))
    query_heads = low(low_back(matmul_high(first_norm, w_query) + query_bias)).reshape(row_total, H, HD)
    key_heads = low(low_back(matmul_high(first_norm, w_key))).reshape(row_total, H, HD)
    value_heads = low(low_back(matmul_high(first_norm, w_value) + value_bias)).reshape(row_total, H, HD)
    doc_of = doc_index(lengths, row_total)
    places = jnp.arange(row_total, dtype=jnp.int32)
    allowed = (doc_of[:, None] == doc_of[None, :]) & ((live_mask[None, :] == 1) | (places[:, None] == places[None, :]))
    scores = low_back(jnp.einsum('qhd,khd->hqk', query_heads, key_heads, precision=highest) / math.sqrt(HD))
    scores = jnp.where(allowed[None, :, :], scores, negative_fill)
    row_top = lax.optimization_barrier(jnp.max(scores, axis=-1, keepdims=True))
    exp_scores = jnp.exp(scores - row_top)
    probability = exp_scores / lax.optimization_barrier(jnp.sum(exp_scores, axis=-1, keepdims=True))
    context = jnp.einsum('hqk,khd->qhd', low(probability), value_heads, precision=highest).reshape(row_total, H * HD)
    context = low(low_back(context))
    hidden = layer_in + low_back(matmul_high(context, w_out) + out_bias)
    sent_rows = low(low_back(hidden))
    second_norm = low(norm_rows(sent_rows, ln2_gain, ln2_bias))
    pre_act = low_back(matmul_high(second_norm, w_up) + up_bias)
    activated = low(jax.nn.gelu(pre_act))
    ffn_out = low(matmul_high(activated, w_down) + down_bias)
    return hidden + jnp.where(live_mask[:, None] == 1, ffn_out, 0.0)

def reference(tokens, token_mask, masked_flags, doc_lengths, mask_embedding, ln1_gain, ln1_bias, w_query, query_bias, w_key, w_value, value_bias, w_out, out_bias, ln2_gain, ln2_bias, w_up, up_bias, w_down, down_bias, cotangent):
    groups = TOKENS // TOK_DEV
    weights = tuple((member.astype(jnp.float32) for member in (mask_embedding, ln1_gain, ln1_bias, w_query, query_bias, w_key, w_value, value_bias, w_out, out_bias, ln2_gain, ln2_bias, w_up, up_bias, w_down, down_bias)))
    tokens_f = tokens.astype(jnp.float32).reshape(groups, TOK_DEV, D)
    mask_groups = token_mask.reshape(groups, TOK_DEV)
    flag_groups = masked_flags.reshape(groups, TOK_DEV)
    length_groups = doc_lengths.reshape(groups, SLOTS)
    checked = jax.checkpoint(layer_group)

    def whole(tokens_all, weight_set):

        def step_group(carried, group_item):
            return (carried, checked(group_item[0], group_item[1], group_item[2], group_item[3], weight_set))
        unused, outputs = lax.scan(step_group, jnp.zeros((), jnp.float32), (tokens_all, mask_groups, flag_groups, length_groups))
        return outputs
    outputs, pullback = jax.vjp(whole, tokens_f, weights)
    input_grad, weight_grads = pullback(cotangent.astype(jnp.float32).reshape(groups, TOK_DEV, D))
    return (outputs.reshape(TOKENS, D).astype(jnp.bfloat16), input_grad.reshape(TOKENS, D), weight_grads[0], weight_grads[1], weight_grads[2], weight_grads[3], weight_grads[4], weight_grads[5], weight_grads[6], weight_grads[7], weight_grads[8], weight_grads[9], weight_grads[10], weight_grads[11], weight_grads[12], weight_grads[13], weight_grads[14], weight_grads[15])
```

```python
import functools
import math

import jax
import jax.numpy as jnp
from jax import lax
from jax.experimental import pallas as pl
from jax.experimental.pallas import tpu as pltpu
from jax.sharding import PartitionSpec as P

HD = 64
EPS = 1e-05
NEG = -2e30
LOG2E = 1.4426950408889634
VMEM_LIMIT = 56 * 2**20
ROWS = 512
KEYS = 512


def dot(a, b, ca=1, cb=0):
    return lax.dot_general(a, b, (((ca,), (cb,)), ((), ())), preferred_element_type=jnp.float32)


def doc_bounds(len_ref, slots, axis):
    shape = (1, 128) if axis == 1 else (128, 1)
    place = lax.broadcasted_iota(jnp.int32, shape, axis)
    starts = jnp.zeros(shape, jnp.int32)
    ends = jnp.zeros(shape, jnp.int32)
    begin = jnp.int32(0)
    for slot in range(slots):
        end = begin + len_ref[slot]
        starts = jnp.where(place == slot, begin, starts)
        ends = jnp.where(place == slot, end, ends)
        begin = end
    return starts, ends


def column(row):
    wide = jnp.broadcast_to(row.astype(jnp.float32), (8, row.shape[1]))
    return jnp.transpose(wide)[:, :1]


def proj_kernel(len_ref, tok_ref, live_ref, flag_ref, emb_ref, gain_ref, bias_ref, wq_ref, bq_ref, wk_ref, wv_ref,
                bv_ref, fn_ref, qx_ref, kx_ref, tt_ref, wdup, wT, bcol, *, heads, slots):
    step = pl.program_id(0)
    width = heads * HD

    @pl.when(step == 0)
    def _():
        for h in range(heads):
            for n, w in enumerate((wq_ref, wk_ref)):
                piece = w[:, h * HD:(h + 1) * HD]
                wdup[:, (2 * h + n) * 128:(2 * h + n + 1) * 128] = jnp.concatenate([piece, piece], axis=1)
        for n, w in enumerate((wq_ref, wk_ref, wv_ref)):
            wT[n * width:(n + 1) * width, :] = jnp.transpose(w[...])
        zero = jnp.zeros((1, width), jnp.float32)
        rows = jnp.concatenate([bq_ref[...].astype(jnp.float32), zero, bv_ref[...].astype(jnp.float32)], axis=1)
        bcol[...] = jnp.transpose(jnp.broadcast_to(rows, (8, 3 * width)))

    flags = column(flag_ref[0])
    live = column(live_ref[0])
    x = jnp.where(flags == 1.0, emb_ref[...].astype(jnp.float32), tok_ref[...].astype(jnp.float32))
    mean = jnp.mean(x, axis=1, keepdims=True)
    c = x - mean
    var = jnp.mean(c * c, axis=1, keepdims=True)
    fn = (c * lax.rsqrt(var + EPS) * gain_ref[...].astype(jnp.float32) + bias_ref[...].astype(jnp.float32)).astype(jnp.bfloat16)
    fn_ref[...] = fn
    starts, ends = doc_bounds(len_ref, slots, 1)
    row = step * ROWS + lax.broadcasted_iota(jnp.int32, (ROWS, 128), 0)
    lane = lax.broadcasted_iota(jnp.int32, (ROWS, 128), 1)
    member = (row >= starts) & (row < ends)
    pen = jnp.where(member & (live == 1.0), 0.0, NEG)
    pen = jnp.where(lane < 16, pen, jnp.where(lane < 19, 1.0, 0.0)).astype(jnp.bfloat16)
    both = dot(fn, wdup[...])
    for h in range(heads):
        bq = bq_ref[:, h * HD:(h + 1) * HD].astype(jnp.float32)
        q = (both[:, 2 * h * 128:(2 * h + 1) * 128] + jnp.concatenate([bq, bq], axis=1)).astype(jnp.bfloat16)
        q = q.astype(jnp.float32) * (LOG2E / math.sqrt(HD))
        high = q.astype(jnp.bfloat16).astype(jnp.float32)
        qx_ref[h] = jnp.where(lane < HD, high, q - high).astype(jnp.bfloat16)
        kx_ref[h, :, :128] = both[:, (2 * h + 1) * 128:(2 * h + 2) * 128].astype(jnp.bfloat16)
        kx_ref[h, :, 128:] = pen
    tt = (dot(wT[...], fn, 1, 1) + bcol[:, :1]).astype(jnp.bfloat16)
    for n in range(3):
        for h in range(heads):
            tt_ref[h, n * HD:(n + 1) * HD, :] = tt[n * width + h * HD:n * width + (h + 1) * HD, :]


def project(lengths, tokens, live, flags, emb, gain, bias, wq, bq, wk, wv, bv):
    rows, feat = tokens.shape
    width = wq.shape[1]
    heads = width // HD
    steps = rows // ROWS
    whole = lambda s: pl.BlockSpec(s, lambda i, *_: (0,) * len(s))
    row1 = lambda a: a.reshape(1, -1)
    return pl.pallas_call(
        functools.partial(proj_kernel, heads=heads, slots=lengths.shape[0]),
        name="project",
        grid_spec=pltpu.PrefetchScalarGridSpec(
            num_scalar_prefetch=1,
            grid=(steps,),
            in_specs=[
                pl.BlockSpec((ROWS, feat), lambda i, *_: (i, 0)),
                pl.BlockSpec((1, 1, ROWS), lambda i, *_: (i, 0, 0)),
                pl.BlockSpec((1, 1, ROWS), lambda i, *_: (i, 0, 0)),
                whole((1, feat)), whole((1, feat)), whole((1, feat)),
                whole((feat, width)), whole((1, width)), whole((feat, width)), whole((feat, width)), whole((1, width)),
            ],
            out_specs=[
                pl.BlockSpec((ROWS, feat), lambda i, *_: (i, 0)),
                pl.BlockSpec((heads, ROWS, 128), lambda i, *_: (0, i, 0)),
                pl.BlockSpec((heads, ROWS, 256), lambda i, *_: (0, i, 0)),
                pl.BlockSpec((heads, 3 * HD, ROWS), lambda i, *_: (0, 0, i)),
            ],
            scratch_shapes=[
                pltpu.VMEM((feat, heads * 256), jnp.bfloat16),
                pltpu.VMEM((3 * width, feat), jnp.bfloat16),
                pltpu.VMEM((3 * width, 8), jnp.float32),
            ],
        ),
        out_shape=[
            jax.ShapeDtypeStruct((rows, feat), jnp.bfloat16),
            jax.ShapeDtypeStruct((heads, rows, 128), jnp.bfloat16),
            jax.ShapeDtypeStruct((heads, rows, 256), jnp.bfloat16),
            jax.ShapeDtypeStruct((heads, 3 * HD, rows), jnp.bfloat16),
        ],
        compiler_params=pltpu.CompilerParams(vmem_limit_bytes=VMEM_LIMIT),
    )(lengths, tokens, live.reshape(steps, 1, ROWS), flags.reshape(steps, 1, ROWS), row1(emb), row1(gain), row1(bias),
      wq, row1(bq), wk, wv, row1(bv))


def key_range(len_ref, slots, first, last, live_end):
    begin = jnp.int32(0)
    low = jnp.int32(0)
    high = jnp.int32(0)
    for slot in range(slots):
        end = begin + len_ref[slot]
        low = jnp.where((first >= begin) & (first < end), begin, low)
        high = jnp.where((last >= begin) & (last < end), end, high)
        begin = end
    return low, jnp.minimum(high, live_end)


def last_live(live_row):
    place = lax.broadcasted_iota(jnp.int32, live_row.shape, 1)
    return jnp.max(jnp.where(live_row == 1, place + 1, 0))


def one_hot_rows(len_ref, slots, first, count):
    starts, ends = doc_bounds(len_ref, slots, 0)
    place = first + lax.broadcasted_iota(jnp.int32, (16, count), 1)
    return (place >= starts[:16]) & (place < ends[:16])


def fwd_kernel(len_ref, live_ref, kx_ref, tt_ref, ctx_ref, lse_ref, qx, *, heads, slots):
    rows = tt_ref.shape[2]
    blocks = rows // ROWS
    live_end = last_live(live_ref[...])

    @pl.loop(0, blocks)
    def _(i):
        first = pl.multiple_of(i * ROWS, ROWS)
        here = pl.ds(first, ROWS)
        low, high = key_range(len_ref, slots, first, first + ROWS - 1, live_end)
        hot = jnp.where(one_hot_rows(len_ref, slots, first, ROWS), 1.0, 0.0)
        dead = live_ref[:, here] != 1
        state = []
        for h in range(heads):
            q = tt_ref[h, :HD, here].astype(jnp.float32)
            k = tt_ref[h, HD:2 * HD, here].astype(jnp.float32)
            v = tt_ref[h, 2 * HD:, here].astype(jnp.float32)
            scaled = q * (LOG2E / math.sqrt(HD))
            top = scaled.astype(jnp.bfloat16)
            qx[h, :HD] = top
            qx[h, HD:128] = (scaled - top.astype(jnp.float32)).astype(jnp.bfloat16)
            qx[h, 128:] = jnp.concatenate([hot, jnp.zeros((112, ROWS), jnp.float32)], axis=0).astype(jnp.bfloat16)
            own = jnp.sum(scaled * k, axis=0, keepdims=True)
            state += [jnp.where(dead, own, -1e30), jnp.where(dead, 1.0, 0.0), jnp.where(dead, v, 0.0)]

        def step(j, carried):
            keys = pl.ds(pl.multiple_of(j * KEYS, KEYS), KEYS)
            out = []
            for h in range(heads):
                top, total, acc = carried[3 * h:3 * h + 3]
                s = dot(kx_ref[h, keys, :], qx[h])
                new = jnp.maximum(top, jnp.max(s, axis=0, keepdims=True))
                p = jnp.exp2(s - new)
                fade = jnp.exp2(top - new)
                total = total * fade + jnp.sum(p, axis=0, keepdims=True)
                acc = acc * fade + dot(tt_ref[h, 2 * HD:, keys], p.astype(jnp.bfloat16))
                out += [new, total, acc]
            return tuple(out)

        state = lax.fori_loop(low // KEYS, (high + KEYS - 1) // KEYS, step, tuple(state))
        for h in range(heads):
            top, total, acc = state[3 * h:3 * h + 3]
            ctx_ref[h * HD:(h + 1) * HD, here] = (acc / total).astype(jnp.bfloat16)
            lse_ref[h:h + 1, here] = top + jnp.log2(total)


def attend(lengths, live, kx, tt):
    heads, _, rows = tt.shape
    vmem = pl.BlockSpec(memory_space=pltpu.VMEM)
    return pl.pallas_call(
        functools.partial(fwd_kernel, heads=heads, slots=lengths.shape[0]),
        name="attend",
        in_specs=[pl.BlockSpec(memory_space=pltpu.SMEM), vmem, vmem, vmem],
        out_specs=[vmem, vmem],
        out_shape=[jax.ShapeDtypeStruct((heads * HD, rows), jnp.bfloat16), jax.ShapeDtypeStruct((heads, rows), jnp.float32)],
        scratch_shapes=[pltpu.VMEM((heads, 256, ROWS), jnp.bfloat16)],
        compiler_params=pltpu.CompilerParams(vmem_limit_bytes=VMEM_LIMIT),
    )(lengths, live.reshape(1, rows), kx, tt)


def split3(x):
    a = x.astype(jnp.bfloat16).astype(jnp.float32)
    b = (x - a).astype(jnp.bfloat16).astype(jnp.float32)
    return a, b, x - a - b


def bwd_kernel(len_ref, live_ref, qx_ref, kx_ref, tt_ref, ctx_ref, lse_ref, dot_ref, grad_ref, qfull, kT, dofull, vT,
               dk, dv, *, slots):
    rows = tt_ref.shape[2]
    blocks = rows // ROWS
    live_end = last_live(live_ref[...])
    lane_zero = jnp.zeros
    kT[:HD] = tt_ref[0, HD:2 * HD, :]
    kT[HD:128] = tt_ref[0, HD:2 * HD, :]
    starts, ends = doc_bounds(len_ref, slots, 0)
    vT[:HD] = tt_ref[0, 2 * HD:, :]
    ones = jnp.where(lax.broadcasted_iota(jnp.int32, (16, ROWS), 0) < 3, 1.0, 0.0)

    @pl.loop(0, blocks)
    def _(i):
        first = pl.multiple_of(i * ROWS, ROWS)
        here = pl.ds(first, ROWS)
        member = one_hot_rows(len_ref, slots, first, ROWS)
        alive = live_ref[:, here] == 1
        dead = jnp.logical_not(alive)
        pen = jnp.where(member & alive, 0.0, NEG)
        kT[128:, here] = jnp.concatenate([pen, ones, lane_zero((96, ROWS), jnp.float32)], axis=0).astype(jnp.bfloat16)
        vT[HD:, here] = jnp.concatenate([ones, lane_zero((48, ROWS), jnp.float32)], axis=0).astype(jnp.bfloat16)
        q = tt_ref[0, :HD, here].astype(jnp.float32)
        k = tt_ref[0, HD:2 * HD, here].astype(jnp.float32)
        v = tt_ref[0, 2 * HD:, here].astype(jnp.float32)
        do = dot_ref[0, :, here].astype(jnp.float32)
        delta = jnp.sum(do * ctx_ref[0, :, here].astype(jnp.float32), axis=0, keepdims=True)
        lse = lse_ref[0, :, here]
        parts = jnp.concatenate([-x for x in split3(lse)], axis=0)
        rest = jnp.concatenate([jnp.where(member, 1.0, 0.0), parts, lane_zero((109, ROWS), jnp.float32)], axis=0)
        qfull[here, :128] = qx_ref[0, here, :]
        qfull[here, 128:] = jnp.transpose(rest).astype(jnp.bfloat16)
        parts = jnp.concatenate([-x for x in split3(delta)], axis=0)
        rest = jnp.concatenate([do, parts, lane_zero((61, ROWS), jnp.float32)], axis=0)
        dofull[here, :] = jnp.transpose(rest).astype(jnp.bfloat16)
        p = jnp.where(dead, jnp.exp2(jnp.sum(q * k, axis=0, keepdims=True) * (LOG2E / math.sqrt(HD)) - lse), 0.0)
        ds = p * (jnp.sum(do * v, axis=0, keepdims=True) - delta)
        dk[:, here] = ds * q
        dv[:, here] = p * do
        grad_ref[0, :HD, here] = (ds * k).astype(jnp.bfloat16)

    @pl.loop(0, blocks)
    def _(i):
        first = pl.multiple_of(i * ROWS, ROWS)
        here = pl.ds(first, ROWS)
        low, high = key_range(len_ref, slots, first, first + ROWS - 1, live_end)

        def step(j, dq):
            keys = pl.ds(pl.multiple_of(j * KEYS, KEYS), KEYS)
            p = jnp.exp2(dot(qfull[here, :], kT[:, keys]))
            ds = (p * dot(dofull[here, :], vT[:, keys])).astype(jnp.bfloat16)
            dv[:, keys] += dot(dot_ref[0, :, here], p.astype(jnp.bfloat16))
            dk[:, keys] += dot(tt_ref[0, :HD, here], ds)
            return dq + dot(ds, kx_ref[0, keys, :128])

        dq = lax.fori_loop(low // KEYS, (high + KEYS - 1) // KEYS, step, jnp.zeros((ROWS, 128), jnp.float32))
        dqT = jnp.transpose(dq)[:HD]
        grad_ref[0, :HD, here] = ((grad_ref[0, :HD, here].astype(jnp.float32) + dqT) * (1 / math.sqrt(HD))).astype(jnp.bfloat16)
    grad_ref[0, HD:2 * HD, :] = (dk[...] * (1 / math.sqrt(HD))).astype(jnp.bfloat16)
    grad_ref[0, 2 * HD:, :] = dv[...].astype(jnp.bfloat16)


def attend_back(lengths, live, qx, kx, tt, ctx, lse, do):
    heads, _, rows = tt.shape
    per = lambda *s: pl.BlockSpec((1,) + s, lambda h: (h, 0, 0))
    vm = pltpu.VMEM
    return pl.pallas_call(
        functools.partial(bwd_kernel, slots=lengths.shape[0]),
        name="attend_back",
        grid=(heads,),
        in_specs=[pl.BlockSpec(memory_space=pltpu.SMEM), pl.BlockSpec((1, rows), lambda h: (0, 0)), per(rows, 128),
                  per(rows, 256), per(3 * HD, rows), per(HD, rows), per(1, rows), per(HD, rows)],
        out_specs=per(3 * HD, rows),
        out_shape=jax.ShapeDtypeStruct((heads, 3 * HD, rows), jnp.bfloat16),
        scratch_shapes=[vm((rows, 256), jnp.bfloat16), vm((256, rows), jnp.bfloat16), vm((rows, 128), jnp.bfloat16),
                        vm((128, rows), jnp.bfloat16), vm((HD, rows), jnp.float32), vm((HD, rows), jnp.float32)],
        compiler_params=pltpu.CompilerParams(vmem_limit_bytes=VMEM_LIMIT),
    )(lengths, live.reshape(1, rows), qx, kx, tt, ctx.reshape(heads, HD, rows), lse.reshape(heads, 1, rows),
      do.reshape(heads, HD, rows))


epsilon = 1e-05
negative_fill = -1e30


def norm_rows(values, gain_row, shift_row):
    average = jnp.mean(values, axis=-1, keepdims=True)
    centred = values - average
    spread = jnp.mean(centred * centred, axis=-1, keepdims=True)
    return centred * lax.rsqrt(spread + epsilon) * gain_row + shift_row


def contract(first_operand, second_operand, first_dim, second_dim):
    return lax.dot_general(
        first_operand,
        second_operand,
        (((first_dim,), (second_dim,)), ((), ())),
        preferred_element_type=jnp.float32,
    )


def doc_index(doc_lengths, row_total):
    doc_ends = jnp.cumsum(doc_lengths)
    places = jnp.arange(row_total, dtype=jnp.int32)
    return jnp.sum((places[:, None] >= doc_ends[None, :]).astype(jnp.int32), axis=1)


def feed_forward(
    sent_rows, grad_rows, live_rows, ln2_gain, ln2_bias, w_up, up_bias, w_down, down_bias
):
    gain_row = ln2_gain.astype(jnp.float32)
    shift_row = ln2_bias.astype(jnp.float32)
    normed, norm_pullback = jax.vjp(norm_rows, sent_rows.astype(jnp.float32), gain_row, shift_row)
    normed_low = jnp.where(live_rows[:, None], normed, 0.0).astype(jnp.bfloat16)
    gathered_norm, gathered_grad = (
        lax.all_gather(normed_low, "tensor", axis=0, tiled=True),
        lax.all_gather(grad_rows, "tensor", axis=0, tiled=True),
    )
    pre_act = jnp.dot(gathered_norm, w_up, preferred_element_type=jnp.float32) + up_bias.astype(
        jnp.float32
    )
    activated, act_pullback = jax.vjp(jax.nn.gelu, pre_act)
    act_low = activated.astype(jnp.bfloat16)
    out_part = jnp.dot(act_low, w_down, preferred_element_type=jnp.float32)
    back_act = contract(gathered_grad, w_down, 1, 1)
    back_pre = act_pullback(back_act)[0].astype(jnp.bfloat16)
    grad_down = contract(act_low, gathered_grad, 0, 0)
    grad_up = contract(gathered_norm, back_pre, 0, 0)
    grad_up_bias = jnp.sum(back_pre, axis=0, dtype=jnp.float32)
    back_norm_part = contract(back_pre, w_up, 1, 1)
    out_sum, back_norm = (
        lax.psum_scatter(
            out_part.astype(jnp.bfloat16), "tensor", scatter_dimension=0, tiled=True
        ).astype(jnp.float32),
        lax.psum_scatter(
            back_norm_part.astype(jnp.bfloat16), "tensor", scatter_dimension=0, tiled=True
        ).astype(jnp.float32),
    )
    ffn_low = (out_sum + down_bias.astype(jnp.float32)).astype(jnp.bfloat16)
    back_norm = jnp.where(live_rows[:, None], back_norm, 0.0)
    back_sent, gain_grad, shift_grad = norm_pullback(back_norm)
    return (
        ffn_low,
        back_sent.astype(jnp.bfloat16),
        grad_up,
        grad_down,
        grad_up_bias,
        gain_grad,
        shift_grad,
    )


def per_device(
    tokens,
    token_mask,
    masked_flags,
    doc_lengths,
    mask_embedding,
    ln1_gain,
    ln1_bias,
    w_query,
    query_bias,
    w_key,
    w_value,
    value_bias,
    w_out,
    out_bias,
    ln2_gain,
    ln2_bias,
    w_up,
    up_bias,
    w_down,
    down_bias,
    cotangent,
):
    row_total, feat_width = tokens.shape
    tensor_size = lax.axis_size("tensor")
    tensor_index = lax.axis_index("tensor")
    quarter = row_total // tensor_size
    quarter_begin = tensor_index * quarter
    local_width = w_query.shape[1]
    head_count = local_width // HD
    hidden_local = w_up.shape[1]
    first_gain = ln1_gain.astype(jnp.float32)
    first_shift = ln1_bias.astype(jnp.float32)
    layer_in = jnp.where(
        masked_flags[:, None] == 1,
        mask_embedding.astype(jnp.float32)[None, :],
        tokens.astype(jnp.float32),
    )
    first_norm, query_pair, key_wide, head_rows = project(
        doc_lengths, tokens, token_mask, masked_flags, mask_embedding, ln1_gain, ln1_bias,
        w_query, query_bias, w_key, w_value, value_bias,
    )
    context_cols, log_totals = attend(doc_lengths, token_mask, key_wide, head_rows)
    attn_rows = lax.psum_scatter(
        contract(context_cols, w_out, 0, 0).astype(jnp.bfloat16),
        "tensor",
        scatter_dimension=0,
        tiled=True,
    ).astype(jnp.float32)
    layer_quarter = lax.dynamic_slice_in_dim(layer_in, quarter_begin, quarter, 0)
    live_quarter = lax.dynamic_slice_in_dim(token_mask, quarter_begin, quarter) == 1
    flag_quarter = lax.dynamic_slice_in_dim(masked_flags, quarter_begin, quarter) == 1
    hidden_rows = layer_quarter + attn_rows + out_bias.astype(jnp.float32)
    sent_rows = hidden_rows.astype(jnp.bfloat16)
    grad_in = jnp.where(live_quarter[:, None], cotangent, jnp.zeros_like(cotangent))
    ffn_low, back_sent, grad_up, grad_down, up_bias_grad, second_gain_grad, second_shift_grad = (
        feed_forward(
            sent_rows, grad_in, live_quarter, ln2_gain, ln2_bias, w_up, up_bias, w_down, down_bias
        )
    )
    ffn_rows = jnp.where(live_quarter[:, None], ffn_low.astype(jnp.float32), 0.0)
    layer_output = (hidden_rows + ffn_rows).astype(jnp.bfloat16)
    back_hidden = cotangent.astype(jnp.float32) + jnp.where(
        live_quarter[:, None], back_sent.astype(jnp.float32), 0.0
    )
    back_attn = back_hidden.astype(jnp.bfloat16)
    out_bias_grad = jnp.sum(back_attn, axis=0, dtype=jnp.float32)
    down_bias_grad = jnp.sum(grad_in, axis=0, dtype=jnp.float32)
    attn_all = lax.all_gather(back_attn, "tensor", axis=0, tiled=True)
    grad_w_out = contract(context_cols, attn_all, 1, 0)
    context_grads = contract(w_out, attn_all, 1, 1).astype(jnp.bfloat16)
    grads = attend_back(
        doc_lengths, token_mask, query_pair, key_wide, head_rows, context_cols, log_totals, context_grads
    )
    back_query, back_key, back_value = (
        grads[:, n * HD : (n + 1) * HD].reshape(local_width, row_total) for n in range(3)
    )
    grad_w_query = contract(first_norm, back_query, 0, 1)
    grad_w_key = contract(first_norm, back_key, 0, 1)
    grad_w_value = contract(first_norm, back_value, 0, 1)
    query_bias_local = jnp.sum(back_query, axis=1, dtype=jnp.float32)
    value_bias_local = jnp.sum(back_value, axis=1, dtype=jnp.float32)
    back_first = lax.psum_scatter(
        (
            contract(back_query, w_query, 0, 1)
            + contract(back_key, w_key, 0, 1)
            + contract(back_value, w_value, 0, 1)
        ).astype(jnp.bfloat16),
        "tensor",
        scatter_dimension=0,
        tiled=True,
    ).astype(jnp.float32)
    unused_rows, first_pullback = jax.vjp(norm_rows, layer_quarter, first_gain, first_shift)
    norm_part, first_gain_grad, first_shift_grad = first_pullback(back_first)
    back_in = back_hidden + norm_part
    mask_grad = jnp.sum(jnp.where(flag_quarter[:, None], back_in, 0.0), axis=0)
    input_grad = jnp.where(flag_quarter[:, None], 0.0, back_in)
    query_bias_full = lax.dynamic_update_slice(
        jnp.zeros((feat_width,), jnp.float32), query_bias_local, (tensor_index * local_width,)
    )
    value_bias_full = lax.dynamic_update_slice(
        jnp.zeros((feat_width,), jnp.float32), value_bias_local, (tensor_index * local_width,)
    )
    up_bias_full = lax.dynamic_update_slice(
        jnp.zeros((hidden_local * tensor_size,), jnp.float32),
        up_bias_grad,
        (tensor_index * hidden_local,),
    )
    sum_wq, sum_wk, sum_wv, sum_wo, sum_up, sum_down = (
        lax.psum_scatter(grad_w_query, "dp", scatter_dimension=0, tiled=True),
        lax.psum_scatter(grad_w_key, "dp", scatter_dimension=0, tiled=True),
        lax.psum_scatter(grad_w_value, "dp", scatter_dimension=0, tiled=True),
        lax.psum_scatter(grad_w_out, "dp", scatter_dimension=1, tiled=True),
        lax.psum_scatter(grad_up, "dp", scatter_dimension=0, tiled=True),
        lax.psum_scatter(grad_down, "dp", scatter_dimension=1, tiled=True),
    )
    (
        sum_mask,
        sum_gain_one,
        sum_shift_one,
        sum_query_bias,
        sum_value_bias,
        sum_out_bias,
        sum_gain_two,
        sum_shift_two,
        sum_up_bias,
        sum_down_bias,
    ) = lax.psum(
        (
            mask_grad,
            first_gain_grad,
            first_shift_grad,
            query_bias_full,
            value_bias_full,
            out_bias_grad,
            second_gain_grad,
            second_shift_grad,
            up_bias_full,
            down_bias_grad,
        ),
        ("dp", "tensor"),
    )
    return (
        layer_output,
        input_grad,
        sum_mask,
        sum_gain_one,
        sum_shift_one,
        sum_wq,
        sum_query_bias,
        sum_wk,
        sum_wv,
        sum_value_bias,
        sum_wo,
        sum_out_bias,
        sum_gain_two,
        sum_shift_two,
        sum_up,
        sum_up_bias,
        sum_down,
        sum_down_bias,
    )


def solution(mesh):
    in_specs = (
        P("dp", None),
        P("dp"),
        P("dp"),
        P("dp"),
        P(),
        P(),
        P(),
        P(None, "tensor"),
        P("tensor"),
        P(None, "tensor"),
        P(None, "tensor"),
        P("tensor"),
        P("tensor", None),
        P(),
        P(),
        P(),
        P(None, "tensor"),
        P("tensor"),
        P("tensor", None),
        P(),
        P(("dp", "tensor"), None),
    )
    out_specs = (
        P(("dp", "tensor"), None),
        P(("dp", "tensor"), None),
        P(),
        P(),
        P(),
        P("dp", "tensor"),
        P(),
        P("dp", "tensor"),
        P("dp", "tensor"),
        P(),
        P("tensor", "dp"),
        P(),
        P(),
        P(),
        P("dp", "tensor"),
        P(),
        P("tensor", "dp"),
        P(),
    )
    return jax.shard_map(
        per_device, mesh=mesh, in_specs=in_specs, out_specs=out_specs, check_vma=False
    )
```

```python
import functools, math
import jax, jax.numpy as jnp
from jax import lax
from jax.experimental import pallas as pl
from jax.experimental.pallas import tpu as pltpu
from jax.sharding import PartitionSpec as P

HD = 64
EPS = 1e-05
NEG = -2e30
LOG2E = 1.4426950408889634
VMEM_LIMIT = 56 * 2**20
ROWS = 512
KEYS = 512


def dot(a, b, ca=1, cb=0):
    return lax.dot_general(a, b, (((ca,), (cb,)), ((), ())), preferred_element_type=jnp.float32)


def doc_bounds(len_ref, slots, axis):
    shape = (1, 128) if axis == 1 else (128, 1)
    place = lax.broadcasted_iota(jnp.int32, shape, axis)
    starts = jnp.zeros(shape, jnp.int32)
    ends = jnp.zeros(shape, jnp.int32)
    begin = jnp.int32(0)
    for slot in range(slots):
        end = begin + len_ref[slot]
        starts = jnp.where(place == slot, begin, starts)
        ends = jnp.where(place == slot, end, ends)
        begin = end
    return starts, ends


def column(row):
    wide = jnp.broadcast_to(row.astype(jnp.float32), (8, row.shape[1]))
    return jnp.transpose(wide)[:, :1]


def proj_kernel(len_ref, tok_ref, live_ref, flag_ref, emb_ref, gain_ref, bias_ref, wq_ref, bq_ref, wk_ref, wv_ref,
                bv_ref, fn_ref, qx_ref, kx_ref, tt_ref, wdup, wT, bcol, *, heads, slots):
    step = pl.program_id(0)
    width = heads * HD

    @pl.when(step == 0)
    def _():
        for h in range(heads):
            for n, w in enumerate((wq_ref, wk_ref)):
                piece = w[:, h * HD:(h + 1) * HD]
                wdup[:, (2 * h + n) * 128:(2 * h + n + 1) * 128] = jnp.concatenate([piece, piece], axis=1)
        for n, w in enumerate((wq_ref, wk_ref, wv_ref)):
            wT[n * width:(n + 1) * width, :] = jnp.transpose(w[...])
        zero = jnp.zeros((1, width), jnp.float32)
        rows = jnp.concatenate([bq_ref[...].astype(jnp.float32), zero, bv_ref[...].astype(jnp.float32)], axis=1)
        bcol[...] = jnp.transpose(jnp.broadcast_to(rows, (8, 3 * width)))

    flags = column(flag_ref[0])
    live = column(live_ref[0])
    x = jnp.where(flags == 1.0, emb_ref[...].astype(jnp.float32), tok_ref[...].astype(jnp.float32))
    mean = jnp.mean(x, axis=1, keepdims=True)
    c = x - mean
    var = jnp.mean(c * c, axis=1, keepdims=True)
    fn = (c * lax.rsqrt(var + EPS) * gain_ref[...].astype(jnp.float32) + bias_ref[...].astype(jnp.float32)).astype(jnp.bfloat16)
    fn_ref[...] = fn
    starts, ends = doc_bounds(len_ref, slots, 1)
    row = step * ROWS + lax.broadcasted_iota(jnp.int32, (ROWS, 128), 0)
    lane = lax.broadcasted_iota(jnp.int32, (ROWS, 128), 1)
    member = (row >= starts) & (row < ends)
    pen = jnp.where(member & (live == 1.0), 0.0, NEG)
    pen = jnp.where(lane < 16, pen, jnp.where(lane < 19, 1.0, 0.0)).astype(jnp.bfloat16)
    both = dot(fn, wdup[...])
    for h in range(heads):
        bq = bq_ref[:, h * HD:(h + 1) * HD].astype(jnp.float32)
        q = (both[:, 2 * h * 128:(2 * h + 1) * 128] + jnp.concatenate([bq, bq], axis=1)).astype(jnp.bfloat16)
        q = q.astype(jnp.float32) * (LOG2E / math.sqrt(HD))
        high = q.astype(jnp.bfloat16).astype(jnp.float32)
        qx_ref[h] = jnp.where(lane < HD, high, q - high).astype(jnp.bfloat16)
        kx_ref[h, :, :128] = both[:, (2 * h + 1) * 128:(2 * h + 2) * 128].astype(jnp.bfloat16)
        kx_ref[h, :, 128:] = pen
    tt = (dot(wT[...], fn, 1, 1) + bcol[:, :1]).astype(jnp.bfloat16)
    for n in range(3):
        for h in range(heads):
            tt_ref[h, n * HD:(n + 1) * HD, :] = tt[n * width + h * HD:n * width + (h + 1) * HD, :]


def project(lengths, tokens, live, flags, emb, gain, bias, wq, bq, wk, wv, bv):
    rows, feat = tokens.shape
    width = wq.shape[1]
    heads = width // HD
    steps = rows // ROWS
    whole = lambda s: pl.BlockSpec(s, lambda i, *_: (0,) * len(s))
    row1 = lambda a: a.reshape(1, -1)
    return pl.pallas_call(
        functools.partial(proj_kernel, heads=heads, slots=lengths.shape[0]),
        name="project",
        grid_spec=pltpu.PrefetchScalarGridSpec(
            num_scalar_prefetch=1,
            grid=(steps,),
            in_specs=[
                pl.BlockSpec((ROWS, feat), lambda i, *_: (i, 0)),
                pl.BlockSpec((1, 1, ROWS), lambda i, *_: (i, 0, 0)),
                pl.BlockSpec((1, 1, ROWS), lambda i, *_: (i, 0, 0)),
                whole((1, feat)), whole((1, feat)), whole((1, feat)),
                whole((feat, width)), whole((1, width)), whole((feat, width)), whole((feat, width)), whole((1, width)),
            ],
            out_specs=[
                pl.BlockSpec((ROWS, feat), lambda i, *_: (i, 0)),
                pl.BlockSpec((heads, ROWS, 128), lambda i, *_: (0, i, 0)),
                pl.BlockSpec((heads, ROWS, 256), lambda i, *_: (0, i, 0)),
                pl.BlockSpec((heads, 3 * HD, ROWS), lambda i, *_: (0, 0, i)),
            ],
            scratch_shapes=[
                pltpu.VMEM((feat, heads * 256), jnp.bfloat16),
                pltpu.VMEM((3 * width, feat), jnp.bfloat16),
                pltpu.VMEM((3 * width, 8), jnp.float32),
            ],
        ),
        out_shape=[
            jax.ShapeDtypeStruct((rows, feat), jnp.bfloat16),
            jax.ShapeDtypeStruct((heads, rows, 128), jnp.bfloat16),
            jax.ShapeDtypeStruct((heads, rows, 256), jnp.bfloat16),
            jax.ShapeDtypeStruct((heads, 3 * HD, rows), jnp.bfloat16),
        ],
        compiler_params=pltpu.CompilerParams(vmem_limit_bytes=VMEM_LIMIT),
    )(lengths, tokens, live.reshape(steps, 1, ROWS), flags.reshape(steps, 1, ROWS), row1(emb), row1(gain), row1(bias),
      wq, row1(bq), wk, wv, row1(bv))


def key_range(len_ref, slots, first, last, live_end):
    begin = jnp.int32(0)
    low = jnp.int32(0)
    high = jnp.int32(0)
    for slot in range(slots):
        end = begin + len_ref[slot]
        low = jnp.where((first >= begin) & (first < end), begin, low)
        high = jnp.where((last >= begin) & (last < end), end, high)
        begin = end
    return low, jnp.minimum(high, live_end)


def last_live(live_row):
    place = lax.broadcasted_iota(jnp.int32, live_row.shape, 1)
    return jnp.max(jnp.where(live_row == 1, place + 1, 0))


def one_hot_rows(len_ref, slots, first, count):
    starts, ends = doc_bounds(len_ref, slots, 0)
    place = first + lax.broadcasted_iota(jnp.int32, (16, count), 1)
    return (place >= starts[:16]) & (place < ends[:16])


def fwd_kernel(len_ref, live_ref, kx_ref, tt_ref, ctx_ref, lse_ref, qx, *, heads, slots):
    rows = tt_ref.shape[2]
    blocks = rows // ROWS
    live_end = last_live(live_ref[...])

    @pl.loop(0, blocks)
    def _(i):
        first = pl.multiple_of(i * ROWS, ROWS)
        here = pl.ds(first, ROWS)
        low, high = key_range(len_ref, slots, first, first + ROWS - 1, live_end)
        hot = jnp.where(one_hot_rows(len_ref, slots, first, ROWS), 1.0, 0.0)
        dead = live_ref[:, here] != 1
        state = []
        for h in range(heads):
            q = tt_ref[h, :HD, here].astype(jnp.float32)
            k = tt_ref[h, HD:2 * HD, here].astype(jnp.float32)
            v = tt_ref[h, 2 * HD:, here].astype(jnp.float32)
            scaled = q * (LOG2E / math.sqrt(HD))
            top = scaled.astype(jnp.bfloat16)
            qx[h, :HD] = top
            qx[h, HD:128] = (scaled - top.astype(jnp.float32)).astype(jnp.bfloat16)
            qx[h, 128:] = jnp.concatenate([hot, jnp.zeros((112, ROWS), jnp.float32)], axis=0).astype(jnp.bfloat16)
            own = jnp.sum(scaled * k, axis=0, keepdims=True)
            state += [jnp.where(dead, own, -1e30), jnp.where(dead, 1.0, 0.0), jnp.where(dead, v, 0.0)]

        def step(j, carried):
            keys = pl.ds(pl.multiple_of(j * KEYS, KEYS), KEYS)
            out = []
            for h in range(heads):
                top, total, acc = carried[3 * h:3 * h + 3]
                s = dot(kx_ref[h, keys, :], qx[h])
                new = jnp.maximum(top, jnp.max(s, axis=0, keepdims=True))
                p = jnp.exp2(s - new)
                fade = jnp.exp2(top - new)
                total = total * fade + jnp.sum(p, axis=0, keepdims=True)
                acc = acc * fade + dot(tt_ref[h, 2 * HD:, keys], p.astype(jnp.bfloat16))
                out += [new, total, acc]
            return tuple(out)

        state = lax.fori_loop(low // KEYS, (high + KEYS - 1) // KEYS, step, tuple(state))
        for h in range(heads):
            top, total, acc = state[3 * h:3 * h + 3]
            ctx_ref[h * HD:(h + 1) * HD, here] = (acc / total).astype(jnp.bfloat16)
            lse_ref[h:h + 1, here] = top + jnp.log2(total)


def attend(lengths, live, kx, tt):
    heads, _, rows = tt.shape
    vmem = pl.BlockSpec(memory_space=pltpu.VMEM)
    return pl.pallas_call(
        functools.partial(fwd_kernel, heads=heads, slots=lengths.shape[0]),
        name="attend",
        in_specs=[pl.BlockSpec(memory_space=pltpu.SMEM), vmem, vmem, vmem],
        out_specs=[vmem, vmem],
        out_shape=[jax.ShapeDtypeStruct((heads * HD, rows), jnp.bfloat16), jax.ShapeDtypeStruct((heads, rows), jnp.float32)],
        scratch_shapes=[pltpu.VMEM((heads, 256, ROWS), jnp.bfloat16)],
        compiler_params=pltpu.CompilerParams(vmem_limit_bytes=VMEM_LIMIT),
    )(lengths, live.reshape(1, rows), kx, tt)


def split3(x):
    a = x.astype(jnp.bfloat16).astype(jnp.float32)
    b = (x - a).astype(jnp.bfloat16).astype(jnp.float32)
    return a, b, x - a - b


def bwd_kernel(len_ref, live_ref, qx_ref, kx_ref, tt_ref, ctx_ref, lse_ref, dot_ref, grad_ref, qfull, kT, dofull, vT,
               dk, dv, *, slots):
    rows = tt_ref.shape[2]
    blocks = rows // ROWS
    live_end = last_live(live_ref[...])
    lane_zero = jnp.zeros
    kT[:HD] = tt_ref[0, HD:2 * HD, :]
    kT[HD:128] = tt_ref[0, HD:2 * HD, :]
    starts, ends = doc_bounds(len_ref, slots, 0)
    vT[:HD] = tt_ref[0, 2 * HD:, :]
    ones = jnp.where(lax.broadcasted_iota(jnp.int32, (16, ROWS), 0) < 3, 1.0, 0.0)

    @pl.loop(0, blocks)
    def _(i):
        first = pl.multiple_of(i * ROWS, ROWS)
        here = pl.ds(first, ROWS)
        member = one_hot_rows(len_ref, slots, first, ROWS)
        alive = live_ref[:, here] == 1
        dead = jnp.logical_not(alive)
        pen = jnp.where(member & alive, 0.0, NEG)
        kT[128:, here] = jnp.concatenate([pen, ones, lane_zero((96, ROWS), jnp.float32)], axis=0).astype(jnp.bfloat16)
        vT[HD:, here] = jnp.concatenate([ones, lane_zero((48, ROWS), jnp.float32)], axis=0).astype(jnp.bfloat16)
        q = tt_ref[0, :HD, here].astype(jnp.float32)
        k = tt_ref[0, HD:2 * HD, here].astype(jnp.float32)
        v = tt_ref[0, 2 * HD:, here].astype(jnp.float32)
        do = dot_ref[0, :, here].astype(jnp.float32)
        delta = jnp.sum(do * ctx_ref[0, :, here].astype(jnp.float32), axis=0, keepdims=True)
        lse = lse_ref[0, :, here]
        parts = jnp.concatenate([-x for x in split3(lse)], axis=0)
        rest = jnp.concatenate([jnp.where(member, 1.0, 0.0), parts, lane_zero((109, ROWS), jnp.float32)], axis=0)
        qfull[here, :128] = qx_ref[0, here, :]
        qfull[here, 128:] = jnp.transpose(rest).astype(jnp.bfloat16)
        parts = jnp.concatenate([-x for x in split3(delta)], axis=0)
        rest = jnp.concatenate([do, parts, lane_zero((61, ROWS), jnp.float32)], axis=0)
        dofull[here, :] = jnp.transpose(rest).astype(jnp.bfloat16)
        p = jnp.where(dead, jnp.exp2(jnp.sum(q * k, axis=0, keepdims=True) * (LOG2E / math.sqrt(HD)) - lse), 0.0)
        ds = p * (jnp.sum(do * v, axis=0, keepdims=True) - delta)
        dk[:, here] = ds * q
        dv[:, here] = p * do
        grad_ref[0, :HD, here] = (ds * k).astype(jnp.bfloat16)

    @pl.loop(0, blocks)
    def _(i):
        first = pl.multiple_of(i * ROWS, ROWS)
        here = pl.ds(first, ROWS)
        low, high = key_range(len_ref, slots, first, first + ROWS - 1, live_end)

        def step(j, dq):
            keys = pl.ds(pl.multiple_of(j * KEYS, KEYS), KEYS)
            p = jnp.exp2(dot(qfull[here, :], kT[:, keys]))
            ds = (p * dot(dofull[here, :], vT[:, keys])).astype(jnp.bfloat16)
            dv[:, keys] += dot(dot_ref[0, :, here], p.astype(jnp.bfloat16))
            dk[:, keys] += dot(tt_ref[0, :HD, here], ds)
            return dq + dot(ds, kx_ref[0, keys, :128])

        dq = lax.fori_loop(low // KEYS, (high + KEYS - 1) // KEYS, step, jnp.zeros((ROWS, 128), jnp.float32))
        dqT = jnp.transpose(dq)[:HD]
        grad_ref[0, :HD, here] = ((grad_ref[0, :HD, here].astype(jnp.float32) + dqT) * (1 / math.sqrt(HD))).astype(jnp.bfloat16)
    grad_ref[0, HD:2 * HD, :] = (dk[...] * (1 / math.sqrt(HD))).astype(jnp.bfloat16)
    grad_ref[0, 2 * HD:, :] = dv[...].astype(jnp.bfloat16)


def attend_back(head, lengths, live, qx, kx, tt, ctx, lse, do):
    heads, _, rows = tt.shape
    per = lambda *s: pl.BlockSpec((1,) + s, lambda i: (head, 0, 0))
    vm = pltpu.VMEM
    return pl.pallas_call(
        functools.partial(bwd_kernel, slots=lengths.shape[0]),
        name="attend_back",
        grid=(1,),
        in_specs=[pl.BlockSpec(memory_space=pltpu.SMEM), pl.BlockSpec((1, rows), lambda i: (0, 0)), per(rows, 128),
                  per(rows, 256), per(3 * HD, rows), per(HD, rows), per(1, rows), per(HD, rows)],
        out_specs=pl.BlockSpec((1, 3 * HD, rows), lambda i: (0, 0, 0)),
        out_shape=jax.ShapeDtypeStruct((1, 3 * HD, rows), jnp.bfloat16),
        scratch_shapes=[vm((rows, 256), jnp.bfloat16), vm((256, rows), jnp.bfloat16), vm((rows, 128), jnp.bfloat16),
                        vm((128, rows), jnp.bfloat16), vm((HD, rows), jnp.float32), vm((HD, rows), jnp.float32)],
        compiler_params=pltpu.CompilerParams(vmem_limit_bytes=VMEM_LIMIT),
    )(lengths, live.reshape(1, rows), qx, kx, tt, ctx.reshape(heads, HD, rows), lse.reshape(heads, 1, rows),
      do.reshape(heads, HD, rows))


GELU_C = math.sqrt(2 / math.pi)
CHUNK = 256


def mid_kernel(tok_ref, ctx_ref, cot_ref, wo_own, wu_own, wd_own, wo_far, wu_far, wd_far, upb_own, live_ref, flag_ref, emb_ref,
               ob_ref, gain_ref, bias_ref, db_ref,
               out_ref, bh_ref, do_ref, upk_ref, ups_ref, dnk_ref, dns_ref, ouk_ref, ous_ref, upsum_ref, sums_ref,
               wo, wu, wd, upb, cx, tok, cot, act, bp, hid, xhat, rstd, acc, bsec, n2, n2T, bf, bfT, atT, bcs, gr, gro, gso,
               loc_sem, w_send, w_recv, b_send, b_recv, c_send, c_recv, d_send, d_recv, d_loc, g_send, g_recv, o_sem,
               *, n):
    quarter, feat = cot.shape
    width = ctx_ref.shape[0]
    chunks = quarter // CHUNK
    me = lax.axis_index("tensor")
    mesh_id = pl.DeviceIdType.MESH

    def other(r):
        return (me, me + 1 - 2 * (me % 2), (me + 2) % n, n - 1 - me)[r]

    def peer(r):
        return {"tensor": other(r)}

    def cols(owner, c):
        return pl.ds(pl.multiple_of(owner * quarter + c * CHUNK, CHUNK), CHUNK)

    barrier = pltpu.get_barrier_semaphore()
    for r in range(1, n):
        pl.semaphore_signal(barrier, inc=1, device_id=peer(r), device_id_type=mesh_id)
    pl.semaphore_wait(barrier, n - 1)

    ctx_copies = {}
    for c in range(chunks):
        for r in (2, 3, 1):
            copy = pltpu.make_async_remote_copy(
                src_ref=ctx_ref.at[:, cols(other(r), c)],
                dst_ref=cx.at[pl.ds(r * width, width), pl.ds(c * CHUNK, CHUNK)],
                send_sem=c_send.at[c * n + r], recv_sem=c_recv.at[c * n + r],
                device_id=peer(r), device_id_type=mesh_id)
            copy.start()
            ctx_copies[c, r] = copy
    own_ctx = pltpu.make_async_copy(
        ctx_ref.at[:, pl.ds(pl.multiple_of(me * quarter, CHUNK), quarter)], cx.at[pl.ds(0, width), :], loc_sem.at[0])
    rows_here = pl.ds(pl.multiple_of(me * quarter, CHUNK), quarter)
    tok_copy = pltpu.make_async_copy(tok_ref.at[rows_here, :], tok, loc_sem.at[1])
    cot_copy = pltpu.make_async_copy(cot_ref, cot, loc_sem.at[2])
    local = {}
    remote = {}
    for i, (own, far, buf) in enumerate(((wo_own, wo_far, wo), (wu_own, wu_far, wu), (wd_own, wd_far, wd))):
        size = own.shape[0]
        for r, src in ((0, own), (2, far)):
            dst = buf.at[pl.ds(r * size, size), :]
            local[i, r] = pltpu.make_async_copy(src, dst, loc_sem.at[3 + 2 * i + r // 2])
            dst = buf.at[pl.ds((r + 1) * size, size), :]
            remote[i, r + 1] = pltpu.make_async_remote_copy(
                src_ref=src, dst_ref=dst, send_sem=w_send.at[2 * i + r // 2], recv_sem=w_recv.at[2 * i + r // 2],
                device_id=peer(1), device_id_type=mesh_id)
    bias_copies = []
    for r in range(1, n):
        copy = pltpu.make_async_remote_copy(
            src_ref=upb_own, dst_ref=upb.at[r], send_sem=b_send.at[r], recv_sem=b_recv.at[r],
            device_id=peer(r), device_id_type=mesh_id)
        copy.start()
        bias_copies.append(copy)
    own_bias = pltpu.make_async_copy(upb_own, upb.at[0], loc_sem.at[9])
    own_ctx.start()
    tok_copy.start()
    cot_copy.start()
    own_bias.start()
    for i in range(3):
        for r in (0, 2):
            local[i, r].start()
            remote[i, r + 1].start()

    live_col = column(live_ref[me])
    flag_col = column(flag_ref[me])
    cot_copy.wait()
    masked = jnp.where(live_col == 1.0, cot[...], jnp.zeros((), jnp.bfloat16))
    bf[...] = masked
    bfT[...] = jnp.transpose(masked)
    sums_ref[...] = jnp.zeros(sums_ref.shape, jnp.float32)
    sums_ref[3:4] = jnp.sum(masked.astype(jnp.float32), axis=0, keepdims=True)
    tok_copy.wait()
    own_ctx.wait()
    for r in (0, 2):
        local[0, r].wait()
        remote[0, r + 1].wait()
    gain = gain_ref[...].astype(jnp.float32)
    shift = bias_ref[...].astype(jnp.float32)
    for c in range(chunks):
        for r in (2, 3, 1):
            ctx_copies[c, r].wait()
        here = pl.ds(c * CHUNK, CHUNK)
        flag_c = flag_col[c * CHUNK:(c + 1) * CHUNK]
        x = jnp.where(flag_c == 1.0, emb_ref[...].astype(jnp.float32), tok[here, :].astype(jnp.float32))
        hidden = x + dot(cx[:, here], wo[...], 0, 0) + ob_ref[...].astype(jnp.float32)
        hid[here, :] = hidden
        sent = hidden.astype(jnp.bfloat16).astype(jnp.float32)
        centred = sent - jnp.mean(sent, axis=1, keepdims=True)
        scale = lax.rsqrt(jnp.mean(centred * centred, axis=1, keepdims=True) + EPS)
        normed = centred * scale
        xhat[here, :] = normed
        rstd[here, :] = jnp.broadcast_to(scale, (CHUNK, 128))
        second = (normed * gain + shift).astype(jnp.bfloat16)
        n2[here, :] = second
        n2T[:, here] = jnp.transpose(second)
    own_bias.wait()
    for copy in bias_copies:
        copy.wait()

    for r in range(n):
        if r % 2 == 0:
            local[1, r].wait()
            local[2, r].wait()
        else:
            remote[1, r].wait()
            remote[2, r].wait()
        up = wu.at[pl.ds(r * feat, feat), :]
        down = wd.at[pl.ds(r * wd_own.shape[0], wd_own.shape[0]), :]
        upsum_ref[r] = jnp.zeros(upsum_ref.shape[1:], jnp.float32)

        @pl.loop(0, chunks)
        def _(c):
            here = pl.ds(pl.multiple_of(c * CHUNK, CHUNK), CHUNK)
            pre = dot(n2[here, :], up[...]) + upb[r, :1, :]
            square = pre * pre
            inner = pre * (square * (GELU_C * 0.044715) + GELU_C)
            t = jnp.tanh(inner)
            half = 0.5 * t + 0.5
            a = pre * half
            slope = half + a * (1.0 - t) * (square * (3 * GELU_C * 0.044715) + GELU_C)
            low = a.astype(jnp.bfloat16)
            act[r, here, :] = low
            back = (dot(bf[here, :], down[...], 1, 1) * slope).astype(jnp.bfloat16)
            bp[r, here, :] = back
            upsum_ref[r, :1, :] += jnp.sum(back.astype(jnp.float32), axis=0, keepdims=True)
            out_part = dot(low, down[...])
            back_part = dot(back, up[...], 1, 1)
            if r == 0:
                acc[here, :] = out_part
                bsec[here, :] = back_part
            else:
                acc[here, :] += out_part
                bsec[here, :] += back_part

    bctx_copies = []
    for c in range(chunks):
        here = pl.ds(c * CHUNK, CHUNK)
        live_c = live_col[c * CHUNK:(c + 1) * CHUNK]
        ffn = (acc[here, :] + db_ref[...].astype(jnp.float32)).astype(jnp.bfloat16).astype(jnp.float32)
        out_ref[here, :] = (hid[here, :] + jnp.where(live_c == 1.0, ffn, 0.0)).astype(jnp.bfloat16)
        back = bsec[here, :]
        normed = xhat[here, :]
        sums_ref[0:1] += jnp.sum(back * normed, axis=0, keepdims=True)
        sums_ref[1:2] += jnp.sum(back, axis=0, keepdims=True)
        m = back * gain
        back_sent = rstd[here, :1] * (
            m - jnp.mean(m, axis=1, keepdims=True) - normed * jnp.mean(m * normed, axis=1, keepdims=True))
        back_hidden = cot[here, :].astype(jnp.float32) + back_sent.astype(jnp.bfloat16).astype(jnp.float32)
        bh_ref[here, :] = back_hidden
        attn = back_hidden.astype(jnp.bfloat16)
        sums_ref[2:3] += jnp.sum(attn.astype(jnp.float32), axis=0, keepdims=True)
        atT[:, here] = jnp.transpose(attn)
        bcs[:, here] = dot(wo[...], attn, 1, 1).astype(jnp.bfloat16)
        for r in (2, 3, 1):
            copy = pltpu.make_async_remote_copy(
                src_ref=bcs.at[pl.ds(r * width, width), pl.ds(c * CHUNK, CHUNK)],
                dst_ref=do_ref.at[:, cols(me, c)],
                send_sem=d_send.at[c * n + r], recv_sem=d_recv.at[c * n + r],
                device_id=peer(r), device_id_type=mesh_id)
            copy.start()
            bctx_copies.append(copy)
        copy = pltpu.make_async_copy(
            bcs.at[pl.ds(0, width), pl.ds(c * CHUNK, CHUNK)], do_ref.at[:, cols(me, c)], d_loc.at[c])
        copy.start()
        bctx_copies.append(copy)

    hidden_units = wd_own.shape[0]
    grad_copies = {}
    for i, r in enumerate((1, 3)):
        up_slot = wd.at[pl.ds(2 * i * feat, feat), :]
        dn_slot = wd.at[pl.ds((2 * i + 1) * feat, feat), :]

        @pl.loop(0, feat // CHUNK)
        def _(c):
            here = pl.ds(pl.multiple_of(c * CHUNK, CHUNK), CHUNK)
            up_slot[here, :] = dot(n2T[here, :], bp[r]).astype(jnp.bfloat16)
            dn_slot[here, :] = dot(bfT[here, :], act[r]).astype(jnp.bfloat16)
            gso[i, here, :] = dot(atT[here, :], cx[r * width:(r + 1) * width, :], 1, 1).astype(jnp.bfloat16)

        for k, (src, dst) in enumerate(((up_slot, gr.at[2 * i]), (dn_slot, gr.at[2 * i + 1]), (gso.at[i], gro.at[i]))):
            copy = pltpu.make_async_remote_copy(
                src_ref=src, dst_ref=dst, send_sem=g_send.at[3 * i + k], recv_sem=g_recv.at[3 * i + k],
                device_id=peer(1), device_id_type=mesh_id)
            copy.start()
            grad_copies[i, k] = copy
    for i, (r, up_out, dn_out, ou_out) in enumerate(((0, upk_ref, dnk_ref, ouk_ref), (2, ups_ref, dns_ref, ous_ref))):
        up_slot = wu.at[pl.ds(2 * i * feat, feat), :]
        dn_slot = wu.at[pl.ds((2 * i + 1) * feat, feat), :]
        for k in range(3):
            grad_copies[i, k].wait()

        @pl.loop(0, feat // CHUNK)
        def _(c):
            here = pl.ds(pl.multiple_of(c * CHUNK, CHUNK), CHUNK)
            up_slot[here, :] = (dot(n2T[here, :], bp[r]) + gr[2 * i, here, :].astype(jnp.float32)).astype(jnp.bfloat16)
            dn_slot[here, :] = (dot(bfT[here, :], act[r]) + gr[2 * i + 1, here, :].astype(jnp.float32)).astype(jnp.bfloat16)
            ou_out[here, :] = (dot(atT[here, :], cx[r * width:(r + 1) * width, :], 1, 1)
                               + gro[i, here, :].astype(jnp.float32)).astype(jnp.bfloat16)

        for k, (src, dst) in enumerate(((up_slot, up_out), (dn_slot, dn_out))):
            copy = pltpu.make_async_copy(src, dst, o_sem.at[2 * i + k])
            copy.start()
            bctx_copies.append(copy)
    for copy in bctx_copies:
        copy.wait()


def middle(n, tokens, ctx, cotangent, own, far, up_bias, live, flags, emb, out_bias, gain, bias, down_bias):
    quarter, feat = cotangent.shape
    width, rows = ctx.shape
    hidden_units = own[1].shape[1]
    vm, any_, vmem = pltpu.VMEM, pl.BlockSpec(memory_space=pl.ANY), pl.BlockSpec(memory_space=pltpu.VMEM)
    row1 = lambda a: a.reshape(1, -1)
    bf16, f32 = jnp.bfloat16, jnp.float32
    chunks = quarter // CHUNK
    sem = pltpu.SemaphoreType.DMA
    flops = 2 * quarter * feat * (6 * n * hidden_units + 3 * n * width)
    grads = [jax.ShapeDtypeStruct((feat, c), bf16) for c in (hidden_units, hidden_units, hidden_units, hidden_units, width, width)]
    return pl.pallas_call(
        functools.partial(mid_kernel, n=n),
        name="middle",
        in_specs=[any_] * 10 + [vmem] * 7,
        out_specs=[vmem, vmem] + [any_] * 5 + [vmem] * 4,
        out_shape=[jax.ShapeDtypeStruct((quarter, feat), bf16), jax.ShapeDtypeStruct((quarter, feat), f32),
                   jax.ShapeDtypeStruct((width, rows), bf16)] + grads + [
                   jax.ShapeDtypeStruct((n, 8, hidden_units), f32), jax.ShapeDtypeStruct((8, feat), f32)],
        scratch_shapes=[
            vm((n * width, feat), bf16), vm((n * feat, hidden_units), bf16), vm((n * hidden_units, feat), bf16),
            vm((n, 8, hidden_units), f32), vm((n * width, quarter), bf16), vm((quarter, feat), bf16), vm((quarter, feat), bf16),
            vm((n, quarter, hidden_units), bf16), vm((n, quarter, hidden_units), bf16),
            vm((quarter, feat), f32), vm((quarter, feat), f32), vm((quarter, 128), f32), vm((quarter, feat), f32),
            vm((quarter, feat), f32), vm((quarter, feat), bf16), vm((feat, quarter), bf16), vm((quarter, feat), bf16),
            vm((feat, quarter), bf16), vm((feat, quarter), bf16), vm((n * width, quarter), bf16),
            vm((4, feat, hidden_units), bf16), vm((2, feat, width), bf16), vm((2, feat, width), bf16),
            sem((10,)), sem((6,)), sem((6,)), sem((n,)), sem((n,)), sem((chunks * n,)), sem((chunks * n,)),
            sem((chunks * n,)), sem((chunks * n,)), sem((chunks,)), sem((6,)), sem((6,)), sem((4,)),
        ],
        cost_estimate=pl.CostEstimate(flops=flops, bytes_accessed=40 * 2**20, transcendentals=0),
        compiler_params=pltpu.CompilerParams(vmem_limit_bytes=60 * 2**20, collective_id=0, has_side_effects=True),
    )(tokens, ctx, cotangent, *own, *far, jnp.broadcast_to(up_bias.astype(f32)[None], (8, hidden_units)),
      live.reshape(n, 1, quarter), flags.reshape(n, 1, quarter), row1(emb), row1(out_bias), row1(gain), row1(bias), row1(down_bias))


def swap(array, axis, distance):
    return lax.ppermute(array, axis, [(i, i ^ distance) for i in range(lax.axis_size(axis))])


def add(*parts):
    return sum(part.astype(jnp.float32) for part in parts)


def pick(array, index, axis):
    return lax.dynamic_index_in_dim(array, index, axis, keepdims=False)


def norm_back(grad, normed, scale, gain):
    m = grad * gain
    return scale * (m - jnp.mean(m, axis=1, keepdims=True) - normed * jnp.mean(m * normed, axis=1, keepdims=True))


def per_device(
    tokens,
    token_mask,
    masked_flags,
    doc_lengths,
    mask_embedding,
    ln1_gain,
    ln1_bias,
    w_query,
    query_bias,
    w_key,
    w_value,
    value_bias,
    w_out,
    out_bias,
    ln2_gain,
    ln2_bias,
    w_up,
    up_bias,
    w_down,
    down_bias,
    cotangent,
):
    row_total, feat = tokens.shape
    n = lax.axis_size("tensor")
    me = lax.axis_index("tensor")
    dp_size = lax.axis_size("dp")
    dp_me = lax.axis_index("dp")
    quarter = row_total // n
    width = w_query.shape[1]
    heads = width // HD
    hidden_units = w_up.shape[1]
    f32, bf16 = jnp.float32, jnp.bfloat16

    own = (w_out, w_up, w_down)
    far = tuple(swap(w, "tensor", 2) for w in own)
    first_norm, query_pair, key_wide, head_rows = project(
        doc_lengths, tokens, token_mask, masked_flags, mask_embedding, ln1_gain, ln1_bias,
        w_query, query_bias, w_key, w_value, value_bias,
    )
    context, log_totals = attend(doc_lengths, token_mask, key_wide, head_rows)
    layer_output, back_hidden, back_context, up_keep, up_send, down_keep, down_send, out_keep, out_send, up_sums, sums = middle(
        n, tokens, context, cotangent, own, far, up_bias, token_mask, masked_flags, mask_embedding, out_bias,
        ln2_gain, ln2_bias, down_bias,
    )

    low_count = 2
    high_count = dp_size // low_count
    dp_low, dp_high = dp_me % low_count, dp_me // low_count

    def over_y(keep, send):
        return add(keep, swap(send, "tensor", 2)).astype(bf16)

    def over_x(piece, axis):
        return add(pick(piece, dp_low, axis), swap(pick(piece, 1 - dp_low, axis), "dp", 1)).astype(bf16)

    def over_z(piece, axis):
        parts = [pick(piece, dp_high, axis)]
        for d in range(1, high_count):
            parts.append(swap(pick(piece, dp_high ^ d, axis), "dp", low_count * d))
        return add(*parts).astype(bf16)

    rows_of = feat // dp_size
    split = lambda g: g.reshape(high_count, low_count, rows_of, g.shape[1])
    a = over_y(up_keep, up_send)
    b = over_x(jnp.stack([split(down_keep), split(down_send)]), 2)
    c = over_z(jnp.stack([split(out_keep), split(out_send)]), 1)
    a = over_x(split(a), 1)
    b = over_z(b, 1)
    c = over_y(c[0], c[1])
    grad_up = over_z(a, 0).astype(f32)
    grad_down = add(b[0], swap(b[1], "tensor", 2)).T
    grad_out = add(pick(c, dp_low, 0), swap(pick(c, 1 - dp_low, 0), "dp", 1)).T

    def columns(array, owner):
        return lax.dynamic_slice_in_dim(array, owner * quarter, quarter, 1)

    weights = (
        jnp.stack([w_query, w_key, w_value]).reshape(3, feat, heads, HD).transpose(2, 0, 3, 1).reshape(heads * 3 * HD, feat)
    )
    weights_far = swap(weights, "tensor", 2)
    weights_all = jnp.concatenate([weights, swap(weights, "tensor", 1), weights_far, swap(weights_far, "tensor", 1)])
    grads, received = [], []
    for head in range(heads):
        g = attend_back(head, doc_lengths, token_mask, query_pair, key_wide, head_rows, context, log_totals, back_context)
        grads.append(g.reshape(3 * HD, row_total))
        received.append(
            [columns(grads[-1], me)] + [swap(columns(grads[-1], me ^ r), "tensor", r) for r in range(1, n)]
        )
    by_owner = jnp.concatenate([received[h][r] for r in range(n) for h in range(heads)])
    back_first = dot(by_owner, weights_all, 0, 0)
    grad_rows = jnp.concatenate(grads)
    head_sums = jnp.sum(grad_rows, axis=1, dtype=f32).reshape(heads, 3, HD)
    grad_heads = dot(grad_rows, first_norm, 1, 0).reshape(heads, 3, HD, feat).transpose(1, 3, 0, 2).reshape(3, feat, width)

    here = me * quarter
    flags = lax.dynamic_slice_in_dim(masked_flags, here, quarter)[:, None] == 1
    layer_in = jnp.where(flags, mask_embedding.astype(f32), lax.dynamic_slice_in_dim(tokens, here, quarter, 0).astype(f32))
    centred = layer_in - jnp.mean(layer_in, axis=1, keepdims=True)
    scale = lax.rsqrt(jnp.mean(centred * centred, axis=1, keepdims=True) + EPS)
    normed = centred * scale
    back_in = back_hidden + norm_back(back_first, normed, scale, ln1_gain.astype(f32))
    input_grad = jnp.where(flags, 0.0, back_in)

    def at_mine(part, total):
        return lax.dynamic_update_slice(jnp.zeros((total,), f32), part, (me * part.shape[0],))

    up_sum_parts = up_sums[:, 0, :]
    up_bias_sum = jnp.concatenate([pick(up_sum_parts, me ^ r, 0) for r in range(n)])
    vectors = lax.psum(
        (
            jnp.sum(jnp.where(flags, back_in, 0.0), axis=0),
            jnp.sum(back_first * normed, axis=0),
            jnp.sum(back_first, axis=0),
            at_mine(head_sums[:, 0].reshape(-1), feat),
            at_mine(head_sums[:, 2].reshape(-1), feat),
            sums[2],
            sums[0],
            sums[1],
            up_bias_sum,
            sums[3],
        ),
        ("dp", "tensor"),
    )
    mask_sum, gain1, bias1, q_bias, v_bias, o_bias, gain2, bias2, u_bias, d_bias = vectors
    gq, gk, gv = (lax.psum_scatter(grad_heads[i], "dp", scatter_dimension=0, tiled=True) for i in range(3))
    return (layer_output, input_grad, mask_sum, gain1, bias1, gq, q_bias, gk, gv, v_bias, grad_out, o_bias, gain2, bias2,
            grad_up, u_bias, grad_down, d_bias)


def solution(mesh):
    in_specs = (
        P("dp", None),
        P("dp"),
        P("dp"),
        P("dp"),
        P(),
        P(),
        P(),
        P(None, "tensor"),
        P("tensor"),
        P(None, "tensor"),
        P(None, "tensor"),
        P("tensor"),
        P("tensor", None),
        P(),
        P(),
        P(),
        P(None, "tensor"),
        P("tensor"),
        P("tensor", None),
        P(),
        P(("dp", "tensor"), None),
    )
    out_specs = (
        P(("dp", "tensor"), None),
        P(("dp", "tensor"), None),
        P(),
        P(),
        P(),
        P("dp", "tensor"),
        P(),
        P("dp", "tensor"),
        P("dp", "tensor"),
        P(),
        P("tensor", "dp"),
        P(),
        P(),
        P(),
        P("dp", "tensor"),
        P(),
        P("tensor", "dp"),
        P(),
    )
    return jax.shard_map(
        per_device, mesh=mesh, in_specs=in_specs, out_specs=out_specs, check_vma=False
    )
```

```python
import functools, math
import jax, jax.numpy as jnp
from jax import lax
from jax.experimental import pallas as pl
from jax.experimental.pallas import tpu as pltpu
from jax.sharding import PartitionSpec as P

HD = 64
EPS = 1e-05
NEG = -2e30
LOG2E = 1.4426950408889634
VMEM_LIMIT = 56 * 2**20
ROWS = 512
KEYS = 512


def dot(a, b, ca=1, cb=0):
    return lax.dot_general(a, b, (((ca,), (cb,)), ((), ())), preferred_element_type=jnp.float32)


def doc_bounds(len_ref, slots, axis):
    shape = (1, 128) if axis == 1 else (128, 1)
    place = lax.broadcasted_iota(jnp.int32, shape, axis)
    starts = jnp.zeros(shape, jnp.int32)
    ends = jnp.zeros(shape, jnp.int32)
    begin = jnp.int32(0)
    for slot in range(slots):
        end = begin + len_ref[slot]
        starts = jnp.where(place == slot, begin, starts)
        ends = jnp.where(place == slot, end, ends)
        begin = end
    return starts, ends


def column(row):
    wide = jnp.broadcast_to(row.astype(jnp.float32), (8, row.shape[1]))
    return jnp.transpose(wide)[:, :1]


def proj_kernel(len_ref, tok_ref, mark_ref, vec_ref, qv_ref, wq_ref, wk_ref, wv_ref, fn_ref, qx_ref, kx_ref, tt_ref,
                wT_ref, wdup, bcol, *, heads, slots):
    step = pl.program_id(0)
    width = heads * HD

    @pl.when(step == 0)
    def _():
        zero = jnp.zeros((1, HD), jnp.float32)
        rows = []
        for h in range(heads):
            piece = slice(h * HD, (h + 1) * HD)
            for n, w in enumerate((wq_ref, wk_ref, wv_ref)):
                begin = (3 * h + n) * HD
                wT_ref[begin:begin + HD, :] = w[piece, :]
                if n < 2:
                    for copy in range(2):
                        begin = ((2 * h + n) * 2 + copy) * HD
                        wdup[begin:begin + HD, :] = w[piece, :]
            rows += [qv_ref[0:1, piece], zero, qv_ref[1:2, piece]]
        bcol[...] = jnp.transpose(jnp.broadcast_to(jnp.concatenate(rows, axis=1), (8, 3 * width)))

    live = column(mark_ref[0:1, :])
    flags = column(mark_ref[1:2, :])
    x = jnp.where(flags == 1.0, vec_ref[0:1], tok_ref[...].astype(jnp.float32))
    mean = jnp.mean(x, axis=1, keepdims=True)
    c = x - mean
    var = jnp.mean(c * c, axis=1, keepdims=True)
    fn = (c * lax.rsqrt(var + EPS) * vec_ref[1:2] + vec_ref[2:3]).astype(jnp.bfloat16)
    fn_ref[...] = fn
    starts, ends = doc_bounds(len_ref, slots, 1)
    row = step * ROWS + lax.broadcasted_iota(jnp.int32, (ROWS, 128), 0)
    lane = lax.broadcasted_iota(jnp.int32, (ROWS, 128), 1)
    member = (row >= starts) & (row < ends)
    pen = jnp.where(member & (live == 1.0), 0.0, NEG)
    pen = jnp.where(lane < 16, pen, jnp.where(lane < 19, 1.0, 0.0)).astype(jnp.bfloat16)
    both = dot(fn, wdup[...], 1, 1)
    for h in range(heads):
        bq = qv_ref[0:1, h * HD:(h + 1) * HD]
        q = (both[:, 2 * h * 128:(2 * h + 1) * 128] + jnp.concatenate([bq, bq], axis=1)).astype(jnp.bfloat16)
        q = q.astype(jnp.float32) * (LOG2E / math.sqrt(HD))
        high = q.astype(jnp.bfloat16).astype(jnp.float32)
        qx_ref[h] = jnp.where(lane < HD, high, q - high).astype(jnp.bfloat16)
        kx_ref[h, :, :128] = both[:, (2 * h + 1) * 128:(2 * h + 2) * 128].astype(jnp.bfloat16)
        kx_ref[h, :, 128:] = pen
    tt = (dot(wT_ref[...], fn, 1, 1) + bcol[:, :1]).astype(jnp.bfloat16)
    for h in range(heads):
        tt_ref[h] = tt[h * 3 * HD:(h + 1) * 3 * HD, :]


def project(lengths, tokens, marks, vectors, qv_bias, wqT, wkT, wvT):
    rows, feat = tokens.shape
    width = wqT.shape[0]
    heads = width // HD
    whole = lambda s: pl.BlockSpec(s, lambda i, *_: (0,) * len(s))
    return pl.pallas_call(
        functools.partial(proj_kernel, heads=heads, slots=lengths.shape[0]),
        name="project",
        grid_spec=pltpu.PrefetchScalarGridSpec(
            num_scalar_prefetch=1,
            grid=(rows // ROWS,),
            in_specs=[
                pl.BlockSpec((ROWS, feat), lambda i, *_: (i, 0)),
                pl.BlockSpec((2, ROWS), lambda i, *_: (0, i)),
                whole(vectors.shape), whole(qv_bias.shape),
                whole((width, feat)), whole((width, feat)), whole((width, feat)),
            ],
            out_specs=[
                pl.BlockSpec((ROWS, feat), lambda i, *_: (i, 0)),
                pl.BlockSpec((heads, ROWS, 128), lambda i, *_: (0, i, 0)),
                pl.BlockSpec((heads, ROWS, 256), lambda i, *_: (0, i, 0)),
                pl.BlockSpec((heads, 3 * HD, ROWS), lambda i, *_: (0, 0, i)),
                whole((3 * width, feat)),
            ],
            scratch_shapes=[
                pltpu.VMEM((heads * 256, feat), jnp.bfloat16),
                pltpu.VMEM((3 * width, 8), jnp.float32),
            ],
        ),
        out_shape=[
            jax.ShapeDtypeStruct((rows, feat), jnp.bfloat16),
            jax.ShapeDtypeStruct((heads, rows, 128), jnp.bfloat16),
            jax.ShapeDtypeStruct((heads, rows, 256), jnp.bfloat16),
            jax.ShapeDtypeStruct((heads, 3 * HD, rows), jnp.bfloat16),
            jax.ShapeDtypeStruct((3 * width, feat), jnp.bfloat16),
        ],
        compiler_params=pltpu.CompilerParams(vmem_limit_bytes=VMEM_LIMIT),
    )(lengths, tokens, marks, vectors, qv_bias, wqT, wkT, wvT)


def key_range(len_ref, slots, first, last, live_end):
    begin = jnp.int32(0)
    low = jnp.int32(0)
    high = jnp.int32(0)
    for slot in range(slots):
        end = begin + len_ref[slot]
        low = jnp.where((first >= begin) & (first < end), begin, low)
        high = jnp.where((last >= begin) & (last < end), end, high)
        begin = end
    return low, jnp.minimum(high, live_end)


def last_live(live_row):
    place = lax.broadcasted_iota(jnp.int32, live_row.shape, 1)
    return jnp.max(jnp.where(live_row == 1, place + 1, 0))


def one_hot_rows(len_ref, slots, first, count):
    starts, ends = doc_bounds(len_ref, slots, 0)
    place = first + lax.broadcasted_iota(jnp.int32, (16, count), 1)
    return (place >= starts[:16]) & (place < ends[:16])


def fwd_kernel(len_ref, live_ref, kx_ref, tt_ref, ctx_ref, lse_ref, qx, *, heads, slots):
    rows = tt_ref.shape[2]
    blocks = rows // ROWS
    live_end = last_live(live_ref[0:1, :])

    @pl.loop(0, blocks)
    def _(i):
        first = pl.multiple_of(i * ROWS, ROWS)
        here = pl.ds(first, ROWS)
        low, high = key_range(len_ref, slots, first, first + ROWS - 1, live_end)
        hot = jnp.where(one_hot_rows(len_ref, slots, first, ROWS), 1.0, 0.0)
        dead = live_ref[0:1, here] != 1
        state = []
        for h in range(heads):
            q = tt_ref[h, :HD, here].astype(jnp.float32)
            k = tt_ref[h, HD:2 * HD, here].astype(jnp.float32)
            v = tt_ref[h, 2 * HD:, here].astype(jnp.float32)
            scaled = q * (LOG2E / math.sqrt(HD))
            top = scaled.astype(jnp.bfloat16)
            qx[h, :HD] = top
            qx[h, HD:128] = (scaled - top.astype(jnp.float32)).astype(jnp.bfloat16)
            qx[h, 128:] = jnp.concatenate([hot, jnp.zeros((112, ROWS), jnp.float32)], axis=0).astype(jnp.bfloat16)
            own = jnp.sum(scaled * k, axis=0, keepdims=True)
            state += [jnp.where(dead, own, -1e30), jnp.where(dead, 1.0, 0.0), jnp.where(dead, v, 0.0)]

        def step(j, carried):
            keys = pl.ds(pl.multiple_of(j * KEYS, KEYS), KEYS)
            out = []
            for h in range(heads):
                top, total, acc = carried[3 * h:3 * h + 3]
                s = dot(kx_ref[h, keys, :], qx[h])
                new = jnp.maximum(top, jnp.max(s, axis=0, keepdims=True))
                p = jnp.exp2(s - new)
                fade = jnp.exp2(top - new)
                total = total * fade + jnp.sum(p, axis=0, keepdims=True)
                acc = acc * fade + dot(tt_ref[h, 2 * HD:, keys], p.astype(jnp.bfloat16))
                out += [new, total, acc]
            return tuple(out)

        state = lax.fori_loop(low // KEYS, (high + KEYS - 1) // KEYS, step, tuple(state))
        for h in range(heads):
            top, total, acc = state[3 * h:3 * h + 3]
            ctx_ref[h * HD:(h + 1) * HD, here] = (acc / total).astype(jnp.bfloat16)
            lse_ref[h, :, here] = top + jnp.log2(total)


def attend(lengths, marks, kx, tt):
    heads, _, rows = tt.shape
    vmem = pl.BlockSpec(memory_space=pltpu.VMEM)
    return pl.pallas_call(
        functools.partial(fwd_kernel, heads=heads, slots=lengths.shape[0]),
        name="attend",
        in_specs=[pl.BlockSpec(memory_space=pltpu.SMEM), vmem, vmem, vmem],
        out_specs=[vmem, vmem],
        out_shape=[jax.ShapeDtypeStruct((heads * HD, rows), jnp.bfloat16), jax.ShapeDtypeStruct((heads, 1, rows), jnp.float32)],
        scratch_shapes=[pltpu.VMEM((heads, 256, ROWS), jnp.bfloat16)],
        compiler_params=pltpu.CompilerParams(vmem_limit_bytes=VMEM_LIMIT),
    )(lengths, marks, kx, tt)


def split3(x):
    a = x.astype(jnp.bfloat16).astype(jnp.float32)
    b = (x - a).astype(jnp.bfloat16).astype(jnp.float32)
    return a, b, x - a - b


def bwd_kernel(len_ref, live_ref, qx_ref, kx_ref, tt_ref, ctx_ref, lse_ref, dot_ref, grad_ref, part0, part1, part2,
               part3, qfull, kT, dofull, vT, dk, dv, *, slots, n):
    rows = tt_ref.shape[2]
    quarter = rows // n
    blocks = rows // ROWS
    live_end = last_live(live_ref[0:1, :])
    lane_zero = jnp.zeros
    kT[:HD] = tt_ref[0, HD:2 * HD, :]
    kT[HD:128] = tt_ref[0, HD:2 * HD, :]
    starts, ends = doc_bounds(len_ref, slots, 0)
    vT[:HD] = tt_ref[0, 2 * HD:, :]
    ones = jnp.where(lax.broadcasted_iota(jnp.int32, (16, ROWS), 0) < 3, 1.0, 0.0)

    @pl.loop(0, blocks)
    def _(i):
        first = pl.multiple_of(i * ROWS, ROWS)
        here = pl.ds(first, ROWS)
        member = one_hot_rows(len_ref, slots, first, ROWS)
        alive = live_ref[0:1, here] == 1
        dead = jnp.logical_not(alive)
        pen = jnp.where(member & alive, 0.0, NEG)
        kT[128:, here] = jnp.concatenate([pen, ones, lane_zero((96, ROWS), jnp.float32)], axis=0).astype(jnp.bfloat16)
        vT[HD:, here] = jnp.concatenate([ones, lane_zero((48, ROWS), jnp.float32)], axis=0).astype(jnp.bfloat16)
        q = tt_ref[0, :HD, here].astype(jnp.float32)
        k = tt_ref[0, HD:2 * HD, here].astype(jnp.float32)
        v = tt_ref[0, 2 * HD:, here].astype(jnp.float32)
        do = dot_ref[:, here].astype(jnp.float32)
        delta = jnp.sum(do * ctx_ref[:, here].astype(jnp.float32), axis=0, keepdims=True)
        lse = lse_ref[0, :, here]
        parts = jnp.concatenate([-x for x in split3(lse)], axis=0)
        rest = jnp.concatenate([jnp.where(member, 1.0, 0.0), parts, lane_zero((109, ROWS), jnp.float32)], axis=0)
        qfull[here, :128] = qx_ref[0, here, :]
        qfull[here, 128:] = jnp.transpose(rest).astype(jnp.bfloat16)
        parts = jnp.concatenate([-x for x in split3(delta)], axis=0)
        rest = jnp.concatenate([do, parts, lane_zero((61, ROWS), jnp.float32)], axis=0)
        dofull[here, :] = jnp.transpose(rest).astype(jnp.bfloat16)
        p = jnp.where(dead, jnp.exp2(jnp.sum(q * k, axis=0, keepdims=True) * (LOG2E / math.sqrt(HD)) - lse), 0.0)
        ds = p * (jnp.sum(do * v, axis=0, keepdims=True) - delta)
        dk[:, here] = ds * q
        dv[:, here] = p * do
        grad_ref[:HD, here] = (ds * k).astype(jnp.bfloat16)

    @pl.loop(0, blocks)
    def _(i):
        first = pl.multiple_of(i * ROWS, ROWS)
        here = pl.ds(first, ROWS)
        low, high = key_range(len_ref, slots, first, first + ROWS - 1, live_end)

        def step(j, dq):
            keys = pl.ds(pl.multiple_of(j * KEYS, KEYS), KEYS)
            p = jnp.exp2(dot(qfull[here, :], kT[:, keys]))
            ds = (p * dot(dofull[here, :], vT[:, keys])).astype(jnp.bfloat16)
            dv[:, keys] += dot(dot_ref[:, here], p.astype(jnp.bfloat16))
            dk[:, keys] += dot(tt_ref[0, :HD, here], ds)
            return dq + dot(ds, kx_ref[0, keys, :128])

        dq = lax.fori_loop(low // KEYS, (high + KEYS - 1) // KEYS, step, jnp.zeros((ROWS, 128), jnp.float32))
        dqT = jnp.transpose(dq)[:HD]
        grad_ref[:HD, here] = ((grad_ref[:HD, here].astype(jnp.float32) + dqT) * (1 / math.sqrt(HD))).astype(jnp.bfloat16)
    grad_ref[HD:2 * HD, :] = (dk[...] * (1 / math.sqrt(HD))).astype(jnp.bfloat16)
    grad_ref[2 * HD:, :] = dv[...].astype(jnp.bfloat16)
    me = lax.axis_index("tensor")
    for owner, part in zip((me, me + 1 - 2 * (me % 2), (me + 2) % n, n - 1 - me), (part0, part1, part2, part3)):
        part[...] = grad_ref[:, pl.ds(pl.multiple_of(owner * quarter, 128), quarter)]


def attend_back(head, n, lengths, marks, qx, kx, tt, ctx, lse, do):
    rows = tt.shape[2]
    per = lambda *s: pl.BlockSpec((1,) + s, lambda i: (head, 0, 0))
    slab = pl.BlockSpec((HD, rows), lambda i: (head, 0))
    whole = lambda *s: pl.BlockSpec(s, lambda i: (0,) * len(s))
    vm = pltpu.VMEM
    quarter = rows // n
    return pl.pallas_call(
        functools.partial(bwd_kernel, slots=lengths.shape[0], n=n),
        name="attend_back",
        grid=(1,),
        in_specs=[pl.BlockSpec(memory_space=pltpu.SMEM), whole(*marks.shape), per(rows, 128),
                  per(rows, 256), per(3 * HD, rows), slab, per(1, rows), slab],
        out_specs=[whole(3 * HD, rows)] + [whole(3 * HD, quarter)] * n,
        out_shape=[jax.ShapeDtypeStruct((3 * HD, rows), jnp.bfloat16)]
        + [jax.ShapeDtypeStruct((3 * HD, quarter), jnp.bfloat16)] * n,
        scratch_shapes=[vm((rows, 256), jnp.bfloat16), vm((256, rows), jnp.bfloat16), vm((rows, 128), jnp.bfloat16),
                        vm((128, rows), jnp.bfloat16), vm((HD, rows), jnp.float32), vm((HD, rows), jnp.float32)],
        cost_estimate=pl.CostEstimate(flops=15 * 10**9, bytes_accessed=6 * 2**20, transcendentals=0),
        compiler_params=pltpu.CompilerParams(vmem_limit_bytes=VMEM_LIMIT),
    )(lengths, marks, qx, kx, tt, ctx, lse, do)


GELU_C = math.sqrt(2 / math.pi)
CHUNK = 256


def mid_kernel(tok_ref, ctx_ref, cot_ref, wo_own, wu_own, wd_own, wo_far, wu_far, wd_far, wT_own, vec_hbm, mark_ref, vec_ref,
               out_ref, bh_ref, do_ref, wT_far, upk_ref, ups_ref, dnk_ref, dns_ref, ouk_ref, ous_ref, upsum_ref, sums_ref,
               wo, wu, wd, upb, cx, tok, cot, act, bp, hid, xhat, rstd, acc, bsec, n2, n2T, bf, bfT, atT, bcs, gr, gro, gso,
               loc_sem, w_send, w_recv, b_send, b_recv, c_send, c_recv, d_send, d_recv, d_loc, g_send, g_recv, o_sem, t_sem,
               *, n):
    quarter, feat = cot.shape
    width = ctx_ref.shape[0]
    chunks = quarter // CHUNK
    me = lax.axis_index("tensor")
    mesh_id = pl.DeviceIdType.MESH

    def other(r):
        return (me, me + 1 - 2 * (me % 2), (me + 2) % n, n - 1 - me)[r]

    def peer(r):
        return {"tensor": other(r)}

    def cols(owner, c):
        return pl.ds(pl.multiple_of(owner * quarter + c * CHUNK, CHUNK), CHUNK)

    barrier = pltpu.get_barrier_semaphore()
    for r in range(1, n):
        pl.semaphore_signal(barrier, inc=1, device_id=peer(r), device_id_type=mesh_id)
    pl.semaphore_wait(barrier, n - 1)

    ctx_copies = {}
    for c in range(chunks):
        for r in (2, 3, 1):
            copy = pltpu.make_async_remote_copy(
                src_ref=ctx_ref.at[:, cols(other(r), c)],
                dst_ref=cx.at[pl.ds(r * width, width), pl.ds(c * CHUNK, CHUNK)],
                send_sem=c_send.at[c * n + r], recv_sem=c_recv.at[c * n + r],
                device_id=peer(r), device_id_type=mesh_id)
            copy.start()
            ctx_copies[c, r] = copy
    own_ctx = pltpu.make_async_copy(
        ctx_ref.at[:, pl.ds(pl.multiple_of(me * quarter, CHUNK), quarter)], cx.at[pl.ds(0, width), :], loc_sem.at[0])
    rows_here = pl.ds(pl.multiple_of(me * quarter, CHUNK), quarter)
    tok_copy = pltpu.make_async_copy(tok_ref.at[rows_here, :], tok, loc_sem.at[1])
    cot_copy = pltpu.make_async_copy(cot_ref, cot, loc_sem.at[2])
    local = {}
    remote = {}
    for i, (own, far, buf) in enumerate(((wo_own, wo_far, wo), (wu_own, wu_far, wu), (wd_own, wd_far, wd))):
        size = own.shape[0]
        for r, src in ((0, own), (2, far)):
            dst = buf.at[pl.ds(r * size, size), :]
            local[i, r] = pltpu.make_async_copy(src, dst, loc_sem.at[3 + 2 * i + r // 2])
            dst = buf.at[pl.ds((r + 1) * size, size), :]
            remote[i, r + 1] = pltpu.make_async_remote_copy(
                src_ref=src, dst_ref=dst, send_sem=w_send.at[2 * i + r // 2], recv_sem=w_recv.at[2 * i + r // 2],
                device_id=peer(1), device_id_type=mesh_id)
    bias_copies = []
    for r in range(1, n):
        copy = pltpu.make_async_remote_copy(
            src_ref=vec_hbm, dst_ref=upb.at[r], send_sem=b_send.at[r], recv_sem=b_recv.at[r],
            device_id=peer(r), device_id_type=mesh_id)
        copy.start()
        bias_copies.append(copy)
    own_bias = pltpu.make_async_copy(vec_hbm, upb.at[0], loc_sem.at[9])
    own_ctx.start()
    tok_copy.start()
    cot_copy.start()
    own_bias.start()
    for i in range(3):
        for r in (0, 2):
            local[i, r].start()
            remote[i, r + 1].start()

    live_col = column(mark_ref[0:1, rows_here])
    flag_col = column(mark_ref[1:2, rows_here])
    cot_copy.wait()
    masked = jnp.where(live_col == 1.0, cot[...], jnp.zeros((), jnp.bfloat16))
    bf[...] = masked
    bfT[...] = jnp.transpose(masked)
    sums_ref[...] = jnp.zeros(sums_ref.shape, jnp.float32)
    sums_ref[3:4] = jnp.sum(masked.astype(jnp.float32), axis=0, keepdims=True)
    tok_copy.wait()
    own_ctx.wait()
    for r in (0, 2):
        local[0, r].wait()
        remote[0, r + 1].wait()
    gain = vec_ref[4:5]
    shift = vec_ref[5:6]
    for c in range(chunks):
        for r in (2, 3, 1):
            ctx_copies[c, r].wait()
        here = pl.ds(c * CHUNK, CHUNK)
        flag_c = flag_col[c * CHUNK:(c + 1) * CHUNK]
        x = jnp.where(flag_c == 1.0, vec_ref[0:1], tok[here, :].astype(jnp.float32))
        hidden = x + dot(cx[:, here], wo[...], 0, 0) + vec_ref[3:4]
        hid[here, :] = hidden
        sent = hidden.astype(jnp.bfloat16).astype(jnp.float32)
        centred = sent - jnp.mean(sent, axis=1, keepdims=True)
        scale = lax.rsqrt(jnp.mean(centred * centred, axis=1, keepdims=True) + EPS)
        normed = centred * scale
        xhat[here, :] = normed
        rstd[here, :] = jnp.broadcast_to(scale, (CHUNK, 128))
        second = (normed * gain + shift).astype(jnp.bfloat16)
        n2[here, :] = second
        n2T[:, here] = jnp.transpose(second)
    own_bias.wait()
    for copy in bias_copies:
        copy.wait()
    far_copy = pltpu.make_async_remote_copy(
        src_ref=wT_own, dst_ref=wT_far, send_sem=t_sem.at[0], recv_sem=t_sem.at[1], device_id=peer(2), device_id_type=mesh_id)
    far_copy.start()

    for r in range(n):
        if r % 2 == 0:
            local[1, r].wait()
            local[2, r].wait()
        else:
            remote[1, r].wait()
            remote[2, r].wait()
        up = wu.at[pl.ds(r * feat, feat), :]
        down = wd.at[pl.ds(r * wd_own.shape[0], wd_own.shape[0]), :]
        upsum_ref[r] = jnp.zeros(upsum_ref.shape[1:], jnp.float32)

        @pl.loop(0, chunks)
        def _(c):
            here = pl.ds(pl.multiple_of(c * CHUNK, CHUNK), CHUNK)
            pre = dot(n2[here, :], up[...]) + upb[r, 7:8, :]
            square = pre * pre
            inner = pre * (square * (GELU_C * 0.044715) + GELU_C)
            t = jnp.tanh(inner)
            half = 0.5 * t + 0.5
            a = pre * half
            slope = half + a * (1.0 - t) * (square * (3 * GELU_C * 0.044715) + GELU_C)
            low = a.astype(jnp.bfloat16)
            act[r, here, :] = low
            back = (dot(bf[here, :], down[...], 1, 1) * slope).astype(jnp.bfloat16)
            bp[r, here, :] = back
            upsum_ref[r, :1, :] += jnp.sum(back.astype(jnp.float32), axis=0, keepdims=True)
            out_part = dot(low, down[...])
            back_part = dot(back, up[...], 1, 1)
            if r == 0:
                acc[here, :] = out_part
                bsec[here, :] = back_part
            else:
                acc[here, :] += out_part
                bsec[here, :] += back_part

    bctx_copies = []
    for c in range(chunks):
        here = pl.ds(c * CHUNK, CHUNK)
        live_c = live_col[c * CHUNK:(c + 1) * CHUNK]
        ffn = (acc[here, :] + vec_ref[6:7]).astype(jnp.bfloat16).astype(jnp.float32)
        out_ref[here, :] = (hid[here, :] + jnp.where(live_c == 1.0, ffn, 0.0)).astype(jnp.bfloat16)
        back = bsec[here, :]
        normed = xhat[here, :]
        sums_ref[0:1] += jnp.sum(back * normed, axis=0, keepdims=True)
        sums_ref[1:2] += jnp.sum(back, axis=0, keepdims=True)
        m = back * gain
        back_sent = rstd[here, :1] * (
            m - jnp.mean(m, axis=1, keepdims=True) - normed * jnp.mean(m * normed, axis=1, keepdims=True))
        back_hidden = cot[here, :].astype(jnp.float32) + back_sent.astype(jnp.bfloat16).astype(jnp.float32)
        bh_ref[here, :] = back_hidden
        attn = back_hidden.astype(jnp.bfloat16)
        sums_ref[2:3] += jnp.sum(attn.astype(jnp.float32), axis=0, keepdims=True)
        atT[:, here] = jnp.transpose(attn)
        bcs[:, here] = dot(wo[...], attn, 1, 1).astype(jnp.bfloat16)
        for r in (2, 3, 1):
            copy = pltpu.make_async_remote_copy(
                src_ref=bcs.at[pl.ds(r * width, width), pl.ds(c * CHUNK, CHUNK)],
                dst_ref=do_ref.at[:, cols(me, c)],
                send_sem=d_send.at[c * n + r], recv_sem=d_recv.at[c * n + r],
                device_id=peer(r), device_id_type=mesh_id)
            copy.start()
            bctx_copies.append(copy)
        copy = pltpu.make_async_copy(
            bcs.at[pl.ds(0, width), pl.ds(c * CHUNK, CHUNK)], do_ref.at[:, cols(me, c)], d_loc.at[c])
        copy.start()
        bctx_copies.append(copy)

    hidden_units = wd_own.shape[0]
    grad_copies = {}
    for i, r in enumerate((1, 3)):
        up_slot = wd.at[pl.ds(2 * i * feat, feat), :]
        dn_slot = wd.at[pl.ds((2 * i + 1) * feat, feat), :]

        @pl.loop(0, feat // CHUNK)
        def _(c):
            here = pl.ds(pl.multiple_of(c * CHUNK, CHUNK), CHUNK)
            up_slot[here, :] = dot(n2T[here, :], bp[r]).astype(jnp.bfloat16)
            dn_slot[here, :] = dot(bfT[here, :], act[r]).astype(jnp.bfloat16)
            gso[i, here, :] = dot(atT[here, :], cx[r * width:(r + 1) * width, :], 1, 1).astype(jnp.bfloat16)

        for k, (src, dst) in enumerate(((up_slot, gr.at[2 * i]), (dn_slot, gr.at[2 * i + 1]), (gso.at[i], gro.at[i]))):
            copy = pltpu.make_async_remote_copy(
                src_ref=src, dst_ref=dst, send_sem=g_send.at[3 * i + k], recv_sem=g_recv.at[3 * i + k],
                device_id=peer(1), device_id_type=mesh_id)
            copy.start()
            grad_copies[i, k] = copy
    for i, (r, up_out, dn_out, ou_out) in enumerate(((0, upk_ref, dnk_ref, ouk_ref), (2, ups_ref, dns_ref, ous_ref))):
        up_slot = wu.at[pl.ds(2 * i * feat, feat), :]
        dn_slot = wu.at[pl.ds((2 * i + 1) * feat, feat), :]
        for k in range(3):
            grad_copies[i, k].wait()

        @pl.loop(0, feat // CHUNK)
        def _(c):
            here = pl.ds(pl.multiple_of(c * CHUNK, CHUNK), CHUNK)
            up_slot[here, :] = (dot(n2T[here, :], bp[r]) + gr[2 * i, here, :].astype(jnp.float32)).astype(jnp.bfloat16)
            dn_slot[here, :] = (dot(bfT[here, :], act[r]) + gr[2 * i + 1, here, :].astype(jnp.float32)).astype(jnp.bfloat16)
            ou_out[here, :] = (dot(atT[here, :], cx[r * width:(r + 1) * width, :], 1, 1)
                               + gro[i, here, :].astype(jnp.float32)).astype(jnp.bfloat16)

        for k, (src, dst) in enumerate(((up_slot, up_out), (dn_slot, dn_out))):
            copy = pltpu.make_async_copy(src, dst, o_sem.at[2 * i + k])
            copy.start()
            bctx_copies.append(copy)
    far_copy.wait()
    for copy in bctx_copies:
        copy.wait()


def middle(n, tokens, ctx, cotangent, own, far, wT, marks, vectors):
    quarter, feat = cotangent.shape
    width, rows = ctx.shape
    hidden_units = own[1].shape[1]
    vm, any_, vmem = pltpu.VMEM, pl.BlockSpec(memory_space=pl.ANY), pl.BlockSpec(memory_space=pltpu.VMEM)
    bf16, f32 = jnp.bfloat16, jnp.float32
    chunks = quarter // CHUNK
    sem = pltpu.SemaphoreType.DMA
    flops = 2 * quarter * feat * (6 * n * hidden_units + 3 * n * width)
    grads = [jax.ShapeDtypeStruct((feat, c), bf16) for c in (hidden_units, hidden_units, hidden_units, hidden_units, width, width)]
    return pl.pallas_call(
        functools.partial(mid_kernel, n=n),
        name="middle",
        in_specs=[any_] * 11 + [vmem] * 2,
        out_specs=[vmem, vmem] + [any_] * 6 + [vmem] * 4,
        out_shape=[jax.ShapeDtypeStruct((quarter, feat), bf16), jax.ShapeDtypeStruct((quarter, feat), f32),
                   jax.ShapeDtypeStruct((width, rows), bf16),
                   jax.ShapeDtypeStruct(wT.shape, bf16)] + grads + [
                   jax.ShapeDtypeStruct((n, 8, hidden_units), f32), jax.ShapeDtypeStruct((8, feat), f32)],
        scratch_shapes=[
            vm((n * width, feat), bf16), vm((n * feat, hidden_units), bf16), vm((n * hidden_units, feat), bf16),
            vm((n, 8, hidden_units), f32), vm((n * width, quarter), bf16), vm((quarter, feat), bf16), vm((quarter, feat), bf16),
            vm((n, quarter, hidden_units), bf16), vm((n, quarter, hidden_units), bf16),
            vm((quarter, feat), f32), vm((quarter, feat), f32), vm((quarter, 128), f32), vm((quarter, feat), f32),
            vm((quarter, feat), f32), vm((quarter, feat), bf16), vm((feat, quarter), bf16), vm((quarter, feat), bf16),
            vm((feat, quarter), bf16), vm((feat, quarter), bf16), vm((n * width, quarter), bf16),
            vm((4, feat, hidden_units), bf16), vm((2, feat, width), bf16), vm((2, feat, width), bf16),
            sem((10,)), sem((6,)), sem((6,)), sem((n,)), sem((n,)), sem((chunks * n,)), sem((chunks * n,)),
            sem((chunks * n,)), sem((chunks * n,)), sem((chunks,)), sem((6,)), sem((6,)), sem((4,)), sem((2,)),
        ],
        cost_estimate=pl.CostEstimate(flops=flops, bytes_accessed=40 * 2**20, transcendentals=0),
        compiler_params=pltpu.CompilerParams(vmem_limit_bytes=60 * 2**20, collective_id=0, has_side_effects=True),
    )(tokens, ctx, cotangent, *own, *far, wT, vectors, marks, vectors)


def fin_kernel(g_refs, blocks0, blocks1, blocks2, wT_own, wT_far, fn_ref, bh_ref, tok_ref, mark_ref, vec_ref, upsum_ref, sums_ref,
               grad_ref, qkv_ref, early_ref, late_ref,
               wall, blk, fn, g, bh, tok, acc, gw, gw_in, e_own, e_t, e_dp, l_own, l_t, l_dp,
               loc_sem, w_send, w_recv, a_send, a_recv, p_send, p_recv, es, er, fs, fr, ls, lr, ms, mr, *, n, dp):
    quarter, feat = acc.shape
    heads = len(g_refs)
    part = g_refs[0].shape[0]
    chunks = quarter // CHUNK
    me = lax.axis_index("tensor")
    dp_me = lax.axis_index("dp")
    mesh_id = pl.DeviceIdType.MESH

    def peer(r):
        return {"tensor": (me, me + 1 - 2 * (me % 2), (me + 2) % n, n - 1 - me)[r]}

    def dp_peer(d):
        return {"dp": (dp_me + d) % dp}

    barrier = pltpu.get_barrier_semaphore()
    for r in range(1, n):
        pl.semaphore_signal(barrier, inc=1, device_id=peer(r), device_id_type=mesh_id)
    for d in range(1, dp):
        pl.semaphore_signal(barrier, inc=1, device_id=dp_peer(d), device_id_type=mesh_id)
    pl.semaphore_wait(barrier, n + dp - 2)

    last = heads - 1
    arrivals = {}
    for c in range(chunks):
        here = pl.ds(c * CHUNK, CHUNK)
        for r in (2, 3, 1):
            copy = pltpu.make_async_remote_copy(
                src_ref=blocks2[r].at[:, here], dst_ref=blk.at[pl.ds((last * n + r) * part, part), here],
                send_sem=a_send.at[c * n + r], recv_sem=a_recv.at[c * n + r], device_id=peer(r), device_id_type=mesh_id)
            copy.start()
            arrivals[c, r] = copy
    waits = []
    sem = iter(range(loc_sem.shape[0]))
    fn_copy = pltpu.make_async_copy(fn_ref, fn, loc_sem.at[next(sem)])
    fn_copy.start()
    g_copies = []
    for h in range(heads):
        copy = pltpu.make_async_copy(g_refs[h], g.at[pl.ds(h * part, part), :], loc_sem.at[next(sem)])
        copy.start()
        g_copies.append(copy)
    for h in range(heads):
        for r, src in ((0, wT_own), (2, wT_far)):
            rows = src.at[pl.ds(h * part, part), :]
            copy = pltpu.make_async_copy(rows, wall.at[pl.ds((h * n + r) * part, part), :], loc_sem.at[next(sem)])
            copy.start()
            waits.append(copy)
            copy = pltpu.make_async_remote_copy(
                src_ref=rows, dst_ref=wall.at[pl.ds((h * n + r + 1) * part, part), :], send_sem=w_send.at[2 * h + r // 2],
                recv_sem=w_recv.at[2 * h + r // 2], device_id=peer(1), device_id_type=mesh_id)
            copy.start()
            waits.append(copy)
    for h, blocks in enumerate((blocks0, blocks1, blocks2)):
        for r in range(n if h < last else 1):
            copy = pltpu.make_async_copy(blocks[r], blk.at[pl.ds((h * n + r) * part, part), :], loc_sem.at[next(sem)])
            copy.start()
            waits.append(copy)
    rows_here = pl.ds(pl.multiple_of(me * quarter, CHUNK), quarter)
    for src, dst in ((bh_ref, bh), (tok_ref.at[rows_here, :], tok)):
        copy = pltpu.make_async_copy(src, dst, loc_sem.at[next(sem)])
        copy.start()
        waits.append(copy)

    fn_copy.wait()
    for copy in g_copies:
        copy.wait()
    for h in range(heads):
        wide = jnp.transpose(dot(g[h * part:(h + 1) * part, :], fn[...]))
        for p in range(dp):
            size = feat // dp
            gw[p, :, h * part:(h + 1) * part] = wide[p * size:(p + 1) * size].astype(jnp.bfloat16)
    gw_copies = []
    for d in range(1, dp):
        copy = pltpu.make_async_remote_copy(
            src_ref=gw.at[(dp_me + d) % dp], dst_ref=gw_in.at[d], send_sem=p_send.at[d], recv_sem=p_recv.at[d],
            device_id=dp_peer(d), device_id_type=mesh_id)
        copy.start()
        gw_copies.append(copy)
    bias = dot(jnp.ones((8, g.shape[1]), jnp.bfloat16), g[...], 1, 1)[:1]
    e_own[...] = jnp.zeros(e_own.shape, jnp.float32)
    zero = lambda k: [jnp.zeros((1, k), jnp.float32)] if k else []
    for row, k in ((0, 0), (1, 2)):
        piece = jnp.concatenate([bias[:, h * part + k * HD:h * part + (k + 1) * HD] for h in range(heads)], axis=1)
        size = piece.shape[1]
        total = jnp.zeros((1, feat), jnp.float32)
        for i in range(n):
            placed = jnp.concatenate(zero(i * size) + [piece] + zero((n - 1 - i) * size), axis=1)
            total = jnp.where(me == i, placed, total)
        e_own[row:row + 1] = total
    e_own[2:6] = sums_ref[:4]
    for i in range(n):
        row = jnp.zeros((1, feat), jnp.float32)
        for r, owner in enumerate((me, me + 1 - 2 * (me % 2), (me + 2) % n, n - 1 - me)):
            row = jnp.where(owner == i, upsum_ref[r, :1, :], row)
        e_own[6 + i:7 + i] = row
    e_copies = []
    for r in range(1, n):
        copy = pltpu.make_async_remote_copy(src_ref=e_own, dst_ref=e_t.at[r], send_sem=es.at[r], recv_sem=er.at[r],
                                            device_id=peer(r), device_id_type=mesh_id)
        copy.start()
        e_copies.append(copy)

    for copy in waits:
        copy.wait()
    first = last * n * part
    for c in range(chunks):
        here = pl.ds(c * CHUNK, CHUNK)
        acc[here, :] = dot(blk[:first, here], wall[:first], 0, 0)
    total = e_own[...]
    for r, copy in enumerate(e_copies):
        copy.wait()
        total = total + e_t[r + 1]
    e_dp[0] = total
    f_copies = []
    for d in range(1, dp):
        copy = pltpu.make_async_remote_copy(src_ref=e_dp.at[0], dst_ref=e_dp.at[d], send_sem=fs.at[d], recv_sem=fr.at[d],
                                            device_id=dp_peer(d), device_id_type=mesh_id)
        copy.start()
        f_copies.append(copy)

    flag_col = column(mark_ref[1:2, rows_here])
    emb = vec_ref[0:1]
    gain = vec_ref[1:2]
    mask_sum = jnp.zeros((1, feat), jnp.float32)
    gain_sum = jnp.zeros((1, feat), jnp.float32)
    bias_sum = jnp.zeros((1, feat), jnp.float32)
    for c in range(chunks):
        here = pl.ds(c * CHUNK, CHUNK)
        flag = flag_col[c * CHUNK:(c + 1) * CHUNK] == 1.0
        for r in (2, 3, 1):
            arrivals[c, r].wait()
        back = acc[here, :] + dot(blk[first:, here], wall[first:], 0, 0)
        x = jnp.where(flag, emb, tok[here, :].astype(jnp.float32))
        centred = x - jnp.mean(x, axis=1, keepdims=True)
        scale = lax.rsqrt(jnp.mean(centred * centred, axis=1, keepdims=True) + EPS)
        normed = centred * scale
        gain_sum += jnp.sum(back * normed, axis=0, keepdims=True)
        bias_sum += jnp.sum(back, axis=0, keepdims=True)
        m = back * gain
        back_in = bh[here, :] + scale * (
            m - jnp.mean(m, axis=1, keepdims=True) - normed * jnp.mean(m * normed, axis=1, keepdims=True))
        grad_ref[here, :] = jnp.where(flag, 0.0, back_in)
        mask_sum += jnp.sum(jnp.where(flag, back_in, 0.0), axis=0, keepdims=True)

    l_own[...] = jnp.zeros(l_own.shape, jnp.float32)
    lanes = feat // 128
    for i, row in enumerate((mask_sum, gain_sum, bias_sum)):
        for j in range(lanes):
            l_own[i * lanes + j:i * lanes + j + 1] = row[:, j * 128:(j + 1) * 128]
    l_copies = []
    for r in range(1, n):
        copy = pltpu.make_async_remote_copy(src_ref=l_own, dst_ref=l_t.at[r], send_sem=ls.at[r], recv_sem=lr.at[r],
                                            device_id=peer(r), device_id_type=mesh_id)
        copy.start()
        l_copies.append(copy)
    total = l_own[...]
    for r, copy in enumerate(l_copies):
        copy.wait()
        total = total + l_t[r + 1]
    l_dp[0] = total
    m_copies = []
    for d in range(1, dp):
        copy = pltpu.make_async_remote_copy(src_ref=l_dp.at[0], dst_ref=l_dp.at[d], send_sem=ms.at[d], recv_sem=mr.at[d],
                                            device_id=dp_peer(d), device_id_type=mesh_id)
        copy.start()
        m_copies.append(copy)
    qkv = gw[dp_me].astype(jnp.float32)
    for d, copy in enumerate(gw_copies):
        copy.wait()
        qkv = qkv + gw_in[d + 1].astype(jnp.float32)
    qkv_ref[...] = qkv
    total = e_dp[0]
    for d, copy in enumerate(f_copies):
        copy.wait()
        total = total + e_dp[d + 1]
    early_ref[...] = total
    total = l_dp[0]
    for d, copy in enumerate(m_copies):
        copy.wait()
        total = total + l_dp[d + 1]
    late_ref[...] = total


def finish(n, dp, grads, blocks, wT_own, wT_far, first_norm, back_hidden, tokens, marks, vectors, upsum, sums):
    quarter, feat = back_hidden.shape
    part, rows = grads[0].shape
    heads = len(grads)
    chunks = quarter // CHUNK
    vm, any_, vmem = pltpu.VMEM, pl.BlockSpec(memory_space=pl.ANY), pl.BlockSpec(memory_space=pltpu.VMEM)
    bf16, f32 = jnp.bfloat16, jnp.float32
    sem = pltpu.SemaphoreType.DMA
    late_rows = -(-3 * (feat // 128) // 8) * 8

    def body(*refs):
        k = heads * (1 + n)
        groups = [refs[heads + i * n:heads + (i + 1) * n] for i in range(heads)]
        fin_kernel(refs[:heads], *groups, *refs[k:], n=n, dp=dp)

    flat = [b for group in blocks for b in group]
    return pl.pallas_call(
        body,
        name="finish",
        in_specs=[any_] * (len(grads) + len(flat) + 5) + [vmem] * 4,
        out_specs=[vmem] * 4,
        out_shape=[jax.ShapeDtypeStruct((quarter, feat), f32), jax.ShapeDtypeStruct((feat // dp, heads * part), f32),
                   jax.ShapeDtypeStruct((16, feat), f32), jax.ShapeDtypeStruct((late_rows, 128), f32)],
        scratch_shapes=[
            vm((heads * n * part, feat), bf16), vm((heads * n * part, quarter), bf16), vm((rows, feat), bf16),
            vm((heads * part, rows), bf16), vm((quarter, feat), f32), vm((quarter, feat), bf16), vm((quarter, feat), f32),
            vm((dp, feat // dp, heads * part), bf16), vm((dp, feat // dp, heads * part), bf16),
            vm((16, feat), f32), vm((n, 16, feat), f32), vm((dp, 16, feat), f32),
            vm((late_rows, 128), f32), vm((n, late_rows, 128), f32), vm((dp, late_rows, 128), f32),
            sem((32,)), sem((2 * heads,)), sem((2 * heads,)), sem((chunks * n,)), sem((chunks * n,)), sem((dp,)), sem((dp,)),
            sem((n,)), sem((n,)), sem((dp,)), sem((dp,)), sem((n,)), sem((n,)), sem((dp,)), sem((dp,)),
        ],
        cost_estimate=pl.CostEstimate(flops=8 * 10**9, bytes_accessed=25 * 2**20, transcendentals=0),
        compiler_params=pltpu.CompilerParams(vmem_limit_bytes=60 * 2**20, collective_id=1, has_side_effects=True),
    )(*grads, *flat, wT_own, wT_far, first_norm, back_hidden, tokens, marks, vectors, upsum, sums)


def pack_kernel(qkv_ref, early_ref, late_ref, a_refs, b_refs, c_refs, q_out, k_out, v_out, up_out, down_out, out_out, *vec_refs):
    heads = q_out.shape[1] // HD
    for n, out in enumerate((q_out, k_out, v_out)):
        for h in range(heads):
            out[:, h * HD:(h + 1) * HD] = qkv_ref[:, (3 * h + n) * HD:(3 * h + n + 1) * HD]
    wide = lambda refs: sum(r[...].astype(jnp.float32) for r in refs)
    up_out[...] = wide(a_refs)
    down_out[...] = wide(b_refs)
    out_out[...] = jnp.transpose(wide(c_refs))
    feat = early_ref.shape[1]
    lanes = feat // 128
    for i in range(3):
        for j in range(lanes):
            vec_refs[i][j * 128:(j + 1) * 128] = late_ref[i * lanes + j, :]
    for i in range(6):
        vec_refs[3 + i][...] = early_ref[i, :]
    size = vec_refs[9].shape[0] // 4
    for i in range(4):
        vec_refs[9][i * size:(i + 1) * size] = early_ref[6 + i, :]


def pack(qkv, early, late, a, b, c, up_units):
    rows, width = qkv.shape[0], qkv.shape[1] // 3
    feat = early.shape[1]
    f32 = jnp.float32
    vmem = pl.BlockSpec(memory_space=pltpu.VMEM)
    counts = (len(a), len(b), len(c))

    def body(*refs):
        i, j, k = 3 + counts[0], 3 + counts[0] + counts[1], 3 + sum(counts)
        pack_kernel(*refs[:3], refs[3:i], refs[i:j], refs[j:k], *refs[k:])

    shape = lambda *s: jax.ShapeDtypeStruct(s, f32)
    return pl.pallas_call(
        body,
        name="pack",
        in_specs=[vmem] * (3 + sum(counts)),
        out_specs=[vmem] * 16,
        out_shape=[shape(rows, width)] * 3 + [shape(rows, a[0].shape[1]), shape(rows, b[0].shape[1]), shape(c[0].shape[1], rows)]
        + [shape(feat)] * 9 + [shape(up_units)],
        compiler_params=pltpu.CompilerParams(vmem_limit_bytes=VMEM_LIMIT),
    )(qkv, early, late, *a, *b, *c)


def swap(array, axis, distance):
    return lax.ppermute(array, axis, [(i, i ^ distance) for i in range(lax.axis_size(axis))])


def add(*parts):
    return sum(part.astype(jnp.float32) for part in parts)


def pick(array, index, axis):
    return lax.dynamic_index_in_dim(array, index, axis, keepdims=False)


def per_device(
    tokens,
    token_mask,
    masked_flags,
    doc_lengths,
    mask_embedding,
    ln1_gain,
    ln1_bias,
    w_query,
    query_bias,
    w_key,
    w_value,
    value_bias,
    w_out,
    out_bias,
    ln2_gain,
    ln2_bias,
    w_up,
    up_bias,
    w_down,
    down_bias,
    cotangent,
):
    row_total, feat = tokens.shape
    n = lax.axis_size("tensor")
    me = lax.axis_index("tensor")
    dp_size = lax.axis_size("dp")
    dp_me = lax.axis_index("dp")
    quarter = row_total // n
    width = w_query.shape[1]
    heads = width // HD
    hidden_units = w_up.shape[1]
    f32, bf16 = jnp.float32, jnp.bfloat16

    marks = jnp.stack([token_mask, masked_flags])
    vectors = jnp.stack(
        [v.astype(f32) for v in (mask_embedding, ln1_gain, ln1_bias, out_bias, ln2_gain, ln2_bias, down_bias, up_bias)]
    )
    qv_bias = jnp.stack([query_bias.astype(f32), value_bias.astype(f32)])
    own = (w_out, w_up, w_down)
    far = tuple(swap(w, "tensor", 2) for w in own)
    first_norm, query_pair, key_wide, head_rows, wT = project(
        doc_lengths, tokens, marks, vectors, qv_bias, w_query.T, w_key.T, w_value.T
    )
    context, log_totals = attend(doc_lengths, marks, key_wide, head_rows)
    (layer_output, back_hidden, back_context, wT_far, up_keep, up_send, down_keep, down_send, out_keep, out_send,
     up_sums, sums) = middle(n, tokens, context, cotangent, own, far, wT, marks, vectors)

    low_count = 2
    high_count = dp_size // low_count
    dp_low, dp_high = dp_me % low_count, dp_me // low_count

    def over_y(keep, send):
        return add(keep, swap(send, "tensor", 2)).astype(bf16)

    def over_x(piece, axis):
        return add(pick(piece, dp_low, axis), swap(pick(piece, 1 - dp_low, axis), "dp", 1)).astype(bf16)

    def over_z(piece, axis):
        parts = [pick(piece, dp_high, axis)]
        for d in range(1, high_count):
            parts.append(swap(pick(piece, dp_high ^ d, axis), "dp", low_count * d))
        return add(*parts).astype(bf16)

    rows_of = feat // dp_size
    split = lambda g: g.reshape(high_count, low_count, rows_of, g.shape[1])
    grads, blocks = [], []

    def back(head, do):
        full, *parts = attend_back(head, n, doc_lengths, marks, query_pair, key_wide, head_rows, context, log_totals, do)
        grads.append(full)
        blocks.append(parts)

    def exchange(parts):
        return [parts[0]] + [swap(parts[r], "tensor", r) for r in range(1, n)]

    a = over_y(up_keep, up_send)
    b = over_x(jnp.stack([split(down_keep), split(down_send)]), 2)
    c = over_z(jnp.stack([split(out_keep), split(out_send)]), 1)
    back(0, back_context)
    blocks[0] = exchange(blocks[0])
    do, a, b, c = lax.optimization_barrier((back_context, a, b, c))
    a = over_x(split(a), 1)
    b = over_z(b, 1)
    c = over_y(c[0], c[1])
    back(1, do)
    blocks[1] = exchange(blocks[1])
    do, a, b, c = lax.optimization_barrier((do, a, b, c))
    def over_last_z(piece):
        return [pick(piece, dp_high, 0)] + [swap(pick(piece, dp_high ^ d, 0), "dp", low_count * d) for d in range(1, high_count)]
    a = over_last_z(a)
    b = [b[0], swap(b[1], "tensor", 2)]
    c = [pick(c, dp_low, 0), swap(pick(c, 1 - dp_low, 0), "dp", 1)]
    back(2, do)
    input_grad, qkv, early, late = finish(
        n, dp_size, grads, blocks, wT, wT_far, first_norm, back_hidden, tokens, marks, vectors, up_sums, sums
    )
    (gq, gk, gv, grad_up, grad_down, grad_out, mask_sum, gain1, bias1, q_bias, v_bias, gain2, bias2, o_bias, d_bias,
     u_bias) = pack(qkv, early, late, a, b, c, n * hidden_units)
    return (layer_output, input_grad, mask_sum, gain1, bias1, gq, q_bias, gk, gv, v_bias, grad_out, o_bias, gain2, bias2,
            grad_up, u_bias, grad_down.T, d_bias)


def solution(mesh):
    in_specs = (
        P("dp", None),
        P("dp"),
        P("dp"),
        P("dp"),
        P(),
        P(),
        P(),
        P(None, "tensor"),
        P("tensor"),
        P(None, "tensor"),
        P(None, "tensor"),
        P("tensor"),
        P("tensor", None),
        P(),
        P(),
        P(),
        P(None, "tensor"),
        P("tensor"),
        P("tensor", None),
        P(),
        P(("dp", "tensor"), None),
    )
    out_specs = (
        P(("dp", "tensor"), None),
        P(("dp", "tensor"), None),
        P(),
        P(),
        P(),
        P("dp", "tensor"),
        P(),
        P("dp", "tensor"),
        P("dp", "tensor"),
        P(),
        P("tensor", "dp"),
        P(),
        P(),
        P(),
        P("dp", "tensor"),
        P(),
        P("tensor", "dp"),
        P(),
    )
    return jax.shard_map(
        per_device, mesh=mesh, in_specs=in_specs, out_specs=out_specs, check_vma=False
    )
```

```python
import functools, math
import jax, jax.numpy as jnp
from jax import lax
from jax.experimental import pallas as pl
from jax.experimental.pallas import tpu as pltpu
from jax.sharding import PartitionSpec as P

HD = 64
EPS = 1e-05
NEG = -2e30
LOG2E = 1.4426950408889634
VMEM_LIMIT = 56 * 2**20
ROWS = 512
KEYS = 1024
START = 256


def dot(a, b, ca=1, cb=0):
    return lax.dot_general(a, b, (((ca,), (cb,)), ((), ())), preferred_element_type=jnp.float32)


def doc_bounds(len_ref, slots, axis):
    shape = (1, 128) if axis == 1 else (128, 1)
    place = lax.broadcasted_iota(jnp.int32, shape, axis)
    starts = jnp.zeros(shape, jnp.int32)
    ends = jnp.zeros(shape, jnp.int32)
    begin = jnp.int32(0)
    for slot in range(slots):
        end = begin + len_ref[slot]
        starts = jnp.where(place == slot, begin, starts)
        ends = jnp.where(place == slot, end, ends)
        begin = end
    return starts, ends


def column(row):
    wide = jnp.broadcast_to(row.astype(jnp.float32), (8, row.shape[1]))
    return jnp.transpose(wide)[:, :1]


def proj_kernel(len_ref, tok_ref, live_ref, flag_ref, *refs, heads, slots):
    flat, (bq_ref, bv_ref, wq_ref, wk_ref, wv_ref, fn_ref, qx_ref, kx_ref, tt_ref, wT_ref, vec_ref, mark_ref, wdup, bcol,
           qv_ref) = refs[:8], refs[8:]
    step = pl.program_id(0)
    width = heads * HD

    @pl.when(step == 0)
    def _():
        for i, ref in enumerate(flat):
            vec_ref[i:i + 1] = ref[...].astype(jnp.float32).reshape(1, -1)
        for i, ref in enumerate((bq_ref, bv_ref)):
            qv_ref[i:i + 1] = ref[...].astype(jnp.float32).reshape(1, -1)
        zero = jnp.zeros((1, HD), jnp.float32)
        rows = []
        for h in range(heads):
            piece = slice(h * HD, (h + 1) * HD)
            for n, w in enumerate((wq_ref, wk_ref, wv_ref)):
                begin = (3 * h + n) * HD
                wT_ref[begin:begin + HD, :] = w[piece, :]
                if n < 2:
                    for copy in range(2):
                        begin = ((2 * h + n) * 2 + copy) * HD
                        wdup[begin:begin + HD, :] = w[piece, :]
            rows += [qv_ref[0:1, piece], zero, qv_ref[1:2, piece]]
        bcol[...] = jnp.transpose(jnp.broadcast_to(jnp.concatenate(rows, axis=1), (8, 3 * width)))

    here = pl.ds(pl.multiple_of(step * ROWS, ROWS), ROWS)
    mark_ref[0:1] = live_ref[here].reshape(1, ROWS)
    mark_ref[1:2] = flag_ref[here].reshape(1, ROWS)
    live = column(mark_ref[0:1, :])
    flags = column(mark_ref[1:2, :])
    x = jnp.where(flags == 1.0, vec_ref[0:1], tok_ref[...].astype(jnp.float32))
    mean = jnp.mean(x, axis=1, keepdims=True)
    c = x - mean
    var = jnp.mean(c * c, axis=1, keepdims=True)
    fn = (c * lax.rsqrt(var + EPS) * vec_ref[1:2] + vec_ref[2:3]).astype(jnp.bfloat16)
    fn_ref[...] = fn
    starts, ends = doc_bounds(len_ref, slots, 1)
    row = step * ROWS + lax.broadcasted_iota(jnp.int32, (ROWS, 128), 0)
    lane = lax.broadcasted_iota(jnp.int32, (ROWS, 128), 1)
    member = (row >= starts) & (row < ends)
    pen = jnp.where(member & (live == 1.0), 0.0, NEG)
    pen = jnp.where(lane < 16, pen, jnp.where(lane < 19, 1.0, 0.0)).astype(jnp.bfloat16)
    both = dot(fn, wdup[...], 1, 1)
    for h in range(heads):
        bq = qv_ref[0:1, h * HD:(h + 1) * HD]
        q = (both[:, 2 * h * 128:(2 * h + 1) * 128] + jnp.concatenate([bq, bq], axis=1)).astype(jnp.bfloat16)
        q = q.astype(jnp.float32) * (LOG2E / math.sqrt(HD))
        high = q.astype(jnp.bfloat16).astype(jnp.float32)
        qx_ref[h] = jnp.where(lane < HD, high, q - high).astype(jnp.bfloat16)
        kx_ref[h, :, :128] = both[:, (2 * h + 1) * 128:(2 * h + 2) * 128].astype(jnp.bfloat16)
        kx_ref[h, :, 128:] = pen
    tt = (dot(wT_ref[...], fn, 1, 1) + bcol[:, :1]).astype(jnp.bfloat16)
    for h in range(heads):
        tt_ref[h] = tt[h * 3 * HD:(h + 1) * 3 * HD, :]


def project(lengths, tokens, live, flags, vectors, biases, wqT, wkT, wvT):
    rows, feat = tokens.shape
    width = wqT.shape[0]
    heads = width // HD
    whole = lambda s: pl.BlockSpec(s, lambda i, *_: (0,) * len(s))
    return pl.pallas_call(
        functools.partial(proj_kernel, heads=heads, slots=lengths.shape[0]),
        name="project",
        grid_spec=pltpu.PrefetchScalarGridSpec(
            num_scalar_prefetch=1,
            grid=(rows // ROWS,),
            in_specs=[
                pl.BlockSpec((ROWS, feat), lambda i, *_: (i, 0)),
                whole((rows,)), whole((rows,)), *[whole((feat,))] * 8, whole((width,)), whole((width,)),
                whole((width, feat)), whole((width, feat)), whole((width, feat)),
            ],
            out_specs=[
                pl.BlockSpec((ROWS, feat), lambda i, *_: (i, 0)),
                pl.BlockSpec((heads, ROWS, 128), lambda i, *_: (0, i, 0)),
                pl.BlockSpec((heads, ROWS, 256), lambda i, *_: (0, i, 0)),
                pl.BlockSpec((heads, 3 * HD, ROWS), lambda i, *_: (0, 0, i)),
                whole((3 * width, feat)), whole((8, feat)), pl.BlockSpec((2, ROWS), lambda i, *_: (0, i)),
            ],
            scratch_shapes=[
                pltpu.VMEM((heads * 256, feat), jnp.bfloat16),
                pltpu.VMEM((3 * width, 8), jnp.float32),
                pltpu.VMEM((8, width), jnp.float32),
            ],
        ),
        out_shape=[
            jax.ShapeDtypeStruct((rows, feat), jnp.bfloat16),
            jax.ShapeDtypeStruct((heads, rows, 128), jnp.bfloat16),
            jax.ShapeDtypeStruct((heads, rows, 256), jnp.bfloat16),
            jax.ShapeDtypeStruct((heads, 3 * HD, rows), jnp.bfloat16),
            jax.ShapeDtypeStruct((3 * width, feat), jnp.bfloat16),
            jax.ShapeDtypeStruct((8, feat), jnp.float32),
            jax.ShapeDtypeStruct((2, rows), jnp.int32),
        ],
        compiler_params=pltpu.CompilerParams(vmem_limit_bytes=VMEM_LIMIT),
    )(lengths, tokens, live, flags, *vectors, *biases, wqT, wkT, wvT)


def key_range(len_ref, slots, first, last, live_end):
    begin = jnp.int32(0)
    low = jnp.int32(0)
    high = jnp.int32(0)
    for slot in range(slots):
        end = begin + len_ref[slot]
        low = jnp.where((first >= begin) & (first < end), begin, low)
        high = jnp.where((last >= begin) & (last < end), end, high)
        begin = end
    return low, jnp.minimum(high, live_end)


def key_blocks(low, high, rows):
    begin = low // START * START
    span = jnp.maximum(high - begin, 0)
    half = KEYS // 2
    whole = span // KEYS
    halves = (span - whole * KEYS + half - 1) // half
    begin = jnp.minimum(begin, rows - whole * KEYS - halves * half)
    return begin, whole, halves


def over_keys(low, high, rows, step, state):
    begin, whole, halves = key_blocks(low, high, rows)
    state = lax.fori_loop(0, whole, lambda j, s: step(pl.multiple_of(begin + j * KEYS, START), KEYS, s), state)
    rest = begin + whole * KEYS
    return lax.fori_loop(0, halves, lambda j, s: step(pl.multiple_of(rest + j * (KEYS // 2), START), KEYS // 2, s), state)


def last_live(live_row):
    place = lax.broadcasted_iota(jnp.int32, live_row.shape, 1)
    return jnp.max(jnp.where(live_row == 1, place + 1, 0))


def one_hot_rows(len_ref, slots, first, count):
    starts, ends = doc_bounds(len_ref, slots, 0)
    place = first + lax.broadcasted_iota(jnp.int32, (16, count), 1)
    return (place >= starts[:16]) & (place < ends[:16])


def fwd_kernel(len_ref, live_ref, kx_ref, tt_ref, ctx_ref, lse_ref, qx, *, heads, slots):
    rows = tt_ref.shape[2]
    blocks = rows // ROWS
    live_end = last_live(live_ref[0:1, :])

    @pl.loop(0, blocks)
    def _(i):
        first = pl.multiple_of(i * ROWS, ROWS)
        here = pl.ds(first, ROWS)
        low, high = key_range(len_ref, slots, first, first + ROWS - 1, live_end)
        hot = jnp.where(one_hot_rows(len_ref, slots, first, ROWS), 1.0, 0.0)
        dead = live_ref[0:1, here] != 1
        state = []
        for h in range(heads):
            q = tt_ref[h, :HD, here].astype(jnp.float32)
            k = tt_ref[h, HD:2 * HD, here].astype(jnp.float32)
            v = tt_ref[h, 2 * HD:, here].astype(jnp.float32)
            scaled = q * (LOG2E / math.sqrt(HD))
            top = scaled.astype(jnp.bfloat16)
            qx[h, :HD] = top
            qx[h, HD:128] = (scaled - top.astype(jnp.float32)).astype(jnp.bfloat16)
            qx[h, 128:] = jnp.concatenate([hot, jnp.zeros((112, ROWS), jnp.float32)], axis=0).astype(jnp.bfloat16)
            own = jnp.sum(scaled * k, axis=0, keepdims=True)
            state += [jnp.where(dead, own, -1e30), jnp.where(dead, 1.0, 0.0), jnp.where(dead, v, 0.0)]

        def step(begin, count, carried):
            keys = pl.ds(begin, count)
            out = []
            scores = [dot(kx_ref[h, keys, :], qx[h]) for h in range(heads)]
            tops = [jnp.maximum(carried[3 * h], jnp.max(scores[h], axis=0, keepdims=True)) for h in range(heads)]
            probs = [jnp.exp2(scores[h] - tops[h]).astype(jnp.bfloat16) for h in range(heads)]
            for h in range(heads):
                _, total, acc = carried[3 * h:3 * h + 3]
                fade = jnp.exp2(carried[3 * h] - tops[h])
                both = dot(jnp.concatenate([tt_ref[h, 2 * HD:, keys], jnp.ones((16, count), jnp.bfloat16)], axis=0), probs[h])
                out += [tops[h], total * fade + both[HD:HD + 1], acc * fade + both[:HD]]
            return tuple(out)

        state = over_keys(low, high, rows, step, tuple(state))
        for h in range(heads):
            top, total, acc = state[3 * h:3 * h + 3]
            ctx_ref[h * HD:(h + 1) * HD, here] = (acc / total).astype(jnp.bfloat16)
            lse_ref[h, :, here] = top + jnp.log2(total)


def attend(lengths, marks, kx, tt):
    heads, _, rows = tt.shape
    vmem = pl.BlockSpec(memory_space=pltpu.VMEM)
    return pl.pallas_call(
        functools.partial(fwd_kernel, heads=heads, slots=lengths.shape[0]),
        name="attend",
        in_specs=[pl.BlockSpec(memory_space=pltpu.SMEM), vmem, vmem, vmem],
        out_specs=[vmem, vmem],
        out_shape=[jax.ShapeDtypeStruct((heads * HD, rows), jnp.bfloat16), jax.ShapeDtypeStruct((heads, 1, rows), jnp.float32)],
        scratch_shapes=[pltpu.VMEM((heads, 256, ROWS), jnp.bfloat16)],
        compiler_params=pltpu.CompilerParams(vmem_limit_bytes=VMEM_LIMIT),
    )(lengths, marks, kx, tt)


def split3(x):
    a = x.astype(jnp.bfloat16).astype(jnp.float32)
    b = (x - a).astype(jnp.bfloat16).astype(jnp.float32)
    return a, b, x - a - b


def bwd_kernel(len_ref, live_ref, qx_ref, kx_ref, tt_ref, ctx_ref, lse_ref, dot_ref, fn_ref, *refs, slots, n, chained):
    held, refs = refs[:(n + 1) * chained], refs[(n + 1) * chained:]
    part_refs, (bias_ref, gw_ref, grad_ref, qfull, kT, dofull, vT, dk, dv, fn, sems) = refs[:n], refs[n:]
    rows = tt_ref.shape[2]
    quarter = rows // n
    copies = [pltpu.make_async_copy(fn_ref, fn, sems.at[n])]
    for i in range(n * chained):
        copies.append(pltpu.make_async_copy(held[i], part_refs[i].at[pl.ds(0, 3 * HD), :], sems.at[i]))
    for copy in copies:
        copy.start()
    blocks = rows // ROWS
    live_end = last_live(live_ref[0:1, :])
    lane_zero = jnp.zeros
    qfull[:, 128:] = jnp.zeros((rows, 128), jnp.bfloat16)
    dofull[...] = jnp.zeros(dofull.shape, jnp.bfloat16)
    kT[:HD] = tt_ref[0, HD:2 * HD, :]
    kT[HD:128] = tt_ref[0, HD:2 * HD, :]
    starts, ends = doc_bounds(len_ref, slots, 0)
    vT[:HD] = tt_ref[0, 2 * HD:, :]
    ones = jnp.where(lax.broadcasted_iota(jnp.int32, (16, ROWS), 0) < 3, 1.0, 0.0)

    @pl.loop(0, blocks)
    def _(i):
        first = pl.multiple_of(i * ROWS, ROWS)
        here = pl.ds(first, ROWS)
        member = one_hot_rows(len_ref, slots, first, ROWS)
        alive = live_ref[0:1, here] == 1
        dead = jnp.logical_not(alive)
        pen = jnp.where(member & alive, 0.0, NEG)
        kT[128:, here] = jnp.concatenate([pen, ones, lane_zero((96, ROWS), jnp.float32)], axis=0).astype(jnp.bfloat16)
        vT[HD:, here] = jnp.concatenate([ones, lane_zero((48, ROWS), jnp.float32)], axis=0).astype(jnp.bfloat16)
        q = tt_ref[0, :HD, here].astype(jnp.float32)
        k = tt_ref[0, HD:2 * HD, here].astype(jnp.float32)
        v = tt_ref[0, 2 * HD:, here].astype(jnp.float32)
        do = dot_ref[:, here].astype(jnp.float32)
        delta = jnp.sum(do * ctx_ref[:, here].astype(jnp.float32), axis=0, keepdims=True)
        lse = lse_ref[0, :, here]
        parts = jnp.concatenate([-x for x in split3(lse)], axis=0)
        rest = jnp.concatenate([jnp.where(member, 1.0, 0.0), parts, lane_zero((13, ROWS), jnp.float32)], axis=0)
        qfull[here, :128] = qx_ref[0, here, :]
        qfull[here, 128:160] = jnp.transpose(rest.astype(jnp.bfloat16))
        parts = jnp.concatenate([-x for x in split3(delta)], axis=0)
        rest = jnp.concatenate([do, parts, lane_zero((13, ROWS), jnp.float32)], axis=0)
        dofull[here, :80] = jnp.transpose(rest.astype(jnp.bfloat16))
        p = jnp.where(dead, jnp.exp2(jnp.sum(q * k, axis=0, keepdims=True) * (LOG2E / math.sqrt(HD)) - lse), 0.0)
        ds = p * (jnp.sum(do * v, axis=0, keepdims=True) - delta)
        dk[:, here] = ds * q
        dv[:, here] = p * do
        grad_ref[:HD, here] = (ds * k).astype(jnp.bfloat16)

    @pl.loop(0, blocks)
    def _(i):
        first = pl.multiple_of(i * ROWS, ROWS)
        here = pl.ds(first, ROWS)
        low, high = key_range(len_ref, slots, first, first + ROWS - 1, live_end)

        def step(begin, count, dq):
            keys = [pl.ds(begin + u, min(count, 512)) for u in range(0, count, 512)]
            scores = [dot(qfull[here, :], kT[:, key]) for key in keys]
            backs = [dot(dofull[here, :], vT[:, key]) for key in keys]
            for key, score, back in zip(keys, scores, backs):
                p = jnp.exp2(score)
                ds = (p * back).astype(jnp.bfloat16)
                dv[:, key] += dot(dot_ref[:, here], p.astype(jnp.bfloat16))
                dk[:, key] += dot(tt_ref[0, :HD, here], ds)
                dq = dq + dot(ds, kx_ref[0, key, :])
            return dq

        dq = over_keys(low, high, rows, step, jnp.zeros((ROWS, 128), jnp.float32))
        dqT = jnp.transpose(dq)[:HD]
        grad_ref[:HD, here] = ((grad_ref[:HD, here].astype(jnp.float32) + dqT) * (1 / math.sqrt(HD))).astype(jnp.bfloat16)
    grad_ref[HD:2 * HD, :] = (dk[...] * (1 / math.sqrt(HD))).astype(jnp.bfloat16)
    grad_ref[2 * HD:, :] = dv[...].astype(jnp.bfloat16)
    me = lax.axis_index("tensor")
    for owner, part in zip((me, me + 1 - 2 * (me % 2), (me + 2) % n, n - 1 - me), part_refs):
        part[3 * HD * chained:, :] = grad_ref[:, pl.ds(pl.multiple_of(owner * quarter, 128), quarter)]
    bias_ref[...] = dot(jnp.ones((8, rows), jnp.bfloat16), grad_ref[...], 1, 1)
    for copy in copies:
        copy.wait()
    gw = jnp.transpose(dot(grad_ref[...], fn[...])).astype(jnp.bfloat16)
    gw_ref[...] = jnp.concatenate([held[n][...], gw], axis=1) if chained else gw


def attend_back(head, n, lengths, marks, qx, kx, tt, ctx, lse, do, fn, held=()):
    rows = tt.shape[2]
    per = lambda *s: pl.BlockSpec((1,) + s, lambda i: (head, 0, 0))
    slab = pl.BlockSpec((HD, rows), lambda i: (head, 0))
    whole = lambda *s: pl.BlockSpec(s, lambda i: (0,) * len(s))
    any_ = pl.BlockSpec(memory_space=pl.ANY)
    vm = pltpu.VMEM
    quarter, feat = rows // n, fn.shape[1]
    chained = 1 if held else 0
    wide = 3 * HD * (1 + chained)
    return pl.pallas_call(
        functools.partial(bwd_kernel, slots=lengths.shape[0], n=n, chained=chained),
        name="attend_back",
        grid=(1,),
        in_specs=[pl.BlockSpec(memory_space=pltpu.SMEM), whole(*marks.shape), per(rows, 128),
                  per(rows, 128), per(3 * HD, rows), slab, per(1, rows), slab, any_]
        + ([any_] * n + [whole(feat, 3 * HD)]) * chained,
        out_specs=[whole(wide, quarter)] * n + [whole(8, 3 * HD), whole(feat, wide)],
        out_shape=[jax.ShapeDtypeStruct((wide, quarter), jnp.bfloat16)] * n
        + [jax.ShapeDtypeStruct((8, 3 * HD), jnp.float32), jax.ShapeDtypeStruct((feat, wide), jnp.bfloat16)],
        scratch_shapes=[vm((3 * HD, rows), jnp.bfloat16), vm((rows, 256), jnp.bfloat16), vm((256, rows), jnp.bfloat16), vm((rows, 128), jnp.bfloat16),
                        vm((128, rows), jnp.bfloat16), vm((HD, rows), jnp.float32), vm((HD, rows), jnp.float32), vm((rows, feat), jnp.bfloat16),
                        pltpu.SemaphoreType.DMA((n + 1,))],
        cost_estimate=pl.CostEstimate(flops=15 * 10**9, bytes_accessed=6 * 2**20, transcendentals=0),
        compiler_params=pltpu.CompilerParams(vmem_limit_bytes=VMEM_LIMIT),
    )(lengths, marks, qx, kx, tt, ctx, lse, do, fn, *held)


GELU_C = math.sqrt(2 / math.pi)
CHUNK = 256


def mid_kernel(tok_ref, ctx_ref, cot_ref, wo_own, wu_own, wd_own, wo_far, far_ref, wT_own, vec_hbm, mark_ref, vec_ref,
               out_ref, bh_ref, do_ref, wT_far, upkk_ref, upks_ref, ups_ref, dnk_ref, dns_ref, upsum_ref, sums_ref,
               wo, ws, upb, cx, tok, cot, act, bp, hid, xhat, rstd, acc, bsec, n2, n2T, bf, bfT, atT, bcs, gr, gro, gso, ga, gb,
               loc_sem, w_send, w_recv, b_send, b_recv, c_send, c_recv, d_send, d_recv, d_loc, g_send, g_recv, o_sem, t_sem, h_sem,
               *, n, dp):
    quarter, feat = cot.shape
    width = ctx_ref.shape[0]
    chunks = quarter // CHUNK
    wu, wd = ws.at[0], ws.at[1]
    me = lax.axis_index("tensor")
    dp_me = lax.axis_index("dp")
    mesh_id = pl.DeviceIdType.MESH

    def other(r):
        return (me, me + 1 - 2 * (me % 2), (me + 2) % n, n - 1 - me)[r]

    def peer(r):
        return {"tensor": other(r)}

    def cols(owner, c):
        return pl.ds(pl.multiple_of(owner * quarter + c * CHUNK, CHUNK), CHUNK)

    def by_low(ref, columns, value):
        low_count, size = 2, value.shape[0] // dp
        for p in range(dp):
            q = p % low_count * (dp // low_count) + p // low_count
            ref[q * size:(q + 1) * size, columns] = value[p * size:(p + 1) * size]

    barrier = pltpu.get_barrier_semaphore()
    for r in range(1, n):
        pl.semaphore_signal(barrier, inc=1, device_id=peer(r), device_id_type=mesh_id)
    x_peer = {"dp": dp_me + 1 - 2 * (dp_me % 2)}
    z_peer = {"dp": dp_me + 2 - 4 * (dp_me // 2 % 2)}
    for device in (x_peer, z_peer):
        pl.semaphore_signal(barrier, inc=1, device_id=device, device_id_type=mesh_id)
    pl.semaphore_wait(barrier, n + 1)

    ctx_copies = {}
    for c in range(chunks):
        for r in (2, 3, 1):
            ctx_copies[c, r] = pltpu.make_async_remote_copy(
                src_ref=ctx_ref.at[:, cols(other(r), c)],
                dst_ref=cx.at[pl.ds(r * width, width), pl.ds(c * CHUNK, CHUNK)],
                send_sem=c_send.at[c * n + r], recv_sem=c_recv.at[c * n + r],
                device_id=peer(r), device_id_type=mesh_id)
    for r in (2, 3, 1):
        ctx_copies[0, r].start()
    own_ctx = pltpu.make_async_copy(
        ctx_ref.at[:, pl.ds(pl.multiple_of(me * quarter, CHUNK), quarter)], cx.at[pl.ds(0, width), :], loc_sem.at[0])
    rows_here = pl.ds(pl.multiple_of(me * quarter, CHUNK), quarter)
    tok_copy = pltpu.make_async_copy(tok_ref.at[rows_here, :], tok, loc_sem.at[1])
    cot_copy = pltpu.make_async_copy(cot_ref, cot, loc_sem.at[2])
    hidden_units = wd_own.shape[0]
    local, remote = {}, {}
    for i, (own, buf) in enumerate(((wo_own, wo), (wu_own, wu), (wd_own, wd))):
        size = own.shape[0]
        for r, src in ((0, own), (2, wo_far))[:2 if i == 0 else 1]:
            local[i, r] = pltpu.make_async_copy(src, buf.at[pl.ds(r * size, size), :], loc_sem.at[3 + 2 * i + r // 2])
            remote[i, r + 1] = pltpu.make_async_remote_copy(
                src_ref=src, dst_ref=buf.at[pl.ds((r + 1) * size, size), :], send_sem=w_send.at[2 * i + r // 2],
                recv_sem=w_recv.at[2 * i + r // 2], device_id=peer(1), device_id_type=mesh_id)
    have = (dp_me % 2 + dp_me // 2) % 2
    lack = 1 - have
    slot = lambda r, first, count: pl.ds(r * feat + first, count)
    held_here = pltpu.make_async_copy(far_ref, ws.at[have, slot(2, 0, feat), :], loc_sem.at[6])
    held_beside = pltpu.make_async_remote_copy(
        src_ref=far_ref, dst_ref=ws.at[have, slot(3, 0, feat), :], send_sem=w_send.at[3], recv_sem=w_recv.at[3],
        device_id=peer(1), device_id_type=mesh_id)
    part = feat // 2
    lacked = [
        pltpu.make_async_remote_copy(
            src_ref=far_ref.at[pl.ds(i * part, part), :], dst_ref=ws.at[have, slot(2, i * part, part), :],
            send_sem=h_sem.at[2 * i], recv_sem=h_sem.at[2 * i + 1], device_id=device, device_id_type=mesh_id)
        for i, device in enumerate((x_peer, z_peer))
    ]
    beside = pltpu.make_async_remote_copy(
        src_ref=ws.at[lack, slot(2, 0, feat), :], dst_ref=ws.at[lack, slot(3, 0, feat), :], send_sem=w_send.at[5],
        recv_sem=w_recv.at[5], device_id=peer(1), device_id_type=mesh_id)
    far_copy = pltpu.make_async_remote_copy(
        src_ref=wT_own, dst_ref=wT_far, send_sem=t_sem.at[0], recv_sem=t_sem.at[1], device_id=peer(2), device_id_type=mesh_id)
    bias_copies = []
    for r in range(1, n):
        copy = pltpu.make_async_remote_copy(
            src_ref=vec_hbm, dst_ref=upb.at[r], send_sem=b_send.at[r], recv_sem=b_recv.at[r],
            device_id=peer(r), device_id_type=mesh_id)
        copy.start()
        bias_copies.append(copy)
    own_bias = pltpu.make_async_copy(vec_hbm, upb.at[0], loc_sem.at[9])
    own_ctx.start()
    tok_copy.start()
    cot_copy.start()
    own_bias.start()
    for copy in (*local.values(), *remote.values(), *lacked, held_here, held_beside):
        copy.start()

    live_col = column(mark_ref[0:1, rows_here])
    flag_col = column(mark_ref[1:2, rows_here])
    cot_copy.wait()
    masked = jnp.where(live_col == 1.0, cot[...], jnp.zeros((), jnp.bfloat16))
    bf[...] = masked
    by_low(bfT, slice(None), jnp.transpose(masked))
    sums_ref[...] = jnp.zeros(sums_ref.shape, jnp.float32)
    sums_ref[3:4] = jnp.sum(masked.astype(jnp.float32), axis=0, keepdims=True)
    tok_copy.wait()
    own_ctx.wait()
    for r in (0, 2):
        local[0, r].wait()
        remote[0, r + 1].wait()
    for i in (1, 2):
        local[i, 0].wait()
        remote[i, 1].wait()
    own_bias.wait()
    for copy in bias_copies:
        copy.wait()
    gain = vec_ref[4:5]
    shift = vec_ref[5:6]
    upsum_ref[...] = jnp.zeros(upsum_ref.shape, jnp.float32)

    def feed(c, first):
        here = pl.ds(c * CHUNK, CHUNK)

        @pl.loop(first, first + n // 2)
        def _(r):
            up = wu.at[pl.ds(pl.multiple_of(r * feat, feat), feat), :]
            down = wd.at[pl.ds(pl.multiple_of(r * hidden_units, hidden_units), hidden_units), :]
            pre = dot(n2[here, :], up[...]) + upb[r, 7:8, :]
            square = pre * pre
            t = jnp.tanh(pre * (square * (GELU_C * 0.044715) + GELU_C))
            half = 0.5 * t + 0.5
            a = pre * half
            slope = half + a * (1.0 - t) * (square * (3 * GELU_C * 0.044715) + GELU_C)
            low = a.astype(jnp.bfloat16)
            act[r, here, :] = low
            back = (dot(bf[here, :], down[...], 1, 1) * slope).astype(jnp.bfloat16)
            bp[r, here, :] = back
            upsum_ref[r, :1, :] += jnp.sum(back.astype(jnp.float32), axis=0, keepdims=True)
            acc[here, :] += dot(low, down[...])
            bsec[here, :] += dot(back, up[...], 1, 1)

    for c in range(chunks):
        for r in (2, 3, 1):
            ctx_copies[c, r].wait()
        if c + 1 < chunks:
            for r in (2, 3, 1):
                ctx_copies[c + 1, r].start()
        else:
            far_copy.start()
        here = pl.ds(c * CHUNK, CHUNK)
        flag_c = flag_col[c * CHUNK:(c + 1) * CHUNK]
        x = jnp.where(flag_c == 1.0, vec_ref[0:1], tok[here, :].astype(jnp.float32))
        hidden = x + dot(cx[:, here], wo[...], 0, 0) + vec_ref[3:4]
        hid[here, :] = hidden
        sent = hidden.astype(jnp.bfloat16).astype(jnp.float32)
        centred = sent - jnp.mean(sent, axis=1, keepdims=True)
        scale = lax.rsqrt(jnp.mean(centred * centred, axis=1, keepdims=True) + EPS)
        normed = centred * scale
        xhat[here, :] = normed
        rstd[here, :] = jnp.broadcast_to(scale, (CHUNK, 128))
        second = (normed * gain + shift).astype(jnp.bfloat16)
        n2[here, :] = second
        by_low(n2T, here, jnp.transpose(second))
        acc[here, :] = jnp.zeros((CHUNK, feat), jnp.float32)
        bsec[here, :] = jnp.zeros((CHUNK, feat), jnp.float32)
        feed(c, 0)
    for copy in (held_here, held_beside, *lacked):
        copy.wait()
    beside.start()
    grad_copies = {}

    def send_grad(i, k, src, dst):
        copy = pltpu.make_async_remote_copy(
            src_ref=src, dst_ref=dst, send_sem=g_send.at[3 * i + k], recv_sem=g_recv.at[3 * i + k],
            device_id=peer(1), device_id_type=mesh_id)
        copy.start()
        grad_copies[i, k] = copy

    def neighbour_grads(i, r):
        for k, (first, second) in enumerate(((n2T, bp), (bfT, act))):
            place = wd.at[pl.ds((2 * i + k) * feat, feat), :]
            place[...] = dot(first[...], second[r]).astype(jnp.bfloat16)
            send_grad(i, k, place, gr.at[2 * i + k])

    neighbour_grads(0, 1)
    beside.wait()

    bctx_copies = []
    for c in range(chunks):
        feed(c, n // 2)
        here = pl.ds(c * CHUNK, CHUNK)
        live_c = live_col[c * CHUNK:(c + 1) * CHUNK]
        ffn = (acc[here, :] + vec_ref[6:7]).astype(jnp.bfloat16).astype(jnp.float32)
        out_ref[here, :] = (hid[here, :] + jnp.where(live_c == 1.0, ffn, 0.0)).astype(jnp.bfloat16)
        back = bsec[here, :]
        normed = xhat[here, :]
        sums_ref[0:1] += jnp.sum(back * normed, axis=0, keepdims=True)
        sums_ref[1:2] += jnp.sum(back, axis=0, keepdims=True)
        m = back * gain
        back_sent = rstd[here, :1] * (
            m - jnp.mean(m, axis=1, keepdims=True) - normed * jnp.mean(m * normed, axis=1, keepdims=True))
        back_hidden = cot[here, :].astype(jnp.float32) + back_sent.astype(jnp.bfloat16).astype(jnp.float32)
        bh_ref[here, :] = back_hidden
        attn = back_hidden.astype(jnp.bfloat16)
        sums_ref[2:3] += jnp.sum(attn.astype(jnp.float32), axis=0, keepdims=True)
        by_low(atT, here, jnp.transpose(attn))
        bcs[:, here] = dot(wo[...], attn, 1, 1).astype(jnp.bfloat16)
        for r in (2, 3, 1):
            copy = pltpu.make_async_remote_copy(
                src_ref=bcs.at[pl.ds(r * width, width), pl.ds(c * CHUNK, CHUNK)],
                dst_ref=do_ref.at[:, cols(me, c)],
                send_sem=d_send.at[c * n + r], recv_sem=d_recv.at[c * n + r],
                device_id=peer(r), device_id_type=mesh_id)
            copy.start()
            bctx_copies.append(copy)
        copy = pltpu.make_async_copy(
            bcs.at[pl.ds(0, width), pl.ds(c * CHUNK, CHUNK)], do_ref.at[:, cols(me, c)], d_loc.at[c])
        copy.start()
        bctx_copies.append(copy)

    neighbour_grads(1, 3)
    for i, r in ((0, 1), (1, 3)):
        gso[i] = dot(atT[...], cx[r * width:(r + 1) * width, :], 1, 1).astype(jnp.bfloat16)
        send_grad(i, 2, gso.at[i], gro.at[i])
    half = feat // 2
    low = dp_me % 2
    mine = pl.ds(pl.multiple_of(low * half, half), half)
    other_half = pl.ds(pl.multiple_of((1 - low) * half, half), half)
    side = width // 2
    for i, r in ((0, 0), (1, 2)):
        for k in range(3):
            grad_copies[i, k].wait()
        out_grad = dot(atT[...], cx[r * width:(r + 1) * width, :], 1, 1) + gro[i].astype(jnp.float32)
        pad = jnp.zeros((feat, ga.shape[2] - hidden_units - side), jnp.float32)
        for buf, first, second, slot, cut in ((ga, n2T, bp, 2 * i, slice(0, side)), (gb, bfT, act, 2 * i + 1, slice(side, width))):
            buf[i, :, :hidden_units] = (dot(first[...], second[r]) + gr[slot].astype(jnp.float32)).astype(jnp.bfloat16)
            buf[i, :, hidden_units:] = jnp.concatenate([out_grad[:, cut], pad], axis=1).astype(jnp.bfloat16)
        places = ((upkk_ref, upks_ref), (ups_ref.at[0], ups_ref.at[1]))[i]
        for k, (src, dst) in enumerate(((ga.at[i, mine, :], places[0]), (ga.at[i, other_half, :], places[1]),
                                        (gb.at[i, mine, :], dnk_ref.at[i]), (gb.at[i, other_half, :], dns_ref.at[i]))):
            copy = pltpu.make_async_copy(src, dst, o_sem.at[4 * i + k])
            copy.start()
            bctx_copies.append(copy)
    far_copy.wait()
    for copy in bctx_copies:
        copy.wait()


def middle(n, dp, tokens, ctx, cotangent, own, out_far, far, wT, marks, vectors):
    quarter, feat = cotangent.shape
    width, rows = ctx.shape
    hidden_units = own[1].shape[1]
    vm, any_, vmem = pltpu.VMEM, pl.BlockSpec(memory_space=pl.ANY), pl.BlockSpec(memory_space=pltpu.VMEM)
    bf16, f32 = jnp.bfloat16, jnp.float32
    chunks = quarter // CHUNK
    sem = pltpu.SemaphoreType.DMA
    flops = 2 * quarter * feat * (6 * n * hidden_units + 3 * n * width)
    wide = -(-(hidden_units + width // 2) // 128) * 128
    grads = [jax.ShapeDtypeStruct(s, bf16) for s in (
        (feat // 2, wide), (feat // 2, wide), (2, feat // 2, wide), (2, feat // 2, wide), (2, feat // 2, wide))]
    return pl.pallas_call(
        functools.partial(mid_kernel, n=n, dp=dp),
        name="middle",
        in_specs=[any_] * 10 + [vmem] * 2,
        out_specs=[vmem, vmem] + [any_] * 7 + [vmem] * 2,
        out_shape=[jax.ShapeDtypeStruct((quarter, feat), bf16), jax.ShapeDtypeStruct((quarter, feat), f32),
                   jax.ShapeDtypeStruct((width, rows), bf16),
                   jax.ShapeDtypeStruct(wT.shape, bf16)] + grads + [
                   jax.ShapeDtypeStruct((n, 8, hidden_units), f32), jax.ShapeDtypeStruct((8, feat), f32)],
        scratch_shapes=[
            vm((n * width, feat), bf16), vm((2, n * feat, hidden_units), bf16),
            vm((n, 8, hidden_units), f32), vm((n * width, quarter), bf16), vm((quarter, feat), bf16), vm((quarter, feat), bf16),
            vm((n, quarter, hidden_units), bf16), vm((n, quarter, hidden_units), bf16),
            vm((quarter, feat), f32), vm((quarter, feat), f32), vm((quarter, 128), f32), vm((quarter, feat), f32),
            vm((quarter, feat), f32), vm((quarter, feat), bf16), vm((feat, quarter), bf16), vm((quarter, feat), bf16),
            vm((feat, quarter), bf16), vm((feat, quarter), bf16), vm((n * width, quarter), bf16),
            vm((4, feat, hidden_units), bf16), vm((2, feat, width), bf16), vm((2, feat, width), bf16),
            vm((2, feat, wide), bf16), vm((2, feat, wide), bf16),
            sem((10,)), sem((6,)), sem((6,)), sem((n,)), sem((n,)), sem((chunks * n,)), sem((chunks * n,)),
            sem((chunks * n,)), sem((chunks * n,)), sem((chunks,)), sem((6,)), sem((6,)), sem((8,)), sem((2,)), sem((4,)),
        ],
        cost_estimate=pl.CostEstimate(flops=flops, bytes_accessed=40 * 2**20, transcendentals=0),
        compiler_params=pltpu.CompilerParams(vmem_limit_bytes=60 * 2**20, collective_id=0, has_side_effects=True),
    )(tokens, ctx, cotangent, *own, out_far, far, wT, vectors, marks, vectors)


def fin_kernel(early_blocks, last_blocks, gw_refs, b_refs, wT_own, wT_far, bh_ref, tok_ref, mark_ref, vec_ref, upsum_ref, sums_ref,
               grad_ref, qkv0_ref, qkv1_ref, early_ref, late_ref,
               wall, blk, bh, tok, acc, gw_mine, gw_x, gw_z, e_own, e_t, e_dp, l_own, l_t, l_dp,
               loc_sem, w_send, w_recv, a_send, a_recv, x_send, x_recv, p_send, p_recv, es, er, fs, fr, hs, hr, ls, lr, ms, mr, *, n, dp):
    qkv_refs = (qkv0_ref, qkv1_ref)
    quarter, feat = acc.shape
    heads = len(b_refs)
    part = last_blocks[0].shape[0]
    chunks = quarter // CHUNK
    me = lax.axis_index("tensor")
    dp_me = lax.axis_index("dp")
    mesh_id = pl.DeviceIdType.MESH

    def other(r):
        return (me, me + 1 - 2 * (me % 2), (me + 2) % n, n - 1 - me)[r]

    def peer(r):
        return {"tensor": other(r)}

    def dp_peer(d):
        return {"dp": (dp_me + d) % dp}

    barrier = pltpu.get_barrier_semaphore()
    for r in range(1, n):
        pl.semaphore_signal(barrier, inc=1, device_id=peer(r), device_id_type=mesh_id)
    for d in range(1, dp):
        pl.semaphore_signal(barrier, inc=1, device_id=dp_peer(d), device_id_type=mesh_id)
    pl.semaphore_wait(barrier, n + dp - 2)

    last = heads - 1
    arrivals = {}
    for c in range(chunks):
        here = pl.ds(c * CHUNK, CHUNK)
        for r in (2, 3, 1):
            copy = pltpu.make_async_remote_copy(
                src_ref=last_blocks[r].at[:, here], dst_ref=blk.at[pl.ds((last * n + r) * part, part), here],
                send_sem=a_send.at[c * n + r], recv_sem=a_recv.at[c * n + r], device_id=peer(r), device_id_type=mesh_id)
            copy.start()
            arrivals[c, r] = copy
    waits = []
    sem = iter(range(loc_sem.shape[0]))
    low_count = 2
    high_count = dp // low_count
    low, high = dp_me % low_count, dp_me // low_count
    x_copies = []
    for z in range(high_count):
        for k, ref in enumerate(gw_refs):
            copy = pltpu.make_async_remote_copy(
                src_ref=ref.at[z * low_count + 1 - low], dst_ref=gw_x[k].at[z], send_sem=x_send.at[2 * z + k],
                recv_sem=x_recv.at[2 * z + k], device_id={"dp": dp_me + 1 - 2 * low}, device_id_type=mesh_id)
            copy.start()
            x_copies.append(copy)
            copy = pltpu.make_async_copy(ref.at[z * low_count + low], gw_mine[k].at[z], loc_sem.at[next(sem)])
            copy.start()
            x_copies.append(copy)
    for h in range(heads):
        for r, src in ((0, wT_own), (2, wT_far)):
            rows = src.at[pl.ds(h * part, part), :]
            copy = pltpu.make_async_copy(rows, wall.at[pl.ds((h * n + r) * part, part), :], loc_sem.at[next(sem)])
            copy.start()
            waits.append(copy)
            copy = pltpu.make_async_remote_copy(
                src_ref=rows, dst_ref=wall.at[pl.ds((h * n + r + 1) * part, part), :], send_sem=w_send.at[2 * h + r // 2],
                recv_sem=w_recv.at[2 * h + r // 2], device_id=peer(1), device_id_type=mesh_id)
            copy.start()
            waits.append(copy)
    pieces = [(last_blocks[0], last, 0)]
    pieces += [(early_blocks[r].at[pl.ds(h * part, part), :], h, r) for r in range(n) for h in range(last)]
    for src, h, r in pieces:
        copy = pltpu.make_async_copy(src, blk.at[pl.ds((h * n + r) * part, part), :], loc_sem.at[next(sem)])
        copy.start()
        waits.append(copy)
    rows_here = pl.ds(pl.multiple_of(me * quarter, CHUNK), quarter)
    for src, dst in ((bh_ref, bh), (tok_ref.at[rows_here, :], tok)):
        copy = pltpu.make_async_copy(src, dst, loc_sem.at[next(sem)])
        copy.start()
        waits.append(copy)

    e_own[...] = jnp.zeros(e_own.shape, jnp.float32)
    rows = []
    zero = lambda k: [jnp.zeros((1, k), jnp.float32)] if k else []
    for k in (0, 2):
        piece = jnp.concatenate([ref[:1, k * HD:(k + 1) * HD] for ref in b_refs], axis=1)
        size = piece.shape[1]
        total = jnp.zeros((1, feat), jnp.float32)
        for i in range(n):
            placed = jnp.concatenate(zero(i * size) + [piece] + zero((n - 1 - i) * size), axis=1)
            total = jnp.where(me == i, placed, total)
        rows.append(total)
    rows += [sums_ref[i:i + 1] for i in range(4)]
    for i in range(n):
        row = jnp.zeros((1, feat), jnp.float32)
        for r in range(n):
            row = jnp.where(other(r) == i, upsum_ref[r, :1, :], row)
        rows.append(row)
    share = -(-len(rows) // n)
    for i, row in enumerate(rows):
        e_own[i // share, i % share:i % share + 1] = row
    e_copies = []
    for r in range(1, n):
        copy = pltpu.make_async_remote_copy(src_ref=e_own.at[other(r)], dst_ref=e_t.at[r], send_sem=es.at[r], recv_sem=er.at[r],
                                            device_id=peer(r), device_id_type=mesh_id)
        copy.start()
        e_copies.append(copy)

    for copy in waits:
        copy.wait()
    first = last * n * part
    for c in range(chunks):
        here = pl.ds(c * CHUNK, CHUNK)
        acc[here, :] = dot(blk[:first, here], wall[:first], 0, 0)
    for copy in x_copies:
        copy.wait()
    for mine, arrived in zip(gw_mine, gw_x):
        mine[...] = (mine[...].astype(jnp.float32) + arrived[...].astype(jnp.float32)).astype(jnp.bfloat16)
    z_copies = []
    for d in range(1, high_count):
        for k, mine in enumerate(gw_mine):
            copy = pltpu.make_async_remote_copy(
                src_ref=mine.at[(high + d) % high_count], dst_ref=gw_z[k].at[d], send_sem=p_send.at[2 * d + k],
                recv_sem=p_recv.at[2 * d + k], device_id={"dp": (dp_me + d * low_count) % dp}, device_id_type=mesh_id)
            copy.start()
            z_copies.append(copy)
    total = e_own[me]
    for r, copy in enumerate(e_copies):
        copy.wait()
        total = total + e_t[r + 1]
    e_dp[0] = total
    f_copies = []
    for d in range(1, dp):
        copy = pltpu.make_async_remote_copy(src_ref=e_dp.at[0], dst_ref=e_dp.at[d], send_sem=fs.at[d], recv_sem=fr.at[d],
                                            device_id=dp_peer(d), device_id_type=mesh_id)
        copy.start()
        f_copies.append(copy)

    flag_col = column(mark_ref[1:2, rows_here])
    emb = vec_ref[0:1]
    gain = vec_ref[1:2]
    mask_sum = jnp.zeros((1, feat), jnp.float32)
    gain_sum = jnp.zeros((1, feat), jnp.float32)
    bias_sum = jnp.zeros((1, feat), jnp.float32)
    for c in range(chunks):
        here = pl.ds(c * CHUNK, CHUNK)
        flag = flag_col[c * CHUNK:(c + 1) * CHUNK] == 1.0
        for r in (2, 3, 1):
            arrivals[c, r].wait()
        back = acc[here, :] + dot(blk[first:, here], wall[first:], 0, 0)
        x = jnp.where(flag, emb, tok[here, :].astype(jnp.float32))
        centred = x - jnp.mean(x, axis=1, keepdims=True)
        scale = lax.rsqrt(jnp.mean(centred * centred, axis=1, keepdims=True) + EPS)
        normed = centred * scale
        gain_sum += jnp.sum(back * normed, axis=0, keepdims=True)
        bias_sum += jnp.sum(back, axis=0, keepdims=True)
        m = back * gain
        back_in = bh[here, :] + scale * (
            m - jnp.mean(m, axis=1, keepdims=True) - normed * jnp.mean(m * normed, axis=1, keepdims=True))
        grad_ref[here, :] = jnp.where(flag, 0.0, back_in)
        mask_sum += jnp.sum(jnp.where(flag, back_in, 0.0), axis=0, keepdims=True)

    total = e_dp[0]
    for d, copy in enumerate(f_copies):
        copy.wait()
        total = total + e_dp[d + 1]
    early_ref[me] = total
    h_copies = []
    for r in range(1, n):
        copy = pltpu.make_async_remote_copy(src_ref=early_ref.at[me], dst_ref=early_ref.at[me], send_sem=hs.at[r],
                                            recv_sem=hr.at[r], device_id=peer(r), device_id_type=mesh_id)
        copy.start()
        h_copies.append(copy)
    l_own[...] = jnp.zeros(l_own.shape, jnp.float32)
    lanes = feat // 128
    for i, row in enumerate((mask_sum, gain_sum, bias_sum)):
        for j in range(lanes):
            l_own[i * lanes + j:i * lanes + j + 1] = row[:, j * 128:(j + 1) * 128]
    l_copies = []
    for r in range(1, n):
        copy = pltpu.make_async_remote_copy(src_ref=l_own, dst_ref=l_t.at[r], send_sem=ls.at[r], recv_sem=lr.at[r],
                                            device_id=peer(r), device_id_type=mesh_id)
        copy.start()
        l_copies.append(copy)
    total = l_own[...]
    for r, copy in enumerate(l_copies):
        copy.wait()
        total = total + l_t[r + 1]
    l_dp[0] = total
    m_copies = []
    for d in range(1, dp):
        copy = pltpu.make_async_remote_copy(src_ref=l_dp.at[0], dst_ref=l_dp.at[d], send_sem=ms.at[d], recv_sem=mr.at[d],
                                            device_id=dp_peer(d), device_id_type=mesh_id)
        copy.start()
        m_copies.append(copy)
    for copy in z_copies:
        copy.wait()
    for k, mine in enumerate(gw_mine):
        qkv = mine[high].astype(jnp.float32)
        for d in range(1, high_count):
            qkv = qkv + gw_z[k][d].astype(jnp.float32)
        qkv_refs[k][...] = qkv
    for copy in h_copies:
        copy.wait()
    total = l_dp[0]
    for d, copy in enumerate(m_copies):
        copy.wait()
        total = total + l_dp[d + 1]
    late_ref[...] = total


def finish(n, dp, early_blocks, last_blocks, gws, biases, wT_own, wT_far, back_hidden, tokens, marks, vectors, upsum, sums):
    quarter, feat = back_hidden.shape
    part = last_blocks[0].shape[0]
    heads = len(biases)
    chunks = quarter // CHUNK
    vm, any_, vmem = pltpu.VMEM, pl.BlockSpec(memory_space=pl.ANY), pl.BlockSpec(memory_space=pltpu.VMEM)
    bf16, f32 = jnp.bfloat16, jnp.float32
    sem = pltpu.SemaphoreType.DMA
    late_rows = -(-3 * (feat // 128) // 8) * 8
    row_count = 6 + n
    share = -(-row_count // n)
    share = -(-share // 8) * 8

    def body(*refs):
        k = 2 * n + 2
        refs = list(refs)
        at = k + heads + 8 + 5 + 5
        fin_kernel(refs[:n], refs[n:2 * n], refs[2 * n:k], refs[k:k + heads], *refs[k + heads:at],
                   *(refs[at + 2 * i:at + 2 * i + 2] for i in range(3)), *refs[at + 6:], n=n, dp=dp)

    return pl.pallas_call(
        body,
        name="finish",
        in_specs=[any_] * (2 * n + 2) + [vmem] * heads + [any_] * 4 + [vmem] * 4,
        out_specs=[vmem] * 5,
        out_shape=[jax.ShapeDtypeStruct((quarter, feat), f32),
                   *(jax.ShapeDtypeStruct((feat // dp, g.shape[2]), f32) for g in gws),
                   jax.ShapeDtypeStruct((n, share, feat), f32), jax.ShapeDtypeStruct((late_rows, 128), f32)],
        scratch_shapes=[
            vm((heads * n * part, feat), bf16), vm((heads * n * part, quarter), bf16),
            vm((quarter, feat), f32), vm((quarter, feat), bf16), vm((quarter, feat), f32),
            *(vm((dp // 2, feat // dp, g.shape[2]), bf16) for _ in range(3) for g in gws),
            vm((n, share, feat), f32), vm((n, share, feat), f32), vm((dp, share, feat), f32),
            vm((late_rows, 128), f32), vm((n, late_rows, 128), f32), vm((dp, late_rows, 128), f32),
            sem((2 * dp + 32,)), sem((2 * heads,)), sem((2 * heads,)), sem((chunks * n,)), sem((chunks * n,)),
            sem((dp,)), sem((dp,)), sem((dp,)), sem((dp,)), sem((n,)), sem((n,)), sem((dp,)), sem((dp,)), sem((n,)), sem((n,)), sem((n,)), sem((n,)), sem((dp,)), sem((dp,)),
        ],
        cost_estimate=pl.CostEstimate(flops=8 * 10**9, bytes_accessed=25 * 2**20, transcendentals=0),
        compiler_params=pltpu.CompilerParams(vmem_limit_bytes=60 * 2**20, collective_id=1, has_side_effects=True),
    )(*early_blocks, *last_blocks, *gws, *biases, wT_own, wT_far, back_hidden, tokens, marks, vectors, upsum, sums)


def pack_kernel(early_ref, late_ref, gw01_ref, gw2_ref, piece_ref, q_out, k_out, v_out, up_out, down_out, out_out, *vec_refs):
    heads = q_out.shape[1] // HD
    for n, out in enumerate((q_out, k_out, v_out)):
        for h in range(heads):
            begin = (3 * h + n) * HD
            piece = gw01_ref[:, begin:begin + HD] if h < heads - 1 else gw2_ref[:, n * HD:(n + 1) * HD]
            out[:, h * HD:(h + 1) * HD] = piece.astype(jnp.float32)
    units, side = up_out.shape[1], out_out.shape[0] // 2
    total = sum(piece_ref[z].astype(jnp.float32) for z in range(piece_ref.shape[0]))
    second = total.shape[1] // 2
    up_out[...] = total[:, :units]
    down_out[...] = total[:, second:second + units]
    out_out[...] = jnp.transpose(
        jnp.concatenate([total[:, units:units + side], total[:, second + units:second + units + side]], axis=1))
    feat = early_ref.shape[2]
    lanes = feat // 128
    for i in range(3):
        for j in range(lanes):
            vec_refs[i][j * 128:(j + 1) * 128] = late_ref[i * lanes + j, :]
    n = vec_refs[9].shape[0] // units
    share = -(-(6 + n) // n)
    row = lambda i: early_ref[i // share, i % share, :]
    for i in range(6):
        vec_refs[3 + i][...] = row(i)
    for i in range(n):
        vec_refs[9][i * units:(i + 1) * units] = row(6 + i)


def pack(early, late, gw01, gw2, pieces, units, up_units):
    rows, width = gw01.shape[0], (gw01.shape[1] + gw2.shape[1]) // 3
    feat = early.shape[2]
    vmem = pl.BlockSpec(memory_space=pltpu.VMEM)
    shape = lambda *s: jax.ShapeDtypeStruct(s, jnp.float32)
    return pl.pallas_call(
        pack_kernel,
        name="pack",
        in_specs=[vmem] * 5,
        out_specs=[vmem] * 16,
        out_shape=[shape(rows, width)] * 3 + [shape(rows, units), shape(rows, units), shape(width, rows)]
        + [shape(feat)] * 9 + [shape(up_units)],
        compiler_params=pltpu.CompilerParams(vmem_limit_bytes=VMEM_LIMIT),
    )(early, late, gw01, gw2, pieces)


def fold_kernel(up_ref, up_in, down_ref, down_in, up_out, down_out):
    up_out[...] = (up_ref[...].astype(jnp.float32) + up_in[0].astype(jnp.float32)).astype(jnp.bfloat16)
    down_out[...] = (down_ref[0].astype(jnp.float32) + down_in[0].astype(jnp.float32)).astype(jnp.bfloat16)


def fold(up, up_in, down, down_in):
    half, units = up.shape
    wide = down.shape[2]
    size = half // 3 if half % 48 == 0 else half
    one = lambda c: pl.BlockSpec((1, size, c), lambda i: (1, i, 0))
    flat = lambda c: pl.BlockSpec((size, c), lambda i: (i, 0))
    return pl.pallas_call(
        fold_kernel,
        name="fold",
        grid=(half // size,),
        in_specs=[flat(units), one(units), one(wide), one(wide)],
        out_specs=[flat(units), flat(wide)],
        out_shape=[jax.ShapeDtypeStruct((half, units), jnp.bfloat16), jax.ShapeDtypeStruct((half, wide), jnp.bfloat16)],
        compiler_params=pltpu.CompilerParams(vmem_limit_bytes=VMEM_LIMIT),
    )(up, up_in, down, down_in)


def deal_kernel(up_ref, up_in, up_in2, down_ref, down_in, down_in2, out_ref):
    units = up_ref.shape[-1]
    wide = lambda *refs: sum(ref[...].reshape(out_ref.shape[1], -1).astype(jnp.float32) for ref in refs)
    out_ref[0, :, :units] = wide(up_ref, up_in, up_in2).astype(jnp.bfloat16)
    out_ref[0, :, units:] = wide(down_ref, down_in, down_in2).astype(jnp.bfloat16)


def deal(count, up, up_in, up_in2, down, down_in, down_in2):
    half, units = up.shape
    wide = down.shape[2]
    size = half // count
    cut = lambda a: a.reshape(a.shape[:-2] + (count, size, a.shape[-1]))
    one = lambda c: pl.BlockSpec((1, 1, size, c), lambda i: (0, i, 0, 0))
    flat = lambda c: pl.BlockSpec((1, size, c), lambda i: (i, 0, 0))
    return pl.pallas_call(
        deal_kernel,
        name="deal",
        grid=(count,),
        in_specs=[flat(units), one(units), flat(units), one(wide), one(wide), flat(wide)],
        out_specs=flat(units + wide),
        out_shape=jax.ShapeDtypeStruct((count, size, units + wide), jnp.bfloat16),
        compiler_params=pltpu.CompilerParams(vmem_limit_bytes=VMEM_LIMIT),
    )(*(cut(a) for a in (up, up_in, up_in2, down, down_in, down_in2)))


def swap(array, axis, distance):
    return lax.ppermute(array, axis, [(i, i ^ distance) for i in range(lax.axis_size(axis))])


def per_device(
    tokens,
    token_mask,
    masked_flags,
    doc_lengths,
    mask_embedding,
    ln1_gain,
    ln1_bias,
    w_query,
    query_bias,
    w_key,
    w_value,
    value_bias,
    w_out,
    out_bias,
    ln2_gain,
    ln2_bias,
    w_up,
    up_bias,
    w_down,
    down_bias,
    cotangent,
):
    feat = tokens.shape[1]
    n = lax.axis_size("tensor")
    dp_size = lax.axis_size("dp")
    hidden_units = w_up.shape[1]

    own = (w_out, w_up, w_down)
    dp_me = lax.axis_index("dp")
    odd = (dp_me % 2 + dp_me // 2) % 2 == 1
    far = swap(jnp.where(odd, w_down, w_up), "tensor", 2)
    out_far = swap(w_out, "tensor", 2)
    first_norm, query_pair, key_wide, head_rows, wT, vectors, marks = project(
        doc_lengths, tokens, token_mask, masked_flags,
        (mask_embedding, ln1_gain, ln1_bias, out_bias, ln2_gain, ln2_bias, down_bias, up_bias), (query_bias, value_bias),
        w_query.T, w_key.T, w_value.T,
    )
    context, log_totals = attend(doc_lengths, marks, key_wide, head_rows)
    (layer_output, back_hidden, back_context, wT_far, up_kk, up_ks, up_s, down_k, down_s, up_sums, sums) = middle(
        n, dp_size, tokens, context, cotangent, own, out_far, far, wT, marks, vectors
    )

    low_count = 2
    high_count = dp_size // low_count

    def back(head, do, held=()):
        *parts, bias, gw = attend_back(
            head, n, doc_lengths, marks, query_pair, key_wide, head_rows, context, log_totals, do, first_norm, held
        )
        return parts, bias, gw

    up_in = swap(up_s, "tensor", 2)
    down_in = swap(down_s, "dp", 1)
    parts, bias0, gw = back(0, back_context)
    up_s, down_s = fold(up_ks, up_in, down_k, down_in)
    do, up_s, down_s, *parts = lax.optimization_barrier((back_context, up_s, down_s, *parts))
    up_in2 = swap(up_s, "dp", 1)
    down_in2 = swap(down_s, "tensor", 2)
    parts, bias1, gw = back(1, do, (*parts, gw))
    dealt = deal(high_count, up_kk, up_in, up_in2, down_k, down_in, down_in2)
    do, dealt, *parts = lax.optimization_barrier((do, dealt, *parts))
    along_z = [[z * low_count + x for z in range(high_count)] for x in range(low_count)]
    pieces = lax.all_to_all(dealt, "dp", 0, 0, axis_index_groups=along_z)
    parts = [parts[0]] + [swap(parts[r], "tensor", r) for r in range(1, n)]
    last, bias2, gw2 = back(2, do)
    rows_of = feat // dp_size
    last, pieces = lax.optimization_barrier((last, pieces))
    gws = [g.reshape(dp_size, rows_of, g.shape[1]) for g in (gw, gw2)]
    input_grad, gw, gw2, early, late = finish(
        n, dp_size, parts, last, gws, (bias0, bias1, bias2), wT, wT_far,
        back_hidden, tokens, marks, vectors, up_sums, sums,
    )
    (gq, gk, gv, grad_up, grad_down, grad_out, mask_sum, gain1, bias1, q_bias, v_bias, gain2, bias2, o_bias, d_bias,
     u_bias) = pack(early, late, gw, gw2, pieces, hidden_units, n * hidden_units)
    return (layer_output, input_grad, mask_sum, gain1, bias1, gq, q_bias, gk, gv, v_bias, grad_out, o_bias, gain2, bias2,
            grad_up, u_bias, grad_down.T, d_bias)


def solution(mesh):
    in_specs = (
        P("dp", None),
        P("dp"),
        P("dp"),
        P("dp"),
        P(),
        P(),
        P(),
        P(None, "tensor"),
        P("tensor"),
        P(None, "tensor"),
        P(None, "tensor"),
        P("tensor"),
        P("tensor", None),
        P(),
        P(),
        P(),
        P(None, "tensor"),
        P("tensor"),
        P("tensor", None),
        P(),
        P(("dp", "tensor"), None),
    )
    out_specs = (
        P(("dp", "tensor"), None),
        P(("dp", "tensor"), None),
        P(),
        P(),
        P(),
        P("dp", "tensor"),
        P(),
        P("dp", "tensor"),
        P("dp", "tensor"),
        P(),
        P("tensor", "dp"),
        P(),
        P(),
        P(),
        P("dp", "tensor"),
        P(),
        P("tensor", "dp"),
        P(),
    )
    return jax.shard_map(
        per_device, mesh=mesh, in_specs=in_specs, out_specs=out_specs, check_vma=False
    )
```

```python
import functools, math
import jax, jax.numpy as jnp
from jax import lax
from jax.experimental import pallas as pl
from jax.experimental.pallas import tpu as pltpu
from jax.sharding import PartitionSpec as P

HD = 64
EPS = 1e-05
NEG = -2e30
LOG2E = 1.4426950408889634
VMEM_LIMIT = 56 * 2**20
ROWS = 512
KEYS = (1024, 512, 256)
START = 128


def dot(a, b, ca=1, cb=0):
    return lax.dot_general(a, b, (((ca,), (cb,)), ((), ())), preferred_element_type=jnp.float32)


def doc_bounds(len_ref, slots, axis):
    shape = (1, 128) if axis == 1 else (128, 1)
    place = lax.broadcasted_iota(jnp.int32, shape, axis)
    starts = jnp.zeros(shape, jnp.int32)
    ends = jnp.zeros(shape, jnp.int32)
    begin = jnp.int32(0)
    for slot in range(slots):
        end = begin + len_ref[slot]
        starts = jnp.where(place == slot, begin, starts)
        ends = jnp.where(place == slot, end, ends)
        begin = end
    return starts, ends


def column(row):
    wide = jnp.broadcast_to(row.astype(jnp.float32), (8, row.shape[1]))
    return jnp.transpose(wide)[:, :1]


def proj_kernel(len_ref, tok_ref, live_ref, flag_ref, *refs, heads, slots):
    flat, (bq_ref, bv_ref, wq_ref, wk_ref, wv_ref, fn_ref, qx_ref, kx_ref, tt_ref, wT_ref, vec_ref, mark_ref, wdup, bcol,
           qv_ref) = refs[:8], refs[8:]
    step = pl.program_id(0)
    width = heads * HD

    @pl.when(step == 0)
    def _():
        for i, ref in enumerate(flat):
            vec_ref[i:i + 1] = ref[...].astype(jnp.float32).reshape(1, -1)
        for i, ref in enumerate((bq_ref, bv_ref)):
            qv_ref[i:i + 1] = ref[...].astype(jnp.float32).reshape(1, -1)
        zero = jnp.zeros((1, HD), jnp.float32)
        rows = []
        for h in range(heads):
            piece = slice(h * HD, (h + 1) * HD)
            for n, w in enumerate((wq_ref, wk_ref, wv_ref)):
                begin = (3 * h + n) * HD
                wT_ref[begin:begin + HD, :] = w[piece, :]
                if n < 2:
                    for copy in range(2):
                        begin = ((2 * h + n) * 2 + copy) * HD
                        wdup[begin:begin + HD, :] = w[piece, :]
            rows += [qv_ref[0:1, piece], zero, qv_ref[1:2, piece]]
        bcol[...] = jnp.transpose(jnp.broadcast_to(jnp.concatenate(rows, axis=1), (8, 3 * width)))

    here = pl.ds(pl.multiple_of(step * ROWS, ROWS), ROWS)
    mark_ref[0:1] = live_ref[here].reshape(1, ROWS)
    mark_ref[1:2] = flag_ref[here].reshape(1, ROWS)
    live = column(mark_ref[0:1, :])
    flags = column(mark_ref[1:2, :])
    x = jnp.where(flags == 1.0, vec_ref[0:1], tok_ref[...].astype(jnp.float32))
    mean = jnp.mean(x, axis=1, keepdims=True)
    c = x - mean
    var = jnp.mean(c * c, axis=1, keepdims=True)
    fn = (c * lax.rsqrt(var + EPS) * vec_ref[1:2] + vec_ref[2:3]).astype(jnp.bfloat16)
    fn_ref[...] = fn
    starts, ends = doc_bounds(len_ref, slots, 1)
    row = step * ROWS + lax.broadcasted_iota(jnp.int32, (ROWS, 128), 0)
    lane = lax.broadcasted_iota(jnp.int32, (ROWS, 128), 1)
    member = (row >= starts) & (row < ends)
    pen = jnp.where(member & (live == 1.0), 0.0, NEG)
    pen = jnp.where(lane < 16, pen, jnp.where(lane < 19, 1.0, 0.0)).astype(jnp.bfloat16)
    both = dot(fn, wdup[...], 1, 1)
    for h in range(heads):
        bq = qv_ref[0:1, h * HD:(h + 1) * HD]
        q = (both[:, 2 * h * 128:(2 * h + 1) * 128] + jnp.concatenate([bq, bq], axis=1)).astype(jnp.bfloat16)
        q = q.astype(jnp.float32) * (LOG2E / math.sqrt(HD))
        high = q.astype(jnp.bfloat16).astype(jnp.float32)
        qx_ref[h] = jnp.where(lane < HD, high, q - high).astype(jnp.bfloat16)
        kx_ref[h, :, :128] = both[:, (2 * h + 1) * 128:(2 * h + 2) * 128].astype(jnp.bfloat16)
        kx_ref[h, :, 128:] = pen
    tt = (dot(wT_ref[...], fn, 1, 1) + bcol[:, :1]).astype(jnp.bfloat16)
    for h in range(heads):
        tt_ref[h] = tt[h * 3 * HD:(h + 1) * 3 * HD, :]


def project(lengths, tokens, live, flags, vectors, biases, wqT, wkT, wvT):
    rows, feat = tokens.shape
    width = wqT.shape[0]
    heads = width // HD
    whole = lambda s: pl.BlockSpec(s, lambda i, *_: (0,) * len(s))
    return pl.pallas_call(
        functools.partial(proj_kernel, heads=heads, slots=lengths.shape[0]),
        name="project",
        grid_spec=pltpu.PrefetchScalarGridSpec(
            num_scalar_prefetch=1,
            grid=(rows // ROWS,),
            in_specs=[
                pl.BlockSpec((ROWS, feat), lambda i, *_: (i, 0)),
                whole((rows,)), whole((rows,)), *[whole((feat,))] * 8, whole((width,)), whole((width,)),
                whole((width, feat)), whole((width, feat)), whole((width, feat)),
            ],
            out_specs=[
                pl.BlockSpec((ROWS, feat), lambda i, *_: (i, 0)),
                pl.BlockSpec((heads, ROWS, 128), lambda i, *_: (0, i, 0)),
                pl.BlockSpec((heads, ROWS, 256), lambda i, *_: (0, i, 0)),
                pl.BlockSpec((heads, 3 * HD, ROWS), lambda i, *_: (0, 0, i)),
                whole((3 * width, feat)), whole((8, feat)), pl.BlockSpec((2, ROWS), lambda i, *_: (0, i)),
            ],
            scratch_shapes=[
                pltpu.VMEM((heads * 256, feat), jnp.bfloat16),
                pltpu.VMEM((3 * width, 8), jnp.float32),
                pltpu.VMEM((8, width), jnp.float32),
            ],
        ),
        out_shape=[
            jax.ShapeDtypeStruct((rows, feat), jnp.bfloat16),
            jax.ShapeDtypeStruct((heads, rows, 128), jnp.bfloat16),
            jax.ShapeDtypeStruct((heads, rows, 256), jnp.bfloat16),
            jax.ShapeDtypeStruct((heads, 3 * HD, rows), jnp.bfloat16),
            jax.ShapeDtypeStruct((3 * width, feat), jnp.bfloat16),
            jax.ShapeDtypeStruct((8, feat), jnp.float32),
            jax.ShapeDtypeStruct((2, rows), jnp.int32),
        ],
        compiler_params=pltpu.CompilerParams(vmem_limit_bytes=VMEM_LIMIT),
    )(lengths, tokens, live, flags, *vectors, *biases, wqT, wkT, wvT)


def key_range(len_ref, slots, first, last, live_end):
    begin = jnp.int32(0)
    low = jnp.int32(0)
    high = jnp.int32(0)
    for slot in range(slots):
        end = begin + len_ref[slot]
        low = jnp.where((first >= begin) & (first < end), begin, low)
        high = jnp.where((last >= begin) & (last < end), end, high)
        begin = end
    return low, jnp.minimum(high, live_end)


def over_keys(sizes, low, high, rows, step, state):
    begin = low // START * START
    rest = jnp.maximum(high - begin, 0)
    counts = []
    for size in sizes[:-1]:
        counts.append(rest // size)
        rest = rest - counts[-1] * size
    counts.append((rest + sizes[-1] - 1) // sizes[-1])
    begin = jnp.minimum(begin, rows - sum(count * size for count, size in zip(counts, sizes)))
    for count, size in zip(counts, sizes):
        state = lax.fori_loop(
            0, count, lambda j, s, at=begin, size=size: step(pl.multiple_of(at + j * size, START), size, s), state)
        begin = begin + count * size
    return state


def last_live(live_row):
    place = lax.broadcasted_iota(jnp.int32, live_row.shape, 1)
    return jnp.max(jnp.where(live_row == 1, place + 1, 0))


def one_hot_rows(len_ref, slots, first, count):
    starts, ends = doc_bounds(len_ref, slots, 0)
    place = first + lax.broadcasted_iota(jnp.int32, (16, count), 1)
    return (place >= starts[:16]) & (place < ends[:16])


def fwd_kernel(len_ref, live_ref, kx_ref, tt_ref, ctx_ref, lse_ref, qx, *, heads, slots):
    rows = tt_ref.shape[2]
    blocks = rows // ROWS
    live_end = last_live(live_ref[0:1, :])

    @pl.loop(0, blocks)
    def _(i):
        first = pl.multiple_of(i * ROWS, ROWS)
        here = pl.ds(first, ROWS)
        low, high = key_range(len_ref, slots, first, first + ROWS - 1, live_end)
        hot = jnp.where(one_hot_rows(len_ref, slots, first, ROWS), 1.0, 0.0)
        dead = live_ref[0:1, here] != 1
        state = []
        for h in range(heads):
            q = tt_ref[h, :HD, here].astype(jnp.float32)
            k = tt_ref[h, HD:2 * HD, here].astype(jnp.float32)
            v = tt_ref[h, 2 * HD:, here].astype(jnp.float32)
            scaled = q * (LOG2E / math.sqrt(HD))
            top = scaled.astype(jnp.bfloat16)
            qx[h, :HD] = top
            qx[h, HD:128] = (scaled - top.astype(jnp.float32)).astype(jnp.bfloat16)
            qx[h, 128:] = jnp.concatenate([hot, jnp.zeros((112, ROWS), jnp.float32)], axis=0).astype(jnp.bfloat16)
            own = jnp.sum(scaled * k, axis=0, keepdims=True)
            state += [jnp.where(dead, own, -1e30), jnp.where(dead, 1.0, 0.0), jnp.where(dead, v, 0.0)]

        def step(begin, count, carried):
            keys = pl.ds(begin, count)
            out = []
            scores = [dot(kx_ref[h, keys, :], qx[h]) for h in range(heads)]
            tops = [jnp.maximum(carried[3 * h], jnp.max(scores[h], axis=0, keepdims=True)) for h in range(heads)]
            probs = [jnp.exp2(scores[h] - tops[h]).astype(jnp.bfloat16) for h in range(heads)]
            for h in range(heads):
                _, total, acc = carried[3 * h:3 * h + 3]
                fade = jnp.exp2(carried[3 * h] - tops[h])
                both = dot(jnp.concatenate([tt_ref[h, 2 * HD:, keys], jnp.ones((16, count), jnp.bfloat16)], axis=0), probs[h])
                out += [tops[h], total * fade + both[HD:HD + 1], acc * fade + both[:HD]]
            return tuple(out)

        state = over_keys(KEYS, low, high, rows, step, tuple(state))
        for h in range(heads):
            top, total, acc = state[3 * h:3 * h + 3]
            ctx_ref[h * HD:(h + 1) * HD, here] = (acc / total).astype(jnp.bfloat16)
            lse_ref[h, :, here] = top + jnp.log2(total)


def attend(lengths, marks, kx, tt):
    heads, _, rows = tt.shape
    vmem = pl.BlockSpec(memory_space=pltpu.VMEM)
    return pl.pallas_call(
        functools.partial(fwd_kernel, heads=heads, slots=lengths.shape[0]),
        name="attend",
        in_specs=[pl.BlockSpec(memory_space=pltpu.SMEM), vmem, vmem, vmem],
        out_specs=[vmem, vmem],
        out_shape=[jax.ShapeDtypeStruct((heads * HD, rows), jnp.bfloat16), jax.ShapeDtypeStruct((heads, 1, rows), jnp.float32)],
        scratch_shapes=[pltpu.VMEM((heads, 256, ROWS), jnp.bfloat16)],
        compiler_params=pltpu.CompilerParams(vmem_limit_bytes=VMEM_LIMIT),
    )(lengths, marks, kx, tt)


def split3(x):
    a = x.astype(jnp.bfloat16).astype(jnp.float32)
    b = (x - a).astype(jnp.bfloat16).astype(jnp.float32)
    return a, b, x - a - b


def bwd_kernel(len_ref, live_ref, qx_ref, kx_ref, tt_ref, ctx_ref, lse_ref, dot_ref, fn_ref, *refs, slots, n, folds, joined):
    joined_refs, refs = refs[:joined], refs[joined:]
    held, refs = refs[:4 * folds], refs[4 * folds:]
    part_refs, bias_ref, gw_ref, refs = refs[:n], refs[n], refs[n + 1], refs[n + 2:]
    fold_refs, (grad_ref, qfull, kT, dofull, vT, dk, dv, fn, sems, *fold_buf) = refs[:2 * folds], refs[2 * folds:]
    rows = tt_ref.shape[2]
    quarter = rows // n
    copies = [pltpu.make_async_copy(fn_ref, fn, sems.at[4])]
    for i in range(4 * folds):
        copies.append(pltpu.make_async_copy(held[i] if i < 2 else held[i].at[1], fold_buf[i // 2].at[i % 2], sems.at[i]))
    for copy in copies:
        copy.start()
    blocks = rows // ROWS
    live_end = last_live(live_ref[0:1, :])
    lane_zero = jnp.zeros
    qfull[:, 128:] = jnp.zeros((rows, 128), jnp.bfloat16)
    dofull[...] = jnp.zeros(dofull.shape, jnp.bfloat16)
    kT[:HD] = tt_ref[0, HD:2 * HD, :]
    kT[HD:128] = tt_ref[0, HD:2 * HD, :]
    starts, ends = doc_bounds(len_ref, slots, 0)
    vT[:HD] = tt_ref[0, 2 * HD:, :]
    ones = jnp.where(lax.broadcasted_iota(jnp.int32, (16, ROWS), 0) < 3, 1.0, 0.0)

    @pl.loop(0, blocks)
    def _(i):
        first = pl.multiple_of(i * ROWS, ROWS)
        here = pl.ds(first, ROWS)
        member = one_hot_rows(len_ref, slots, first, ROWS)
        alive = live_ref[0:1, here] == 1
        dead = jnp.logical_not(alive)
        pen = jnp.where(member & alive, 0.0, NEG)
        kT[128:, here] = jnp.concatenate([pen, ones, lane_zero((96, ROWS), jnp.float32)], axis=0).astype(jnp.bfloat16)
        vT[HD:, here] = jnp.concatenate([ones, lane_zero((48, ROWS), jnp.float32)], axis=0).astype(jnp.bfloat16)
        q = tt_ref[0, :HD, here].astype(jnp.float32)
        k = tt_ref[0, HD:2 * HD, here].astype(jnp.float32)
        v = tt_ref[0, 2 * HD:, here].astype(jnp.float32)
        do = dot_ref[:, here].astype(jnp.float32)
        delta = jnp.sum(do * ctx_ref[:, here].astype(jnp.float32), axis=0, keepdims=True)
        lse = lse_ref[0, :, here]
        parts = jnp.concatenate([-x for x in split3(lse)], axis=0)
        rest = jnp.concatenate([jnp.where(member, 1.0, 0.0), parts, lane_zero((13, ROWS), jnp.float32)], axis=0)
        qfull[here, :128] = qx_ref[0, here, :]
        qfull[here, 128:160] = jnp.transpose(rest.astype(jnp.bfloat16))
        parts = jnp.concatenate([-x for x in split3(delta)], axis=0)
        rest = jnp.concatenate([do, parts, lane_zero((13, ROWS), jnp.float32)], axis=0)
        dofull[here, :80] = jnp.transpose(rest.astype(jnp.bfloat16))
        p = jnp.where(dead, jnp.exp2(jnp.sum(q * k, axis=0, keepdims=True) * (LOG2E / math.sqrt(HD)) - lse), 0.0)
        ds = p * (jnp.sum(do * v, axis=0, keepdims=True) - delta)
        dk[:, here] = ds * q
        dv[:, here] = p * do
        grad_ref[:HD, here] = (ds * k).astype(jnp.bfloat16)

    @pl.loop(0, blocks)
    def _(i):
        first = pl.multiple_of(i * ROWS, ROWS)
        here = pl.ds(first, ROWS)
        low, high = key_range(len_ref, slots, first, first + ROWS - 1, live_end)

        def step(begin, count, dq):
            keys = [pl.ds(begin + u, min(count, 512)) for u in range(0, count, 512)]
            scores = [dot(qfull[here, :], kT[:, key]) for key in keys]
            backs = [dot(dofull[here, :], vT[:, key]) for key in keys]
            for key, score, back in zip(keys, scores, backs):
                p = jnp.exp2(score)
                ds = (p * back).astype(jnp.bfloat16)
                dv[:, key] += dot(dot_ref[:, here], p.astype(jnp.bfloat16))
                dk[:, key] += dot(tt_ref[0, :HD, here], ds)
                dq = dq + dot(ds, kx_ref[0, key, :])
            return dq

        dq = over_keys(KEYS[:2], low, high, rows, step, jnp.zeros((ROWS, 128), jnp.float32))
        dqT = jnp.transpose(dq)[:HD]
        grad_ref[:HD, here] = ((grad_ref[:HD, here].astype(jnp.float32) + dqT) * (1 / math.sqrt(HD))).astype(jnp.bfloat16)
    grad_ref[HD:2 * HD, :] = (dk[...] * (1 / math.sqrt(HD))).astype(jnp.bfloat16)
    grad_ref[2 * HD:, :] = dv[...].astype(jnp.bfloat16)
    me = lax.axis_index("tensor")
    for owner, part in zip((me, me + 1 - 2 * (me % 2), (me + 2) % n, n - 1 - me), part_refs):
        part[...] = grad_ref[:, pl.ds(pl.multiple_of(owner * quarter, 128), quarter)]
    bias_ref[...] = dot(jnp.ones((8, rows), jnp.bfloat16), grad_ref[...], 1, 1)
    for copy in copies:
        copy.wait()
    gw = jnp.transpose(dot(grad_ref[...], fn[...])).astype(jnp.bfloat16)
    if joined:
        first = joined_refs[0][...]
        if joined == 2:
            packed = joined_refs[1][...]
            wide = first.shape[1]
            packed = jnp.concatenate([packed[:, :wide], packed[:, wide:]], axis=0)
            first = (first.astype(jnp.float32) + packed.astype(jnp.float32)).astype(jnp.bfloat16)
        gw = jnp.concatenate([first, gw], axis=1)
    gw_ref[...] = gw
    for i in range(2 * folds):
        buf = fold_buf[i]
        fold_refs[i][...] = (buf[0].astype(jnp.float32) + buf[1].astype(jnp.float32)).astype(jnp.bfloat16)


def attend_back(head, n, lengths, marks, qx, kx, tt, ctx, lse, do, fn, join=(), held=()):
    rows = tt.shape[2]
    per = lambda *s: pl.BlockSpec((1,) + s, lambda i: (head, 0, 0))
    slab = pl.BlockSpec((HD, rows), lambda i: (head, 0))
    whole = lambda *s: pl.BlockSpec(s, lambda i: (0,) * len(s))
    any_ = pl.BlockSpec(memory_space=pl.ANY)
    vm = pltpu.VMEM
    quarter, feat = rows // n, fn.shape[1]
    folds = 1 if held else 0
    joined = len(join)
    wide = 3 * HD + (join[0].shape[1] if joined else 0)
    pairs = (held[0].shape, held[2].shape[1:]) if held else ()
    return pl.pallas_call(
        functools.partial(bwd_kernel, slots=lengths.shape[0], n=n, folds=folds, joined=joined),
        name="attend_back",
        grid=(1,),
        in_specs=[pl.BlockSpec(memory_space=pltpu.SMEM), whole(*marks.shape), per(rows, 128),
                  per(rows, 128), per(3 * HD, rows), slab, per(1, rows), slab, any_]
        + [whole(*j.shape) for j in join] + [any_] * (4 * folds),
        out_specs=[whole(3 * HD, quarter)] * n + [whole(8, 3 * HD), whole(feat, wide)]
        + [whole(*pair) for pair in pairs],
        out_shape=[jax.ShapeDtypeStruct((3 * HD, quarter), jnp.bfloat16)] * n
        + [jax.ShapeDtypeStruct((8, 3 * HD), jnp.float32), jax.ShapeDtypeStruct((feat, wide), jnp.bfloat16)]
        + [jax.ShapeDtypeStruct(pair, jnp.bfloat16) for pair in pairs],
        scratch_shapes=[vm((3 * HD, rows), jnp.bfloat16), vm((rows, 256), jnp.bfloat16), vm((256, rows), jnp.bfloat16), vm((rows, 128), jnp.bfloat16),
                        vm((128, rows), jnp.bfloat16), vm((HD, rows), jnp.float32), vm((HD, rows), jnp.float32), vm((rows, feat), jnp.bfloat16),
                        pltpu.SemaphoreType.DMA((5,))] + [vm((2,) + pair, jnp.bfloat16) for pair in pairs],
        cost_estimate=pl.CostEstimate(flops=15 * 10**9, bytes_accessed=6 * 2**20, transcendentals=0),
        compiler_params=pltpu.CompilerParams(vmem_limit_bytes=VMEM_LIMIT),
    )(lengths, marks, qx, kx, tt, ctx, lse, do, fn, *join, *held)


GELU_C = math.sqrt(2 / math.pi)
CHUNK = 256


def mid_kernel(tok_ref, ctx_ref, cot_ref, wo_own, wu_own, wd_own, wo_far, far_ref, vec_hbm, mark_ref, vec_ref,
               out_ref, bh_ref, do_ref, upk_ref, ups_ref, dnk_ref, dns_ref, early_ref, og_ref, ogs_ref,
               wo, ws, upb, cx, tok, cot, act, bp, hid, xhat, rstd, acc, bsec, n2, n2T, bf, bfT, atT, bcs, gr, gro, gso, ga, gb, upsum_ref, sums_ref, e_own, e_t, out_buf, bh_buf,
               loc_sem, w_send, w_recv, b_send, b_recv, c_send, c_recv, d_send, d_recv, d_loc, g_send, g_recv, o_sem, h_sem, es, er, f_sem,
               *, n, dp):
    quarter, feat = cot.shape
    width = ctx_ref.shape[0]
    chunks = quarter // CHUNK
    wu, wd = ws.at[0], ws.at[1]
    me = lax.axis_index("tensor")
    dp_me = lax.axis_index("dp")
    mesh_id = pl.DeviceIdType.MESH

    def other(r):
        return (me, me + 1 - 2 * (me % 2), (me + 2) % n, n - 1 - me)[r]

    def peer(r):
        return {"tensor": other(r)}

    def cols(owner, c):
        return pl.ds(pl.multiple_of(owner * quarter + c * CHUNK, CHUNK), CHUNK)

    def by_low(ref, columns, value):
        low_count, size = 2, value.shape[0] // dp
        for p in range(dp):
            q = p % low_count * (dp // low_count) + p // low_count
            ref[q * size:(q + 1) * size, columns] = value[p * size:(p + 1) * size]

    barrier = pltpu.get_barrier_semaphore()
    for r in range(1, n):
        pl.semaphore_signal(barrier, inc=1, device_id=peer(r), device_id_type=mesh_id)
    x_peer = {"dp": dp_me + 1 - 2 * (dp_me % 2)}
    z_peer = {"dp": dp_me + 2 - 4 * (dp_me // 2 % 2)}
    for device in (x_peer, z_peer):
        pl.semaphore_signal(barrier, inc=1, device_id=device, device_id_type=mesh_id)
    pl.semaphore_wait(barrier, n + 1)

    ctx_copies = {}
    for c in range(chunks):
        for r in (2, 3, 1):
            ctx_copies[c, r] = pltpu.make_async_remote_copy(
                src_ref=ctx_ref.at[:, cols(other(r), c)],
                dst_ref=cx.at[pl.ds(r * width, width), pl.ds(c * CHUNK, CHUNK)],
                send_sem=c_send.at[c * n + r], recv_sem=c_recv.at[c * n + r],
                device_id=peer(r), device_id_type=mesh_id)
    for r in (2, 3, 1):
        ctx_copies[0, r].start()
    own_ctx = pltpu.make_async_copy(
        ctx_ref.at[:, pl.ds(pl.multiple_of(me * quarter, CHUNK), quarter)], cx.at[pl.ds(0, width), :], loc_sem.at[0])
    rows_here = pl.ds(pl.multiple_of(me * quarter, CHUNK), quarter)
    tok_copy = pltpu.make_async_copy(tok_ref.at[rows_here, :], tok, loc_sem.at[1])
    cot_copy = pltpu.make_async_copy(cot_ref, cot, loc_sem.at[2])
    hidden_units = wd_own.shape[0]
    local, remote = {}, {}
    for i, (own, buf) in enumerate(((wo_own, wo), (wu_own, wu), (wd_own, wd))):
        size = own.shape[0]
        for r, src in ((0, own), (2, wo_far))[:2 if i == 0 else 1]:
            local[i, r] = pltpu.make_async_copy(src, buf.at[pl.ds(r * size, size), :], loc_sem.at[3 + 2 * i + r // 2])
            remote[i, r + 1] = pltpu.make_async_remote_copy(
                src_ref=src, dst_ref=buf.at[pl.ds((r + 1) * size, size), :], send_sem=w_send.at[2 * i + r // 2],
                recv_sem=w_recv.at[2 * i + r // 2], device_id=peer(1), device_id_type=mesh_id)
    have = (dp_me % 2 + dp_me // 2) % 2
    lack = 1 - have
    slot = lambda r, first, count: pl.ds(r * feat + first, count)
    held_here = pltpu.make_async_copy(far_ref, ws.at[have, slot(2, 0, feat), :], loc_sem.at[6])
    held_beside = pltpu.make_async_remote_copy(
        src_ref=far_ref, dst_ref=ws.at[have, slot(3, 0, feat), :], send_sem=w_send.at[3], recv_sem=w_recv.at[3],
        device_id=peer(1), device_id_type=mesh_id)
    part = feat // 2
    lacked = [
        pltpu.make_async_remote_copy(
            src_ref=far_ref.at[pl.ds(i * part, part), :], dst_ref=ws.at[have, slot(2, i * part, part), :],
            send_sem=h_sem.at[2 * i], recv_sem=h_sem.at[2 * i + 1], device_id=device, device_id_type=mesh_id)
        for i, device in enumerate((x_peer, z_peer))
    ]
    beside = pltpu.make_async_remote_copy(
        src_ref=ws.at[lack, slot(2, 0, feat), :], dst_ref=ws.at[lack, slot(3, 0, feat), :], send_sem=w_send.at[5],
        recv_sem=w_recv.at[5], device_id=peer(1), device_id_type=mesh_id)
    bias_copies = []
    for r in range(1, n):
        copy = pltpu.make_async_remote_copy(
            src_ref=vec_hbm, dst_ref=upb.at[r], send_sem=b_send.at[r], recv_sem=b_recv.at[r],
            device_id=peer(r), device_id_type=mesh_id)
        copy.start()
        bias_copies.append(copy)
    own_bias = pltpu.make_async_copy(vec_hbm, upb.at[0], loc_sem.at[9])
    own_ctx.start()
    tok_copy.start()
    cot_copy.start()
    own_bias.start()
    for copy in (*local.values(), *remote.values(), *lacked, held_here, held_beside):
        copy.start()

    live_col = column(mark_ref[0:1, rows_here])
    flag_col = column(mark_ref[1:2, rows_here])
    cot_copy.wait()
    masked = jnp.where(live_col == 1.0, cot[...], jnp.zeros((), jnp.bfloat16))
    bf[...] = masked
    by_low(bfT, slice(None), jnp.transpose(masked))
    sums_ref[...] = jnp.zeros(sums_ref.shape, jnp.float32)
    sums_ref[3:4] = jnp.sum(masked.astype(jnp.float32), axis=0, keepdims=True)
    tok_copy.wait()
    own_ctx.wait()
    own_bias.wait()
    for copy in bias_copies:
        copy.wait()
    gain = vec_ref[4:5]
    shift = vec_ref[5:6]
    upsum_ref[...] = jnp.zeros(upsum_ref.shape, jnp.float32)

    def feed(c, first, count):
        here = pl.ds(c * CHUNK, CHUNK)

        @pl.loop(first, first + count)
        def _(r):
            up = wu.at[pl.ds(pl.multiple_of(r * feat, feat), feat), :]
            down = wd.at[pl.ds(pl.multiple_of(r * hidden_units, hidden_units), hidden_units), :]
            pre = dot(n2[here, :], up[...]) + upb[r, 7:8, :]
            square = pre * pre
            t = jnp.tanh(pre * (square * (GELU_C * 0.044715) + GELU_C))
            half = 0.5 * t + 0.5
            a = pre * half
            slope = half + a * (1.0 - t) * (square * (3 * GELU_C * 0.044715) + GELU_C)
            low = a.astype(jnp.bfloat16)
            act[r, here, :] = low
            back = (dot(bf[here, :], down[...], 1, 1) * slope).astype(jnp.bfloat16)
            bp[r, here, :] = back
            upsum_ref[r, :1, :] += jnp.sum(back.astype(jnp.float32), axis=0, keepdims=True)
            acc[here, :] += dot(low, down[...])
            bsec[here, :] += dot(back, up[...], 1, 1)

    for c in range(chunks):
        for r in (2, 3, 1):
            ctx_copies[c, r].wait_send()
        if c + 1 < chunks:
            for r in (2, 3, 1):
                ctx_copies[c + 1, r].start()
        for r in (2, 3, 1):
            ctx_copies[c, r].wait_recv()
        if c == 0:
            for r in (0, 2):
                local[0, r].wait()
                remote[0, r + 1].wait()
        here = pl.ds(c * CHUNK, CHUNK)
        flag_c = flag_col[c * CHUNK:(c + 1) * CHUNK]
        x = jnp.where(flag_c == 1.0, vec_ref[0:1], tok[here, :].astype(jnp.float32))
        hidden = x + dot(cx[:, here], wo[...], 0, 0) + vec_ref[3:4]
        hid[here, :] = hidden
        sent = hidden.astype(jnp.bfloat16).astype(jnp.float32)
        centred = sent - jnp.mean(sent, axis=1, keepdims=True)
        scale = lax.rsqrt(jnp.mean(centred * centred, axis=1, keepdims=True) + EPS)
        normed = centred * scale
        xhat[here, :] = normed
        rstd[here, :] = jnp.broadcast_to(scale, (CHUNK, 128))
        second = (normed * gain + shift).astype(jnp.bfloat16)
        n2[here, :] = second
        n2T[:, here] = jnp.transpose(second)
        acc[here, :] = jnp.zeros((CHUNK, feat), jnp.float32)
        bsec[here, :] = jnp.zeros((CHUNK, feat), jnp.float32)
        if c == 0:
            for r, copies in ((0, local), (1, remote)):
                for i in (1, 2):
                    copies[i, r].wait()
                feed(c, r, 1)
        else:
            feed(c, 0, n // 2)
    for copy in (held_here, held_beside, *lacked):
        copy.wait()
    beside.start()
    grad_copies = {}

    def send_grad(i, k, src, dst):
        copy = pltpu.make_async_remote_copy(
            src_ref=src, dst_ref=dst, send_sem=g_send.at[3 * i + k], recv_sem=g_recv.at[3 * i + k],
            device_id=peer(1), device_id_type=mesh_id)
        copy.start()
        grad_copies[i, k] = copy

    def neighbour_grads(i, r):
        for k, (first, second) in enumerate(((n2T, bp), (bfT, act))):
            place = wd.at[pl.ds((2 * i + k) * feat, feat), :]
            place[...] = dot(first[...], second[r]).astype(jnp.bfloat16)
            send_grad(i, k, place, gr.at[2 * i + k])

    neighbour_grads(0, 1)
    beside.wait()

    bctx_copies = []
    for c in range(chunks):
        feed(c, n // 2, n // 2)
        here = pl.ds(c * CHUNK, CHUNK)
        live_c = live_col[c * CHUNK:(c + 1) * CHUNK]
        ffn = (acc[here, :] + vec_ref[6:7]).astype(jnp.bfloat16).astype(jnp.float32)
        out_buf[here, :] = (hid[here, :] + jnp.where(live_c == 1.0, ffn, 0.0)).astype(jnp.bfloat16)
        back = bsec[here, :]
        normed = xhat[here, :]
        sums_ref[0:1] += jnp.sum(back * normed, axis=0, keepdims=True)
        sums_ref[1:2] += jnp.sum(back, axis=0, keepdims=True)
        m = back * gain
        back_sent = rstd[here, :1] * (
            m - jnp.mean(m, axis=1, keepdims=True) - normed * jnp.mean(m * normed, axis=1, keepdims=True))
        back_hidden = cot[here, :].astype(jnp.float32) + back_sent.astype(jnp.bfloat16).astype(jnp.float32)
        bh_buf[here, :] = back_hidden
        for k, (src, dst) in enumerate(((out_buf, out_ref), (bh_buf, bh_ref))):
            copy = pltpu.make_async_copy(src.at[here, :], dst.at[here, :], f_sem.at[2 * c + k])
            copy.start()
            bctx_copies.append(copy)
        attn = back_hidden.astype(jnp.bfloat16)
        sums_ref[2:3] += jnp.sum(attn.astype(jnp.float32), axis=0, keepdims=True)
        atT[:, here] = jnp.transpose(attn)
        bcs[:, here] = dot(wo[...], attn, 1, 1).astype(jnp.bfloat16)
        for r in (2, 3, 1):
            copy = pltpu.make_async_remote_copy(
                src_ref=bcs.at[pl.ds(r * width, width), pl.ds(c * CHUNK, CHUNK)],
                dst_ref=do_ref.at[:, cols(me, c)],
                send_sem=d_send.at[c * n + r], recv_sem=d_recv.at[c * n + r],
                device_id=peer(r), device_id_type=mesh_id)
            copy.start()
            bctx_copies.append(copy)
        copy = pltpu.make_async_copy(
            bcs.at[pl.ds(0, width), pl.ds(c * CHUNK, CHUNK)], do_ref.at[:, cols(me, c)], d_loc.at[c])
        copy.start()
        bctx_copies.append(copy)

    rows = [sums_ref[i:i + 1] for i in range(4)]
    for i in range(n):
        row = jnp.zeros((1, hidden_units), jnp.float32)
        for r in range(n):
            row = jnp.where(other(r) == i, upsum_ref[r, :1, :], row)
        rows.append(row)
    e_own[...] = jnp.zeros(e_own.shape, jnp.float32)
    share = -(-len(rows) // n)
    for i, row in enumerate(rows):
        e_own[i // share, i % share:i % share + 1] = row
    e_copies = []
    for r in range(1, n):
        copy = pltpu.make_async_remote_copy(src_ref=e_own.at[other(r)], dst_ref=e_t.at[r], send_sem=es.at[r], recv_sem=er.at[r],
                                            device_id=peer(r), device_id_type=mesh_id)
        copy.start()
        e_copies.append(copy)

    out_grad = lambda r: dot(atT[...], cx[r * width:(r + 1) * width, :], 1, 1)
    gso[...] = jnp.concatenate([out_grad(1), out_grad(3)], axis=1).astype(jnp.bfloat16)
    beside_out = pltpu.make_async_remote_copy(
        src_ref=gso, dst_ref=gro, send_sem=g_send.at[2], recv_sem=g_recv.at[2], device_id=peer(1), device_id_type=mesh_id)
    beside_out.start()
    neighbour_grads(1, 3)
    half = feat // 2
    low = dp_me % 2
    mine = pl.ds(pl.multiple_of(low * half, half), half)
    other_half = pl.ds(pl.multiple_of((1 - low) * half, half), half)
    for i, r in ((0, 0), (1, 2)):
        for k in range(2):
            grad_copies[i, k].wait()
        if i == 1:
            near_grad = out_grad(0)
            far_grad = out_grad(2)
            beside_out.wait()
            far_grad = far_grad + gro[:, width:].astype(jnp.float32)
            ogs_ref[...] = jnp.concatenate([far_grad[:half], far_grad[half:]], axis=1).astype(jnp.bfloat16)
            og_ref[...] = (near_grad + gro[:, :width].astype(jnp.float32)).astype(jnp.bfloat16)
        for buf, first, second, slot in ((ga, n2T, bp, 2 * i), (gb, bfT, act, 2 * i + 1)):
            buf[i] = (dot(first[...], second[r]) + gr[slot].astype(jnp.float32)).astype(jnp.bfloat16)
        for k, (src, dst) in enumerate(((ga.at[i], (upk_ref, ups_ref)[i]), (gb.at[i, mine, :], dnk_ref.at[i]),
                                        (gb.at[i, other_half, :], dns_ref.at[i]))):
            copy = pltpu.make_async_copy(src, dst, o_sem.at[4 * i + k])
            copy.start()
            bctx_copies.append(copy)
    total = e_own[me]
    for r, copy in enumerate(e_copies):
        copy.wait()
        total = total + e_t[r + 1]
    early_ref[...] = total
    for copy in bctx_copies:
        copy.wait()


def middle(n, dp, tokens, ctx, cotangent, own, out_far, far, marks, vectors):
    quarter, feat = cotangent.shape
    width, rows = ctx.shape
    hidden_units = own[1].shape[1]
    vm, any_, vmem = pltpu.VMEM, pl.BlockSpec(memory_space=pl.ANY), pl.BlockSpec(memory_space=pltpu.VMEM)
    bf16, f32 = jnp.bfloat16, jnp.float32
    chunks = quarter // CHUNK
    sem = pltpu.SemaphoreType.DMA
    flops = 2 * quarter * feat * (6 * n * hidden_units + 3 * n * width)
    wide = hidden_units
    grads = [jax.ShapeDtypeStruct(s, bf16) for s in (
        (feat, wide), (feat, wide), (2, feat // 2, wide), (2, feat // 2, wide))]
    return pl.pallas_call(
        functools.partial(mid_kernel, n=n, dp=dp),
        name="middle",
        in_specs=[any_] * 9 + [vmem] * 2,
        out_specs=[any_] * 7 + [vmem] * 3,
        out_shape=[jax.ShapeDtypeStruct((quarter, feat), bf16), jax.ShapeDtypeStruct((quarter, feat), f32),
                   jax.ShapeDtypeStruct((width, rows), bf16)] + grads + [
                   jax.ShapeDtypeStruct((8, feat), f32), jax.ShapeDtypeStruct((feat, width), bf16),
                   jax.ShapeDtypeStruct((feat // 2, 2 * width), bf16)],
        scratch_shapes=[
            vm((n * width, feat), bf16), vm((2, n * feat, hidden_units), bf16),
            vm((n, 8, hidden_units), f32), vm((n * width, quarter), bf16), vm((quarter, feat), bf16), vm((quarter, feat), bf16),
            vm((n, quarter, hidden_units), bf16), vm((n, quarter, hidden_units), bf16),
            vm((quarter, feat), f32), vm((quarter, feat), f32), vm((quarter, 128), f32), vm((quarter, feat), f32),
            vm((quarter, feat), f32), vm((quarter, feat), bf16), vm((feat, quarter), bf16), vm((quarter, feat), bf16),
            vm((feat, quarter), bf16), vm((feat, quarter), bf16), vm((n * width, quarter), bf16),
            vm((4, feat, hidden_units), bf16), vm((feat, 2 * width), bf16), vm((feat, 2 * width), bf16),
            vm((2, feat, wide), bf16), vm((2, feat, wide), bf16),
            vm((n, 8, hidden_units), f32), vm((8, feat), f32), vm((n, 8, feat), f32), vm((n, 8, feat), f32),
            vm((quarter, feat), bf16), vm((quarter, feat), f32),
            sem((10,)), sem((6,)), sem((6,)), sem((n,)), sem((n,)), sem((chunks * n,)), sem((chunks * n,)),
            sem((chunks * n,)), sem((chunks * n,)), sem((chunks,)), sem((6,)), sem((6,)), sem((8,)), sem((4,)), sem((n,)), sem((n,)), sem((2 * chunks,)),
        ],
        cost_estimate=pl.CostEstimate(flops=flops, bytes_accessed=40 * 2**20, transcendentals=0),
        compiler_params=pltpu.CompilerParams(vmem_limit_bytes=60 * 2**20, collective_id=0, has_side_effects=True),
    )(tokens, ctx, cotangent, *own, out_far, far, vectors, marks, vectors)


def fin_kernel(early_blocks, last_blocks, gw_refs, b_refs, sum_refs, wT_own, wT_far, bh_ref, tok_ref, mark_ref, vec_ref, e_part,
               grad_ref, qkv_ref, up_ref, down_ref, early_ref, late_ref,
               wall, blk, bh, tok, acc, gw_mine, gw_x, gw_z, ups, up_send, up_in, parts, big, big_z, e_dp, l_own, l_t, l_dp,
               loc_sem, w_send, w_recv, a_send, a_recv, x_send, x_recv, p_send, p_recv, b_send, b_recv, u_sem, fs, fr, hs, hr, ls, lr, ms, mr, *, n, dp):
    quarter, feat = acc.shape
    heads = len(b_refs)
    part = last_blocks[0].shape[0]
    chunks = quarter // CHUNK
    me = lax.axis_index("tensor")
    dp_me = lax.axis_index("dp")
    mesh_id = pl.DeviceIdType.MESH

    def other(r):
        return (me, me + 1 - 2 * (me % 2), (me + 2) % n, n - 1 - me)[r]

    def peer(r):
        return {"tensor": other(r)}

    def dp_peer(d):
        return {"dp": (dp_me + d) % dp}

    barrier = pltpu.get_barrier_semaphore()
    for r in range(1, n):
        pl.semaphore_signal(barrier, inc=1, device_id=peer(r), device_id_type=mesh_id)
    for d in range(1, dp):
        pl.semaphore_signal(barrier, inc=1, device_id=dp_peer(d), device_id_type=mesh_id)
    pl.semaphore_wait(barrier, n + dp - 2)

    last = heads - 1
    arrivals = {}
    for c in range(chunks):
        here = pl.ds(c * CHUNK, CHUNK)
        for r in (2, 3, 1):
            copy = pltpu.make_async_remote_copy(
                src_ref=last_blocks[r].at[:, here], dst_ref=blk.at[pl.ds((last * n + r) * part, part), here],
                send_sem=a_send.at[c * n + r], recv_sem=a_recv.at[c * n + r], device_id=peer(r), device_id_type=mesh_id)
            arrivals[c, r] = copy

    def ask(c):
        for r in (2, 3, 1):
            arrivals[c, r].start()

    ask(0)
    e_dp[0] = e_part[...]
    f_copies = []
    for d in range(1, dp):
        copy = pltpu.make_async_remote_copy(src_ref=e_dp.at[0], dst_ref=e_dp.at[d], send_sem=fs.at[d], recv_sem=fr.at[d],
                                            device_id=dp_peer(d), device_id_type=mesh_id)
        copy.start()
        f_copies.append(copy)
    waits = []
    sem = iter(range(loc_sem.shape[0]))
    low_count = 2
    high_count = dp // low_count
    low, high = dp_me % low_count, dp_me // low_count
    x_peer = {"dp": dp_me + 1 - 2 * low}
    part_copies = []
    for i, ref in enumerate(sum_refs):
        copy = pltpu.make_async_copy(
            ref if len(ref.shape) != 3 or i == 0 else ref.at[0], ups if i == 0 else parts.at[i - 1], loc_sem.at[next(sem)])
        copy.start()
        part_copies.append(copy)
    x_copies = []
    for k, ref in enumerate(gw_refs):
        copy = pltpu.make_async_remote_copy(
            src_ref=ref.at[:, 1 - low], dst_ref=gw_x.at[k], send_sem=x_send.at[k], recv_sem=x_recv.at[k],
            device_id=x_peer, device_id_type=mesh_id)
        copy.start()
        x_copies.append(copy)
        copy = pltpu.make_async_copy(ref.at[:, low], gw_mine.at[k], loc_sem.at[next(sem)])
        copy.start()
        x_copies.append(copy)
    for h in range(heads):
        for r, src in ((0, wT_own), (2, wT_far)):
            rows = src.at[pl.ds(h * part, part), :]
            copy = pltpu.make_async_copy(rows, wall.at[pl.ds((h * n + r) * part, part), :], loc_sem.at[next(sem)])
            copy.start()
            waits.append(copy)
            copy = pltpu.make_async_remote_copy(
                src_ref=rows, dst_ref=wall.at[pl.ds((h * n + r + 1) * part, part), :], send_sem=w_send.at[2 * h + r // 2],
                recv_sem=w_recv.at[2 * h + r // 2], device_id=peer(1), device_id_type=mesh_id)
            copy.start()
            waits.append(copy)
    pieces = [(last_blocks[0], last, 0)]
    pieces += [(early_blocks[h * n + r], h, r) for r in range(n) for h in range(last)]
    for src, h, r in pieces:
        copy = pltpu.make_async_copy(src, blk.at[pl.ds((h * n + r) * part, part), :], loc_sem.at[next(sem)])
        copy.start()
        waits.append(copy)
    rows_here = pl.ds(pl.multiple_of(me * quarter, CHUNK), quarter)
    for src, dst in ((bh_ref, bh), (tok_ref.at[rows_here, :], tok)):
        copy = pltpu.make_async_copy(src, dst, loc_sem.at[next(sem)])
        copy.start()
        waits.append(copy)

    for copy in part_copies:
        copy.wait()
    size = parts.shape[1] // high_count
    total = sum(parts[i].astype(jnp.float32) for i in range(3)).astype(jnp.bfloat16)
    for z in range(high_count):
        big[z] = total[z * size:(z + 1) * size]
    b_copies = []
    for d in range(1, high_count):
        copy = pltpu.make_async_remote_copy(
            src_ref=big.at[(high + d) % high_count], dst_ref=big_z.at[d], send_sem=b_send.at[d], recv_sem=b_recv.at[d],
            device_id={"dp": (dp_me + d * low_count) % dp}, device_id_type=mesh_id)
        copy.start()
        b_copies.append(copy)
    total = sum(ups[z].astype(jnp.float32) for z in range(high_count)).astype(jnp.bfloat16)
    for x in range(low_count):
        up_send[x] = total[x * size:(x + 1) * size]
    up_copy = pltpu.make_async_remote_copy(
        src_ref=up_send.at[1 - low], dst_ref=up_in, send_sem=u_sem.at[0], recv_sem=u_sem.at[1], device_id=x_peer,
        device_id_type=mesh_id)
    up_copy.start()
    rows = []
    zero = lambda k: [jnp.zeros((1, k), jnp.float32)] if k else []
    for k in (0, 2):
        piece = jnp.concatenate([ref[:1, k * HD:(k + 1) * HD] for ref in b_refs], axis=1)
        size = piece.shape[1]
        total = jnp.zeros((1, feat), jnp.float32)
        for i in range(n):
            placed = jnp.concatenate(zero(i * size) + [piece] + zero((n - 1 - i) * size), axis=1)
            total = jnp.where(me == i, placed, total)
        rows.append(total)

    for copy in waits:
        copy.wait()
    first = last * n * part
    for c in range(chunks):
        here = pl.ds(c * CHUNK, CHUNK)
        acc[here, :] = dot(blk[:first, here], wall[:first], 0, 0)
        if c == 0 and chunks > 1:
            ask(1)
    for copy in x_copies:
        copy.wait()
    gw_mine[...] = (gw_mine[...].astype(jnp.float32) + gw_x[...].astype(jnp.float32)).astype(jnp.bfloat16)
    z_copies = []
    for d in range(1, high_count):
        copy = pltpu.make_async_remote_copy(
            src_ref=gw_mine.at[:, (high + d) % high_count], dst_ref=gw_z.at[d], send_sem=p_send.at[d], recv_sem=p_recv.at[d],
            device_id={"dp": (dp_me + d * low_count) % dp}, device_id_type=mesh_id)
        copy.start()
        z_copies.append(copy)

    flag_col = column(mark_ref[1:2, rows_here])
    emb = vec_ref[0:1]
    gain = vec_ref[1:2]
    mask_sum = jnp.zeros((1, feat), jnp.float32)
    gain_sum = jnp.zeros((1, feat), jnp.float32)
    bias_sum = jnp.zeros((1, feat), jnp.float32)
    for c in range(chunks):
        here = pl.ds(c * CHUNK, CHUNK)
        flag = flag_col[c * CHUNK:(c + 1) * CHUNK] == 1.0
        for r in (2, 3, 1):
            arrivals[c, r].wait()
        if c + 2 < chunks:
            ask(c + 2)
        back = acc[here, :] + dot(blk[first:, here], wall[first:], 0, 0)
        x = jnp.where(flag, emb, tok[here, :].astype(jnp.float32))
        centred = x - jnp.mean(x, axis=1, keepdims=True)
        scale = lax.rsqrt(jnp.mean(centred * centred, axis=1, keepdims=True) + EPS)
        normed = centred * scale
        gain_sum += jnp.sum(back * normed, axis=0, keepdims=True)
        bias_sum += jnp.sum(back, axis=0, keepdims=True)
        m = back * gain
        back_in = bh[here, :] + scale * (
            m - jnp.mean(m, axis=1, keepdims=True) - normed * jnp.mean(m * normed, axis=1, keepdims=True))
        grad_ref[here, :] = jnp.where(flag, 0.0, back_in)
        mask_sum += jnp.sum(jnp.where(flag, back_in, 0.0), axis=0, keepdims=True)

    l_own[...] = jnp.zeros(l_own.shape, jnp.float32)
    lanes = feat // 128
    for i, row in enumerate((mask_sum, gain_sum, bias_sum, *rows)):
        for j in range(lanes):
            l_own[i * lanes + j:i * lanes + j + 1] = row[:, j * 128:(j + 1) * 128]
    l_copies = []
    for r in range(1, n):
        copy = pltpu.make_async_remote_copy(src_ref=l_own, dst_ref=l_t.at[r], send_sem=ls.at[r], recv_sem=lr.at[r],
                                            device_id=peer(r), device_id_type=mesh_id)
        copy.start()
        l_copies.append(copy)
    total = e_dp[0]
    for d, copy in enumerate(f_copies):
        copy.wait()
        total = total + e_dp[d + 1]
    early_ref[me] = total
    h_copies = []
    for r in range(1, n):
        copy = pltpu.make_async_remote_copy(src_ref=early_ref.at[me], dst_ref=early_ref.at[me], send_sem=hs.at[r],
                                            recv_sem=hr.at[r], device_id=peer(r), device_id_type=mesh_id)
        copy.start()
        h_copies.append(copy)
    total = l_own[...]
    for r, copy in enumerate(l_copies):
        copy.wait()
        total = total + l_t[r + 1]
    l_dp[0] = total
    m_copies = []
    for d in range(1, dp):
        copy = pltpu.make_async_remote_copy(src_ref=l_dp.at[0], dst_ref=l_dp.at[d], send_sem=ms.at[d], recv_sem=mr.at[d],
                                            device_id=dp_peer(d), device_id_type=mesh_id)
        copy.start()
        m_copies.append(copy)
    up_copy.wait()
    up_ref[...] = up_send[low].astype(jnp.float32) + up_in[...].astype(jnp.float32)
    for copies, mine, arrived, out in ((b_copies, big[high], big_z, down_ref), (z_copies, gw_mine[:, high], gw_z, qkv_ref)):
        total = mine.astype(jnp.float32)
        for d, copy in enumerate(copies):
            copy.wait()
            total = total + arrived[d + 1].astype(jnp.float32)
        out[...] = total
    for copy in h_copies:
        copy.wait()
    total = l_dp[0]
    for d, copy in enumerate(m_copies):
        copy.wait()
        total = total + l_dp[d + 1]
    late_ref[...] = total


def finish(n, dp, early_blocks, last_blocks, gws, biases, sums, wT_own, wT_far, back_hidden, tokens, marks, vectors, early):
    quarter, feat = back_hidden.shape
    part = last_blocks[0].shape[0]
    heads = len(biases)
    chunks = quarter // CHUNK
    vm, any_, vmem = pltpu.VMEM, pl.BlockSpec(memory_space=pl.ANY), pl.BlockSpec(memory_space=pltpu.VMEM)
    bf16, f32 = jnp.bfloat16, jnp.float32
    sem = pltpu.SemaphoreType.DMA
    late_rows = -(-5 * (feat // 128) // 8) * 8
    share = early.shape[0]
    count, size = dp // 2, feat // dp
    half, units = sums[3].shape
    kinds = len(gws)
    wide = gws[0].shape[1]
    gws = [g.reshape(count, 2, size, wide) for g in gws]
    early_blocks = [b for blocks in early_blocks for b in blocks]

    def body(*refs):
        cut = [len(early_blocks), n, kinds, heads, len(sums)]
        groups = []
        for width in cut:
            groups.append(refs[:width])
            refs = refs[width:]
        fin_kernel(*groups, *refs, n=n, dp=dp)

    return pl.pallas_call(
        body,
        name="finish",
        in_specs=[any_] * (len(early_blocks) + n + kinds) + [vmem] * heads + [any_] * (len(sums) + 4) + [vmem] * 3,
        out_specs=[vmem] * 6,
        out_shape=[jax.ShapeDtypeStruct((quarter, feat), f32), jax.ShapeDtypeStruct((kinds, size, wide), f32),
                   jax.ShapeDtypeStruct((size, units), f32), jax.ShapeDtypeStruct((size, units), f32), jax.ShapeDtypeStruct((n, share, feat), f32),
                   jax.ShapeDtypeStruct((late_rows, 128), f32)],
        scratch_shapes=[
            vm((heads * n * part, feat), bf16), vm((heads * n * part, quarter), bf16),
            vm((quarter, feat), f32), vm((quarter, feat), bf16), vm((quarter, feat), f32),
            vm((kinds, count, size, wide), bf16), vm((kinds, count, size, wide), bf16), vm((count, kinds, size, wide), bf16),
            vm((count, 2 * size, units), bf16), vm((2, size, units), bf16), vm((size, units), bf16),
            vm((3, half, units), bf16), vm((count, size, units), bf16), vm((count, size, units), bf16),
            vm((dp, share, feat), f32),
            vm((late_rows, 128), f32), vm((n, late_rows, 128), f32), vm((dp, late_rows, 128), f32),
            sem((dp + 40,)), sem((2 * heads,)), sem((2 * heads,)), sem((chunks * n,)), sem((chunks * n,)),
            sem((dp,)), sem((dp,)), sem((dp,)), sem((dp,)), sem((dp,)), sem((dp,)), sem((2,)), sem((dp,)), sem((dp,)), sem((n,)), sem((n,)),
            sem((n,)), sem((n,)), sem((dp,)), sem((dp,)),
        ],
        cost_estimate=pl.CostEstimate(flops=8 * 10**9, bytes_accessed=25 * 2**20, transcendentals=0),
        compiler_params=pltpu.CompilerParams(vmem_limit_bytes=60 * 2**20, collective_id=1, has_side_effects=True),
    )(*early_blocks, *last_blocks, *gws, *biases, *sums, wT_own, wT_far, back_hidden, tokens, marks, vectors, early)


def pack_kernel(early_ref, late_ref, qkv_ref, up_ref, down_ref, q_out, k_out, v_out, up_out, down_out, out_out, *vec_refs):
    heads = q_out.shape[1] // HD
    part = 3 * HD
    places = [(0, 0), (0, part), (1, part)]
    for n, out in enumerate((q_out, k_out, v_out)):
        for h in range(heads):
            out[:, h * HD:(h + 1) * HD] = qkv_ref[places[h][0], :, places[h][1] + n * HD:places[h][1] + (n + 1) * HD]
    units = up_out.shape[1]
    up_out[...] = up_ref[...]
    down_out[...] = down_ref[...]
    out_out[...] = jnp.transpose(qkv_ref[1, :, :part])
    feat = early_ref.shape[2]
    lanes = feat // 128
    for i in range(5):
        for j in range(lanes):
            vec_refs[i][j * 128:(j + 1) * 128] = late_ref[i * lanes + j, :]
    n = vec_refs[9].shape[0] // units
    share = -(-(4 + n) // n)
    row = lambda i: early_ref[i // share, i % share, :]
    for i in range(4):
        vec_refs[5 + i][...] = row(i)
    for i in range(n):
        vec_refs[9][i * units:(i + 1) * units] = row(4 + i)


def pack(early, late, qkv, up, down, up_units):
    kinds, rows, width = qkv.shape
    width //= 2
    feat = early.shape[2]
    vmem = pl.BlockSpec(memory_space=pltpu.VMEM)
    shape = lambda *s: jax.ShapeDtypeStruct(s, jnp.float32)
    return pl.pallas_call(
        pack_kernel,
        name="pack",
        in_specs=[vmem] * 5,
        out_specs=[vmem] * 16,
        out_shape=[shape(rows, width)] * 3 + [shape(*up.shape), shape(*down.shape), shape(width, rows)]
        + [shape(feat)] * 9 + [shape(up_units)],
        compiler_params=pltpu.CompilerParams(vmem_limit_bytes=VMEM_LIMIT),
    )(early, late, qkv, up, down)


def swap(array, axis, distance):
    return lax.ppermute(array, axis, [(i, i ^ distance) for i in range(lax.axis_size(axis))])


def per_device(
    tokens,
    token_mask,
    masked_flags,
    doc_lengths,
    mask_embedding,
    ln1_gain,
    ln1_bias,
    w_query,
    query_bias,
    w_key,
    w_value,
    value_bias,
    w_out,
    out_bias,
    ln2_gain,
    ln2_bias,
    w_up,
    up_bias,
    w_down,
    down_bias,
    cotangent,
):
    n = lax.axis_size("tensor")
    dp_size = lax.axis_size("dp")
    hidden_units = w_up.shape[1]

    own = (w_out, w_up, w_down)
    dp_me = lax.axis_index("dp")
    odd = (dp_me % 2 + dp_me // 2) % 2 == 1
    far = swap(jnp.where(odd, w_down, w_up), "tensor", 2)
    out_far = swap(w_out, "tensor", 2)
    first_norm, query_pair, key_wide, head_rows, wT, vectors, marks = project(
        doc_lengths, tokens, token_mask, masked_flags,
        (mask_embedding, ln1_gain, ln1_bias, out_bias, ln2_gain, ln2_bias, down_bias, up_bias), (query_bias, value_bias),
        w_query.T, w_key.T, w_value.T,
    )
    wT_far = swap(wT, "tensor", 2)
    context, log_totals = attend(doc_lengths, marks, key_wide, head_rows)
    context, wT_far = lax.optimization_barrier((context, wT_far))
    layer_output, back_hidden, back_context, up_k, up_s, down_k, down_s, early, out_grad, out_send = middle(
        n, dp_size, tokens, context, cotangent, own, out_far, far, marks, vectors
    )

    low_count = 2
    high_count = dp_size // low_count
    along_z = [[z * low_count + x for z in range(high_count)] for x in range(low_count)]

    def back(head, do, join=(), held=()):
        outs = attend_back(
            head, n, doc_lengths, marks, query_pair, key_wide, head_rows, context, log_totals, do, first_norm, join, held
        )
        return outs[:n], *outs[n:]

    def exchange(parts):
        return [parts[0]] + [swap(parts[r], "tensor", r) for r in range(1, n)]

    up_in = swap(up_s, "tensor", 2)
    down_in = swap(down_s, "dp", 1)
    parts, bias0, gw = back(0, back_context)
    parts, out_send = lax.optimization_barrier((parts, out_send))
    out_in = swap(out_send, "tensor", 2)
    blocks0 = exchange(parts)
    parts, bias1, gw01, up, down_s = back(1, back_context, (gw,), (up_k, up_in, down_k, down_in))
    do, blocks0, out_in, parts, up, down_s = lax.optimization_barrier((back_context, blocks0, out_in, parts, up, down_s))
    up = lax.all_to_all(up.reshape(high_count, -1, hidden_units), "dp", 0, 0, axis_index_groups=along_z)
    down_in2 = swap(down_s, "tensor", 2)
    blocks1 = exchange(parts)
    last, bias2, gw2 = back(2, do, (out_grad, out_in))
    input_grad, qkv, up, down, early, late = finish(
        n, dp_size, (blocks0, blocks1), last, (gw01, gw2), (bias0, bias1, bias2),
        (up, down_k, down_in, down_in2), wT, wT_far, back_hidden, tokens, marks, vectors, early,
    )
    (gq, gk, gv, grad_up, grad_down, grad_out, mask_sum, gain1, bias1, q_bias, v_bias, gain2, bias2, o_bias, d_bias,
     u_bias) = pack(early, late, qkv, up, down, n * hidden_units)
    return (layer_output, input_grad, mask_sum, gain1, bias1, gq, q_bias, gk, gv, v_bias, grad_out, o_bias, gain2, bias2,
            grad_up, u_bias, grad_down.T, d_bias)


def solution(mesh):
    in_specs = (
        P("dp", None),
        P("dp"),
        P("dp"),
        P("dp"),
        P(),
        P(),
        P(),
        P(None, "tensor"),
        P("tensor"),
        P(None, "tensor"),
        P(None, "tensor"),
        P("tensor"),
        P("tensor", None),
        P(),
        P(),
        P(),
        P(None, "tensor"),
        P("tensor"),
        P("tensor", None),
        P(),
        P(("dp", "tensor"), None),
    )
    out_specs = (
        P(("dp", "tensor"), None),
        P(("dp", "tensor"), None),
        P(),
        P(),
        P(),
        P("dp", "tensor"),
        P(),
        P("dp", "tensor"),
        P("dp", "tensor"),
        P(),
        P("tensor", "dp"),
        P(),
        P(),
        P(),
        P("dp", "tensor"),
        P(),
        P("tensor", "dp"),
        P(),
    )
    return jax.shard_map(
        per_device, mesh=mesh, in_specs=in_specs, out_specs=out_specs, check_vma=False
    )
```

```python
import functools, math
import jax, jax.numpy as jnp
from jax import lax
from jax.experimental import pallas as pl
from jax.experimental.pallas import tpu as pltpu
from jax.sharding import PartitionSpec as P

HD = 64
EPS = 1e-05
NEG = -2e30
LOG2E = 1.4426950408889634
VMEM_LIMIT = 56 * 2**20
ROWS = 512
PROJ_ROWS = 768
KEYS = (1024, 512, 256)
START = 128


def dot(a, b, ca=1, cb=0):
    return lax.dot_general(a, b, (((ca,), (cb,)), ((), ())), preferred_element_type=jnp.float32)


def doc_bounds(len_ref, slots, axis):
    shape = (1, 128) if axis == 1 else (128, 1)
    place = lax.broadcasted_iota(jnp.int32, shape, axis)
    starts = jnp.zeros(shape, jnp.int32)
    ends = jnp.zeros(shape, jnp.int32)
    begin = jnp.int32(0)
    for slot in range(slots):
        end = begin + len_ref[slot]
        starts = jnp.where(place == slot, begin, starts)
        ends = jnp.where(place == slot, end, ends)
        begin = end
    return starts, ends


def column(row):
    wide = jnp.broadcast_to(row.astype(jnp.float32), (8, row.shape[1]))
    return jnp.transpose(wide)[:, :1]


def proj_kernel(len_ref, tok_ref, live_ref, flag_ref, *refs, heads, slots):
    flat, (bq_ref, bv_ref, wq_ref, wk_ref, wv_ref, fn_ref, qx_ref, kx_ref, tt_ref, wT_ref, vec_ref, mark_ref, wdup, bcol,
           qv_ref) = refs[:8], refs[8:]
    step = pl.program_id(0)
    width = heads * HD

    @pl.when(step == 0)
    def _():
        for i, ref in enumerate(flat):
            vec_ref[i:i + 1] = ref[...].astype(jnp.float32).reshape(1, -1)
        for i, ref in enumerate((bq_ref, bv_ref)):
            qv_ref[i:i + 1] = ref[...].astype(jnp.float32).reshape(1, -1)
        zero = jnp.zeros((1, HD), jnp.float32)
        rows = []
        for h in range(heads):
            piece = slice(h * HD, (h + 1) * HD)
            for n, w in enumerate((wq_ref, wk_ref, wv_ref)):
                begin = (3 * h + n) * HD
                wT_ref[begin:begin + HD, :] = w[piece, :]
                if n < 2:
                    for copy in range(2):
                        begin = ((2 * h + n) * 2 + copy) * HD
                        wdup[begin:begin + HD, :] = w[piece, :]
            rows += [qv_ref[0:1, piece], zero, qv_ref[1:2, piece]]
        bcol[...] = jnp.transpose(jnp.broadcast_to(jnp.concatenate(rows, axis=1), (8, 3 * width)))

    here = pl.ds(pl.multiple_of(step * PROJ_ROWS, PROJ_ROWS), PROJ_ROWS)
    mark_ref[0:1] = live_ref[here].reshape(1, PROJ_ROWS)
    mark_ref[1:2] = flag_ref[here].reshape(1, PROJ_ROWS)
    live = column(mark_ref[0:1, :])
    flags = column(mark_ref[1:2, :])
    x = jnp.where(flags == 1.0, vec_ref[0:1], tok_ref[...].astype(jnp.float32))
    mean = jnp.mean(x, axis=1, keepdims=True)
    c = x - mean
    var = jnp.mean(c * c, axis=1, keepdims=True)
    fn = (c * lax.rsqrt(var + EPS) * vec_ref[1:2] + vec_ref[2:3]).astype(jnp.bfloat16)
    fn_ref[...] = fn
    starts, ends = doc_bounds(len_ref, slots, 1)
    row = step * PROJ_ROWS + lax.broadcasted_iota(jnp.int32, (PROJ_ROWS, 128), 0)
    lane = lax.broadcasted_iota(jnp.int32, (PROJ_ROWS, 128), 1)
    member = (row >= starts) & (row < ends)
    pen = jnp.where(member & (live == 1.0), 0.0, NEG)
    pen = jnp.where(lane < 16, pen, jnp.where(lane < 19, 1.0, 0.0)).astype(jnp.bfloat16)
    both = dot(fn, wdup[...], 1, 1)
    for h in range(heads):
        bq = qv_ref[0:1, h * HD:(h + 1) * HD]
        q = (both[:, 2 * h * 128:(2 * h + 1) * 128] + jnp.concatenate([bq, bq], axis=1)).astype(jnp.bfloat16)
        q = q.astype(jnp.float32) * (LOG2E / math.sqrt(HD))
        high = q.astype(jnp.bfloat16).astype(jnp.float32)
        qx_ref[h] = jnp.where(lane < HD, high, q - high).astype(jnp.bfloat16)
        kx_ref[h, :, :128] = both[:, (2 * h + 1) * 128:(2 * h + 2) * 128].astype(jnp.bfloat16)
        kx_ref[h, :, 128:] = pen
    tt = (dot(wT_ref[...], fn, 1, 1) + bcol[:, :1]).astype(jnp.bfloat16)
    for h in range(heads):
        tt_ref[h] = tt[h * 3 * HD:(h + 1) * 3 * HD, :]


def project(lengths, tokens, live, flags, vectors, biases, wqT, wkT, wvT):
    rows, feat = tokens.shape
    width = wqT.shape[0]
    heads = width // HD
    whole = lambda s: pl.BlockSpec(s, lambda i, *_: (0,) * len(s))
    return pl.pallas_call(
        functools.partial(proj_kernel, heads=heads, slots=lengths.shape[0]),
        name="project",
        grid_spec=pltpu.PrefetchScalarGridSpec(
            num_scalar_prefetch=1,
            grid=(rows // PROJ_ROWS,),
            in_specs=[
                pl.BlockSpec((PROJ_ROWS, feat), lambda i, *_: (i, 0)),
                whole((rows,)), whole((rows,)), *[whole((feat,))] * 8, whole((width,)), whole((width,)),
                whole((width, feat)), whole((width, feat)), whole((width, feat)),
            ],
            out_specs=[
                pl.BlockSpec((PROJ_ROWS, feat), lambda i, *_: (i, 0)),
                pl.BlockSpec((heads, PROJ_ROWS, 128), lambda i, *_: (0, i, 0)),
                pl.BlockSpec((heads, PROJ_ROWS, 256), lambda i, *_: (0, i, 0)),
                pl.BlockSpec((heads, 3 * HD, PROJ_ROWS), lambda i, *_: (0, 0, i)),
                whole((3 * width, feat)), whole((8, feat)), pl.BlockSpec((2, PROJ_ROWS), lambda i, *_: (0, i)),
            ],
            scratch_shapes=[
                pltpu.VMEM((heads * 256, feat), jnp.bfloat16),
                pltpu.VMEM((3 * width, 8), jnp.float32),
                pltpu.VMEM((8, width), jnp.float32),
            ],
        ),
        out_shape=[
            jax.ShapeDtypeStruct((rows, feat), jnp.bfloat16),
            jax.ShapeDtypeStruct((heads, rows, 128), jnp.bfloat16),
            jax.ShapeDtypeStruct((heads, rows, 256), jnp.bfloat16),
            jax.ShapeDtypeStruct((heads, 3 * HD, rows), jnp.bfloat16),
            jax.ShapeDtypeStruct((3 * width, feat), jnp.bfloat16),
            jax.ShapeDtypeStruct((8, feat), jnp.float32),
            jax.ShapeDtypeStruct((2, rows), jnp.int32),
        ],
        compiler_params=pltpu.CompilerParams(vmem_limit_bytes=VMEM_LIMIT),
    )(lengths, tokens, live, flags, *vectors, *biases, wqT, wkT, wvT)


def key_range(len_ref, slots, first, last, live_end):
    begin = jnp.int32(0)
    low = jnp.int32(0)
    high = jnp.int32(0)
    for slot in range(slots):
        end = begin + len_ref[slot]
        low = jnp.where((first >= begin) & (first < end), begin, low)
        high = jnp.where((last >= begin) & (last < end), end, high)
        begin = end
    return low, jnp.minimum(high, live_end)


def over_keys(sizes, low, high, rows, step, state):
    begin = low // START * START
    rest = jnp.maximum(high - begin, 0)
    counts = []
    for size in sizes[:-1]:
        counts.append(rest // size)
        rest = rest - counts[-1] * size
    counts.append((rest + sizes[-1] - 1) // sizes[-1])
    begin = jnp.minimum(begin, rows - sum(count * size for count, size in zip(counts, sizes)))
    for count, size in zip(counts, sizes):
        state = lax.fori_loop(
            0, count, lambda j, s, at=begin, size=size: step(pl.multiple_of(at + j * size, START), size, s), state)
        begin = begin + count * size
    return state


def last_live(live_row):
    place = lax.broadcasted_iota(jnp.int32, live_row.shape, 1)
    return jnp.max(jnp.where(live_row == 1, place + 1, 0))


def one_hot_rows(len_ref, slots, first, count):
    starts, ends = doc_bounds(len_ref, slots, 0)
    place = first + lax.broadcasted_iota(jnp.int32, (16, count), 1)
    return (place >= starts[:16]) & (place < ends[:16])


def fwd_kernel(len_ref, live_ref, kx_ref, tt_ref, ctx_ref, lse_ref, qx, *, heads, slots):
    rows = tt_ref.shape[2]
    blocks = rows // ROWS
    live_end = last_live(live_ref[0:1, :])

    @pl.loop(0, blocks)
    def _(i):
        first = pl.multiple_of(i * ROWS, ROWS)
        here = pl.ds(first, ROWS)
        low, high = key_range(len_ref, slots, first, first + ROWS - 1, live_end)
        hot = jnp.where(one_hot_rows(len_ref, slots, first, ROWS), 1.0, 0.0)
        dead = live_ref[0:1, here] != 1
        state = []
        for h in range(heads):
            q = tt_ref[h, :HD, here].astype(jnp.float32)
            k = tt_ref[h, HD:2 * HD, here].astype(jnp.float32)
            v = tt_ref[h, 2 * HD:, here].astype(jnp.float32)
            scaled = q * (LOG2E / math.sqrt(HD))
            top = scaled.astype(jnp.bfloat16)
            qx[h, :HD] = top
            qx[h, HD:128] = (scaled - top.astype(jnp.float32)).astype(jnp.bfloat16)
            qx[h, 128:] = jnp.concatenate([hot, jnp.zeros((112, ROWS), jnp.float32)], axis=0).astype(jnp.bfloat16)
            own = jnp.sum(scaled * k, axis=0, keepdims=True)
            state += [jnp.where(dead, own, -1e30), jnp.where(dead, 1.0, 0.0), jnp.where(dead, v, 0.0)]

        def step(begin, count, carried):
            keys = pl.ds(begin, count)
            out = []
            scores = [dot(kx_ref[h, keys, :], qx[h]) for h in range(heads)]
            tops = [jnp.maximum(carried[3 * h], jnp.max(scores[h], axis=0, keepdims=True)) for h in range(heads)]
            probs = [jnp.exp2(scores[h] - tops[h]).astype(jnp.bfloat16) for h in range(heads)]
            for h in range(heads):
                _, total, acc = carried[3 * h:3 * h + 3]
                fade = jnp.exp2(carried[3 * h] - tops[h])
                both = dot(jnp.concatenate([tt_ref[h, 2 * HD:, keys], jnp.ones((16, count), jnp.bfloat16)], axis=0), probs[h])
                out += [tops[h], total * fade + both[HD:HD + 1], acc * fade + both[:HD]]
            return tuple(out)

        state = over_keys(KEYS, low, high, rows, step, tuple(state))
        for h in range(heads):
            top, total, acc = state[3 * h:3 * h + 3]
            ctx_ref[h * HD:(h + 1) * HD, here] = (acc / total).astype(jnp.bfloat16)
            lse_ref[h, :, here] = top + jnp.log2(total)


def attend(lengths, marks, kx, tt):
    heads, _, rows = tt.shape
    vmem = pl.BlockSpec(memory_space=pltpu.VMEM)
    return pl.pallas_call(
        functools.partial(fwd_kernel, heads=heads, slots=lengths.shape[0]),
        name="attend",
        in_specs=[pl.BlockSpec(memory_space=pltpu.SMEM), vmem, vmem, vmem],
        out_specs=[vmem, vmem],
        out_shape=[jax.ShapeDtypeStruct((heads * HD, rows), jnp.bfloat16), jax.ShapeDtypeStruct((heads, 1, rows), jnp.float32)],
        scratch_shapes=[pltpu.VMEM((heads, 256, ROWS), jnp.bfloat16)],
        compiler_params=pltpu.CompilerParams(vmem_limit_bytes=VMEM_LIMIT),
    )(lengths, marks, kx, tt)


def split3(x):
    a = x.astype(jnp.bfloat16).astype(jnp.float32)
    b = (x - a).astype(jnp.bfloat16).astype(jnp.float32)
    return a, b, x - a - b


def bwd_kernel(len_ref, live_ref, qx_ref, kx_ref, tt_ref, ctx_ref, lse_ref, dot_ref, fn_ref, *refs, slots, n, folds, joined):
    joined_refs, refs = refs[:joined], refs[joined:]
    held, refs = refs[:4 * folds], refs[4 * folds:]
    part_refs, bias_ref, gw_ref, refs = refs[:n], refs[n], refs[n + 1], refs[n + 2:]
    fold_refs, (grad_ref, qfull, kT, dofull, vT, dk, dv, fn, sems, *fold_buf) = refs[:2 * folds], refs[2 * folds:]
    rows = tt_ref.shape[2]
    quarter = rows // n
    copies = [pltpu.make_async_copy(fn_ref, fn, sems.at[4])]
    for i in range(4 * folds):
        copies.append(pltpu.make_async_copy(held[i] if i < 2 else held[i].at[1], fold_buf[i // 2].at[i % 2], sems.at[i]))
    for copy in copies:
        copy.start()
    blocks = rows // ROWS
    live_end = last_live(live_ref[0:1, :])
    lane_zero = jnp.zeros
    qfull[:, 128:] = jnp.zeros((rows, 128), jnp.bfloat16)
    dofull[...] = jnp.zeros(dofull.shape, jnp.bfloat16)
    kT[:HD] = tt_ref[0, HD:2 * HD, :]
    kT[HD:128] = tt_ref[0, HD:2 * HD, :]
    starts, ends = doc_bounds(len_ref, slots, 0)
    vT[:HD] = tt_ref[0, 2 * HD:, :]
    ones = jnp.where(lax.broadcasted_iota(jnp.int32, (16, ROWS), 0) < 3, 1.0, 0.0)

    @pl.loop(0, blocks)
    def _(i):
        first = pl.multiple_of(i * ROWS, ROWS)
        here = pl.ds(first, ROWS)
        member = one_hot_rows(len_ref, slots, first, ROWS)
        alive = live_ref[0:1, here] == 1
        dead = jnp.logical_not(alive)
        pen = jnp.where(member & alive, 0.0, NEG)
        kT[128:, here] = jnp.concatenate([pen, ones, lane_zero((96, ROWS), jnp.float32)], axis=0).astype(jnp.bfloat16)
        vT[HD:, here] = jnp.concatenate([ones, lane_zero((48, ROWS), jnp.float32)], axis=0).astype(jnp.bfloat16)
        q = tt_ref[0, :HD, here].astype(jnp.float32)
        k = tt_ref[0, HD:2 * HD, here].astype(jnp.float32)
        v = tt_ref[0, 2 * HD:, here].astype(jnp.float32)
        do = dot_ref[:, here].astype(jnp.float32)
        delta = jnp.sum(do * ctx_ref[:, here].astype(jnp.float32), axis=0, keepdims=True)
        lse = lse_ref[0, :, here]
        parts = jnp.concatenate([-x for x in split3(lse)], axis=0)
        rest = jnp.concatenate([jnp.where(member, 1.0, 0.0), parts, lane_zero((13, ROWS), jnp.float32)], axis=0)
        qfull[here, :128] = qx_ref[0, here, :]
        qfull[here, 128:160] = jnp.transpose(rest.astype(jnp.bfloat16))
        parts = jnp.concatenate([-x for x in split3(delta)], axis=0)
        rest = jnp.concatenate([do, parts, lane_zero((13, ROWS), jnp.float32)], axis=0)
        dofull[here, :80] = jnp.transpose(rest.astype(jnp.bfloat16))
        p = jnp.where(dead, jnp.exp2(jnp.sum(q * k, axis=0, keepdims=True) * (LOG2E / math.sqrt(HD)) - lse), 0.0)
        ds = p * (jnp.sum(do * v, axis=0, keepdims=True) - delta)
        dk[:, here] = ds * q
        dv[:, here] = p * do
        grad_ref[:HD, here] = (ds * k).astype(jnp.bfloat16)

    @pl.loop(0, blocks)
    def _(i):
        first = pl.multiple_of(i * ROWS, ROWS)
        here = pl.ds(first, ROWS)
        low, high = key_range(len_ref, slots, first, first + ROWS - 1, live_end)

        def step(begin, count, dq):
            keys = [pl.ds(begin + u, min(count, 512)) for u in range(0, count, 512)]
            scores = [dot(qfull[here, :], kT[:, key]) for key in keys]
            backs = [dot(dofull[here, :], vT[:, key]) for key in keys]
            for key, score, back in zip(keys, scores, backs):
                p = jnp.exp2(score)
                ds = (p * back).astype(jnp.bfloat16)
                dv[:, key] += dot(dot_ref[:, here], p.astype(jnp.bfloat16))
                dk[:, key] += dot(tt_ref[0, :HD, here], ds)
                dq = dq + dot(ds, kx_ref[0, key, :])
            return dq

        dq = over_keys(KEYS[:2], low, high, rows, step, jnp.zeros((ROWS, 128), jnp.float32))
        dqT = jnp.transpose(dq)[:HD]
        grad_ref[:HD, here] = ((grad_ref[:HD, here].astype(jnp.float32) + dqT) * (1 / math.sqrt(HD))).astype(jnp.bfloat16)
    grad_ref[HD:2 * HD, :] = (dk[...] * (1 / math.sqrt(HD))).astype(jnp.bfloat16)
    grad_ref[2 * HD:, :] = dv[...].astype(jnp.bfloat16)
    me = lax.axis_index("tensor")
    for owner, part in zip((me, me + 1 - 2 * (me % 2), (me + 2) % n, n - 1 - me), part_refs):
        part[...] = grad_ref[:, pl.ds(pl.multiple_of(owner * quarter, 128), quarter)]
    bias_ref[...] = dot(jnp.ones((8, rows), jnp.bfloat16), grad_ref[...], 1, 1)
    for copy in copies:
        copy.wait()
    gw = jnp.transpose(dot(grad_ref[...], fn[...])).astype(jnp.bfloat16)
    if joined:
        first = joined_refs[0][...]
        if joined == 2:
            packed = joined_refs[1][...]
            wide = first.shape[1]
            packed = jnp.concatenate([packed[:, :wide], packed[:, wide:]], axis=0)
            first = (first.astype(jnp.float32) + packed.astype(jnp.float32)).astype(jnp.bfloat16)
        gw = jnp.concatenate([first, gw], axis=1)
    gw_ref[...] = gw
    for i in range(2 * folds):
        buf = fold_buf[i]
        fold_refs[i][...] = (buf[0].astype(jnp.float32) + buf[1].astype(jnp.float32)).astype(jnp.bfloat16)


def attend_back(head, n, lengths, marks, qx, kx, tt, ctx, lse, do, fn, join=(), held=()):
    rows = tt.shape[2]
    per = lambda *s: pl.BlockSpec((1,) + s, lambda i: (head, 0, 0))
    slab = pl.BlockSpec((HD, rows), lambda i: (head, 0))
    whole = lambda *s: pl.BlockSpec(s, lambda i: (0,) * len(s))
    any_ = pl.BlockSpec(memory_space=pl.ANY)
    vm = pltpu.VMEM
    quarter, feat = rows // n, fn.shape[1]
    folds = 1 if held else 0
    joined = len(join)
    wide = 3 * HD + (join[0].shape[1] if joined else 0)
    pairs = (held[0].shape, held[2].shape[1:]) if held else ()
    return pl.pallas_call(
        functools.partial(bwd_kernel, slots=lengths.shape[0], n=n, folds=folds, joined=joined),
        name="attend_back",
        grid=(1,),
        in_specs=[pl.BlockSpec(memory_space=pltpu.SMEM), whole(*marks.shape), per(rows, 128),
                  per(rows, 128), per(3 * HD, rows), slab, per(1, rows), slab, any_]
        + [whole(*j.shape) for j in join] + [any_] * (4 * folds),
        out_specs=[whole(3 * HD, quarter)] * n + [whole(8, 3 * HD), whole(feat, wide)]
        + [whole(*pair) for pair in pairs],
        out_shape=[jax.ShapeDtypeStruct((3 * HD, quarter), jnp.bfloat16)] * n
        + [jax.ShapeDtypeStruct((8, 3 * HD), jnp.float32), jax.ShapeDtypeStruct((feat, wide), jnp.bfloat16)]
        + [jax.ShapeDtypeStruct(pair, jnp.bfloat16) for pair in pairs],
        scratch_shapes=[vm((3 * HD, rows), jnp.bfloat16), vm((rows, 256), jnp.bfloat16), vm((256, rows), jnp.bfloat16), vm((rows, 128), jnp.bfloat16),
                        vm((128, rows), jnp.bfloat16), vm((HD, rows), jnp.float32), vm((HD, rows), jnp.float32), vm((rows, feat), jnp.bfloat16),
                        pltpu.SemaphoreType.DMA((5,))] + [vm((2,) + pair, jnp.bfloat16) for pair in pairs],
        cost_estimate=pl.CostEstimate(flops=15 * 10**9, bytes_accessed=6 * 2**20, transcendentals=0),
        compiler_params=pltpu.CompilerParams(vmem_limit_bytes=VMEM_LIMIT),
    )(lengths, marks, qx, kx, tt, ctx, lse, do, fn, *join, *held)


GELU_C = math.sqrt(2 / math.pi)
CHUNK = 256


def mid_kernel(tok_ref, ctx_ref, cot_ref, wo_own, wu_own, wd_own, wo_far, far_ref, vec_hbm, mark_ref, vec_ref,
               out_ref, bh_ref, do_ref, upk_ref, ups_ref, dnk_ref, dns_ref, early_ref, og_ref, ogs_ref,
               wo, ws, upb, cx, tok, cot, act, bp, hid, xhat, rstd, acc, bsec, n2, n2T, bf, bfT, atT, bcs, gr, gro, gso, ga, gb, upsum_ref, sums_ref, e_own, e_t, out_buf, bh_buf,
               loc_sem, w_send, w_recv, b_send, b_recv, c_send, c_recv, d_send, d_recv, d_loc, g_send, g_recv, o_sem, h_sem, es, er, f_sem,
               *, n, dp):
    quarter, feat = cot.shape
    width = ctx_ref.shape[0]
    chunks = quarter // CHUNK
    wu, wd = ws.at[0], ws.at[1]
    me = lax.axis_index("tensor")
    dp_me = lax.axis_index("dp")
    mesh_id = pl.DeviceIdType.MESH

    def other(r):
        return (me, me + 1 - 2 * (me % 2), (me + 2) % n, n - 1 - me)[r]

    def peer(r):
        return {"tensor": other(r)}

    def cols(owner, c):
        return pl.ds(pl.multiple_of(owner * quarter + c * CHUNK, CHUNK), CHUNK)

    def by_low(ref, columns, value):
        low_count, size = 2, value.shape[0] // dp
        for p in range(dp):
            q = p % low_count * (dp // low_count) + p // low_count
            ref[q * size:(q + 1) * size, columns] = value[p * size:(p + 1) * size]

    barrier = pltpu.get_barrier_semaphore()
    for r in range(1, n):
        pl.semaphore_signal(barrier, inc=1, device_id=peer(r), device_id_type=mesh_id)
    x_peer = {"dp": dp_me + 1 - 2 * (dp_me % 2)}
    z_peer = {"dp": dp_me + 2 - 4 * (dp_me // 2 % 2)}
    for device in (x_peer, z_peer):
        pl.semaphore_signal(barrier, inc=1, device_id=device, device_id_type=mesh_id)
    pl.semaphore_wait(barrier, n + 1)

    ctx_copies = {}
    for c in range(chunks):
        for r in (2, 3, 1):
            ctx_copies[c, r] = pltpu.make_async_remote_copy(
                src_ref=ctx_ref.at[:, cols(other(r), c)],
                dst_ref=cx.at[pl.ds(r * width, width), pl.ds(c * CHUNK, CHUNK)],
                send_sem=c_send.at[c * n + r], recv_sem=c_recv.at[c * n + r],
                device_id=peer(r), device_id_type=mesh_id)
    for r in (2, 3, 1):
        ctx_copies[0, r].start()
    own_ctx = pltpu.make_async_copy(
        ctx_ref.at[:, pl.ds(pl.multiple_of(me * quarter, CHUNK), quarter)], cx.at[pl.ds(0, width), :], loc_sem.at[0])
    rows_here = pl.ds(pl.multiple_of(me * quarter, CHUNK), quarter)
    tok_copy = pltpu.make_async_copy(tok_ref.at[rows_here, :], tok, loc_sem.at[1])
    cot_copy = pltpu.make_async_copy(cot_ref, cot, loc_sem.at[2])
    hidden_units = wd_own.shape[0]
    local, remote = {}, {}
    for i, (own, buf) in enumerate(((wo_own, wo), (wu_own, wu), (wd_own, wd))):
        size = own.shape[0]
        for r, src in ((0, own), (2, wo_far))[:2 if i == 0 else 1]:
            local[i, r] = pltpu.make_async_copy(src, buf.at[pl.ds(r * size, size), :], loc_sem.at[3 + 2 * i + r // 2])
            remote[i, r + 1] = pltpu.make_async_remote_copy(
                src_ref=src, dst_ref=buf.at[pl.ds((r + 1) * size, size), :], send_sem=w_send.at[2 * i + r // 2],
                recv_sem=w_recv.at[2 * i + r // 2], device_id=peer(1), device_id_type=mesh_id)
    have = (dp_me % 2 + dp_me // 2) % 2
    lack = 1 - have
    slot = lambda r, first, count: pl.ds(r * feat + first, count)
    held_here = pltpu.make_async_copy(far_ref, ws.at[have, slot(2, 0, feat), :], loc_sem.at[6])
    held_beside = pltpu.make_async_remote_copy(
        src_ref=far_ref, dst_ref=ws.at[have, slot(3, 0, feat), :], send_sem=w_send.at[3], recv_sem=w_recv.at[3],
        device_id=peer(1), device_id_type=mesh_id)
    part = feat // 2
    lacked = [
        pltpu.make_async_remote_copy(
            src_ref=far_ref.at[pl.ds(i * part, part), :], dst_ref=ws.at[have, slot(2, i * part, part), :],
            send_sem=h_sem.at[2 * i], recv_sem=h_sem.at[2 * i + 1], device_id=device, device_id_type=mesh_id)
        for i, device in enumerate((x_peer, z_peer))
    ]
    beside = pltpu.make_async_remote_copy(
        src_ref=ws.at[lack, slot(2, 0, feat), :], dst_ref=ws.at[lack, slot(3, 0, feat), :], send_sem=w_send.at[5],
        recv_sem=w_recv.at[5], device_id=peer(1), device_id_type=mesh_id)
    bias_copies = []
    for r in range(1, n):
        copy = pltpu.make_async_remote_copy(
            src_ref=vec_hbm, dst_ref=upb.at[r], send_sem=b_send.at[r], recv_sem=b_recv.at[r],
            device_id=peer(r), device_id_type=mesh_id)
        copy.start()
        bias_copies.append(copy)
    own_bias = pltpu.make_async_copy(vec_hbm, upb.at[0], loc_sem.at[9])
    own_ctx.start()
    tok_copy.start()
    cot_copy.start()
    own_bias.start()
    for copy in (*local.values(), *remote.values(), *lacked, held_here, held_beside):
        copy.start()

    live_col = column(mark_ref[0:1, rows_here])
    flag_col = column(mark_ref[1:2, rows_here])
    cot_copy.wait()
    masked = jnp.where(live_col == 1.0, cot[...], jnp.zeros((), jnp.bfloat16))
    bf[...] = masked
    by_low(bfT, slice(None), jnp.transpose(masked))
    sums_ref[...] = jnp.zeros(sums_ref.shape, jnp.float32)
    sums_ref[3:4] = jnp.sum(masked.astype(jnp.float32), axis=0, keepdims=True)
    tok_copy.wait()
    own_ctx.wait()
    own_bias.wait()
    for copy in bias_copies:
        copy.wait()
    gain = vec_ref[4:5]
    shift = vec_ref[5:6]
    upsum_ref[...] = jnp.zeros(upsum_ref.shape, jnp.float32)

    def feed(c, first, count):
        here = pl.ds(c * CHUNK, CHUNK)

        @pl.loop(first, first + count)
        def _(r):
            up = wu.at[pl.ds(pl.multiple_of(r * feat, feat), feat), :]
            down = wd.at[pl.ds(pl.multiple_of(r * hidden_units, hidden_units), hidden_units), :]
            pre = dot(n2[here, :], up[...]) + upb[r, 7:8, :]
            square = pre * pre
            t = jnp.tanh(pre * (square * (GELU_C * 0.044715) + GELU_C))
            half = 0.5 * t + 0.5
            a = pre * half
            slope = half + a * (1.0 - t) * (square * (3 * GELU_C * 0.044715) + GELU_C)
            low = a.astype(jnp.bfloat16)
            act[r, here, :] = low
            back = (dot(bf[here, :], down[...], 1, 1) * slope).astype(jnp.bfloat16)
            bp[r, here, :] = back
            upsum_ref[r, :1, :] += jnp.sum(back.astype(jnp.float32), axis=0, keepdims=True)
            acc[here, :] += dot(low, down[...])
            bsec[here, :] += dot(back, up[...], 1, 1)

    for c in range(chunks):
        for r in (2, 3, 1):
            ctx_copies[c, r].wait_send()
        if c + 1 < chunks:
            for r in (2, 3, 1):
                ctx_copies[c + 1, r].start()
        for r in (2, 3, 1):
            ctx_copies[c, r].wait_recv()
        if c == 0:
            for r in (0, 2):
                local[0, r].wait()
                remote[0, r + 1].wait()
        here = pl.ds(c * CHUNK, CHUNK)
        flag_c = flag_col[c * CHUNK:(c + 1) * CHUNK]
        x = jnp.where(flag_c == 1.0, vec_ref[0:1], tok[here, :].astype(jnp.float32))
        hidden = x + dot(cx[:, here], wo[...], 0, 0) + vec_ref[3:4]
        hid[here, :] = hidden
        sent = hidden.astype(jnp.bfloat16).astype(jnp.float32)
        centred = sent - jnp.mean(sent, axis=1, keepdims=True)
        scale = lax.rsqrt(jnp.mean(centred * centred, axis=1, keepdims=True) + EPS)
        normed = centred * scale
        xhat[here, :] = normed
        rstd[here, :] = jnp.broadcast_to(scale, (CHUNK, 128))
        second = (normed * gain + shift).astype(jnp.bfloat16)
        n2[here, :] = second
        n2T[:, here] = jnp.transpose(second)
        acc[here, :] = jnp.zeros((CHUNK, feat), jnp.float32)
        bsec[here, :] = jnp.zeros((CHUNK, feat), jnp.float32)
        if c == 0:
            for r, copies in ((0, local), (1, remote)):
                for i in (1, 2):
                    copies[i, r].wait()
                feed(c, r, 1)
        else:
            feed(c, 0, n // 2)
    for copy in (held_here, held_beside, *lacked):
        copy.wait()
    beside.start()
    grad_copies = {}

    def send_grad(i, k, src, dst):
        copy = pltpu.make_async_remote_copy(
            src_ref=src, dst_ref=dst, send_sem=g_send.at[3 * i + k], recv_sem=g_recv.at[3 * i + k],
            device_id=peer(1), device_id_type=mesh_id)
        copy.start()
        grad_copies[i, k] = copy

    def neighbour_grads(i, r):
        for k, (first, second) in enumerate(((n2T, bp), (bfT, act))):
            place = wd.at[pl.ds((2 * i + k) * feat, feat), :]
            place[...] = dot(first[...], second[r]).astype(jnp.bfloat16)
            send_grad(i, k, place, gr.at[2 * i + k])

    neighbour_grads(0, 1)
    beside.wait()

    bctx_copies = []
    for c in range(chunks):
        feed(c, n // 2, n // 2)
        here = pl.ds(c * CHUNK, CHUNK)
        live_c = live_col[c * CHUNK:(c + 1) * CHUNK]
        ffn = (acc[here, :] + vec_ref[6:7]).astype(jnp.bfloat16).astype(jnp.float32)
        out_buf[here, :] = (hid[here, :] + jnp.where(live_c == 1.0, ffn, 0.0)).astype(jnp.bfloat16)
        back = bsec[here, :]
        normed = xhat[here, :]
        sums_ref[0:1] += jnp.sum(back * normed, axis=0, keepdims=True)
        sums_ref[1:2] += jnp.sum(back, axis=0, keepdims=True)
        m = back * gain
        back_sent = rstd[here, :1] * (
            m - jnp.mean(m, axis=1, keepdims=True) - normed * jnp.mean(m * normed, axis=1, keepdims=True))
        back_hidden = cot[here, :].astype(jnp.float32) + back_sent.astype(jnp.bfloat16).astype(jnp.float32)
        bh_buf[here, :] = back_hidden
        for k, (src, dst) in enumerate(((out_buf, out_ref), (bh_buf, bh_ref))):
            copy = pltpu.make_async_copy(src.at[here, :], dst.at[here, :], f_sem.at[2 * c + k])
            copy.start()
            bctx_copies.append(copy)
        attn = back_hidden.astype(jnp.bfloat16)
        sums_ref[2:3] += jnp.sum(attn.astype(jnp.float32), axis=0, keepdims=True)
        atT[:, here] = jnp.transpose(attn)
        bcs[:, here] = dot(wo[...], attn, 1, 1).astype(jnp.bfloat16)
        for r in (2, 3, 1):
            copy = pltpu.make_async_remote_copy(
                src_ref=bcs.at[pl.ds(r * width, width), pl.ds(c * CHUNK, CHUNK)],
                dst_ref=do_ref.at[:, cols(me, c)],
                send_sem=d_send.at[c * n + r], recv_sem=d_recv.at[c * n + r],
                device_id=peer(r), device_id_type=mesh_id)
            copy.start()
            bctx_copies.append(copy)
        copy = pltpu.make_async_copy(
            bcs.at[pl.ds(0, width), pl.ds(c * CHUNK, CHUNK)], do_ref.at[:, cols(me, c)], d_loc.at[c])
        copy.start()
        bctx_copies.append(copy)

    rows = [sums_ref[i:i + 1] for i in range(4)]
    for i in range(n):
        row = jnp.zeros((1, hidden_units), jnp.float32)
        for r in range(n):
            row = jnp.where(other(r) == i, upsum_ref[r, :1, :], row)
        rows.append(row)
    e_own[...] = jnp.zeros(e_own.shape, jnp.float32)
    share = -(-len(rows) // n)
    for i, row in enumerate(rows):
        e_own[i // share, i % share:i % share + 1] = row
    e_copies = []
    for r in range(1, n):
        copy = pltpu.make_async_remote_copy(src_ref=e_own.at[other(r)], dst_ref=e_t.at[r], send_sem=es.at[r], recv_sem=er.at[r],
                                            device_id=peer(r), device_id_type=mesh_id)
        copy.start()
        e_copies.append(copy)

    out_grad = lambda r: dot(atT[...], cx[r * width:(r + 1) * width, :], 1, 1)
    gso[...] = jnp.concatenate([out_grad(1), out_grad(3)], axis=1).astype(jnp.bfloat16)
    beside_out = pltpu.make_async_remote_copy(
        src_ref=gso, dst_ref=gro, send_sem=g_send.at[2], recv_sem=g_recv.at[2], device_id=peer(1), device_id_type=mesh_id)
    beside_out.start()
    neighbour_grads(1, 3)
    half = feat // 2
    low = dp_me % 2
    mine = pl.ds(pl.multiple_of(low * half, half), half)
    other_half = pl.ds(pl.multiple_of((1 - low) * half, half), half)
    for i, r in ((0, 0), (1, 2)):
        for k in range(2):
            grad_copies[i, k].wait()
        if i == 1:
            near_grad = out_grad(0)
            far_grad = out_grad(2)
            beside_out.wait()
            far_grad = far_grad + gro[:, width:].astype(jnp.float32)
            ogs_ref[...] = jnp.concatenate([far_grad[:half], far_grad[half:]], axis=1).astype(jnp.bfloat16)
            og_ref[...] = (near_grad + gro[:, :width].astype(jnp.float32)).astype(jnp.bfloat16)
        for buf, first, second, slot in ((ga, n2T, bp, 2 * i), (gb, bfT, act, 2 * i + 1)):
            buf[i] = (dot(first[...], second[r]) + gr[slot].astype(jnp.float32)).astype(jnp.bfloat16)
        for k, (src, dst) in enumerate(((ga.at[i], (upk_ref, ups_ref)[i]), (gb.at[i, mine, :], dnk_ref.at[i]),
                                        (gb.at[i, other_half, :], dns_ref.at[i]))):
            copy = pltpu.make_async_copy(src, dst, o_sem.at[4 * i + k])
            copy.start()
            bctx_copies.append(copy)
    total = e_own[me]
    for r, copy in enumerate(e_copies):
        copy.wait()
        total = total + e_t[r + 1]
    early_ref[...] = total
    for copy in bctx_copies:
        copy.wait()


def middle(n, dp, tokens, ctx, cotangent, own, out_far, far, marks, vectors):
    quarter, feat = cotangent.shape
    width, rows = ctx.shape
    hidden_units = own[1].shape[1]
    vm, any_, vmem = pltpu.VMEM, pl.BlockSpec(memory_space=pl.ANY), pl.BlockSpec(memory_space=pltpu.VMEM)
    bf16, f32 = jnp.bfloat16, jnp.float32
    chunks = quarter // CHUNK
    sem = pltpu.SemaphoreType.DMA
    flops = 2 * quarter * feat * (6 * n * hidden_units + 3 * n * width)
    wide = hidden_units
    grads = [jax.ShapeDtypeStruct(s, bf16) for s in (
        (feat, wide), (feat, wide), (2, feat // 2, wide), (2, feat // 2, wide))]
    return pl.pallas_call(
        functools.partial(mid_kernel, n=n, dp=dp),
        name="middle",
        in_specs=[any_] * 9 + [vmem] * 2,
        out_specs=[any_] * 7 + [vmem] * 3,
        out_shape=[jax.ShapeDtypeStruct((quarter, feat), bf16), jax.ShapeDtypeStruct((quarter, feat), f32),
                   jax.ShapeDtypeStruct((width, rows), bf16)] + grads + [
                   jax.ShapeDtypeStruct((8, feat), f32), jax.ShapeDtypeStruct((feat, width), bf16),
                   jax.ShapeDtypeStruct((feat // 2, 2 * width), bf16)],
        scratch_shapes=[
            vm((n * width, feat), bf16), vm((2, n * feat, hidden_units), bf16),
            vm((n, 8, hidden_units), f32), vm((n * width, quarter), bf16), vm((quarter, feat), bf16), vm((quarter, feat), bf16),
            vm((n, quarter, hidden_units), bf16), vm((n, quarter, hidden_units), bf16),
            vm((quarter, feat), f32), vm((quarter, feat), f32), vm((quarter, 128), f32), vm((quarter, feat), f32),
            vm((quarter, feat), f32), vm((quarter, feat), bf16), vm((feat, quarter), bf16), vm((quarter, feat), bf16),
            vm((feat, quarter), bf16), vm((feat, quarter), bf16), vm((n * width, quarter), bf16),
            vm((4, feat, hidden_units), bf16), vm((feat, 2 * width), bf16), vm((feat, 2 * width), bf16),
            vm((2, feat, wide), bf16), vm((2, feat, wide), bf16),
            vm((n, 8, hidden_units), f32), vm((8, feat), f32), vm((n, 8, feat), f32), vm((n, 8, feat), f32),
            vm((quarter, feat), bf16), vm((quarter, feat), f32),
            sem((10,)), sem((6,)), sem((6,)), sem((n,)), sem((n,)), sem((chunks * n,)), sem((chunks * n,)),
            sem((chunks * n,)), sem((chunks * n,)), sem((chunks,)), sem((6,)), sem((6,)), sem((8,)), sem((4,)), sem((n,)), sem((n,)), sem((2 * chunks,)),
        ],
        cost_estimate=pl.CostEstimate(flops=flops, bytes_accessed=40 * 2**20, transcendentals=0),
        compiler_params=pltpu.CompilerParams(vmem_limit_bytes=60 * 2**20, collective_id=0, has_side_effects=True),
    )(tokens, ctx, cotangent, *own, out_far, far, vectors, marks, vectors)


def fin_kernel(early_blocks, last_blocks, gw_refs, b_refs, sum_refs, wT_own, wT_far, bh_ref, tok_ref, mark_ref, vec_ref, e_part,
               grad_ref, qkv_ref, up_ref, down_ref, early_ref, late_ref,
               wall, blk, bh, tok, acc, gw_mine, gw_x, gw_z, ups, up_send, up_in, parts, big, big_z, e_dp, l_own, l_t, l_dp,
               loc_sem, w_send, w_recv, a_send, a_recv, x_send, x_recv, p_send, p_recv, b_send, b_recv, u_sem, fs, fr, hs, hr, ls, lr, ms, mr, r_sem, *, n, dp):
    quarter, feat = acc.shape
    heads = len(b_refs)
    part = last_blocks[0].shape[0]
    chunks = quarter // CHUNK
    me = lax.axis_index("tensor")
    dp_me = lax.axis_index("dp")
    mesh_id = pl.DeviceIdType.MESH

    def other(r):
        return (me, me + 1 - 2 * (me % 2), (me + 2) % n, n - 1 - me)[r]

    def peer(r):
        return {"tensor": other(r)}

    def dp_peer(d):
        return {"dp": (dp_me + d) % dp}

    barrier = pltpu.get_barrier_semaphore()
    for r in range(1, n):
        pl.semaphore_signal(barrier, inc=1, device_id=peer(r), device_id_type=mesh_id)
    for d in range(1, dp):
        pl.semaphore_signal(barrier, inc=1, device_id=dp_peer(d), device_id_type=mesh_id)
    pl.semaphore_wait(barrier, n + dp - 2)

    last = heads - 1
    arrivals = {}
    for c in range(chunks):
        here = pl.ds(c * CHUNK, CHUNK)
        for r in (2, 3, 1):
            copy = pltpu.make_async_remote_copy(
                src_ref=last_blocks[r].at[:, here], dst_ref=blk.at[pl.ds((last * n + r) * part, part), here],
                send_sem=a_send.at[c * n + r], recv_sem=a_recv.at[c * n + r], device_id=peer(r), device_id_type=mesh_id)
            arrivals[c, r] = copy

    def ask(c):
        for r in (2, 3, 1):
            arrivals[c, r].start()

    ask(0)
    e_dp[0] = e_part[...]
    f_copies = []
    for d in range(1, dp):
        copy = pltpu.make_async_remote_copy(src_ref=e_dp.at[0], dst_ref=e_dp.at[d], send_sem=fs.at[d], recv_sem=fr.at[d],
                                            device_id=dp_peer(d), device_id_type=mesh_id)
        copy.start()
        f_copies.append(copy)
    waits = []
    sem = iter(range(loc_sem.shape[0]))
    low_count = 2
    high_count = dp // low_count
    low, high = dp_me % low_count, dp_me // low_count
    x_peer = {"dp": dp_me + 1 - 2 * low}
    part_copies = []
    for i, ref in enumerate(sum_refs):
        copy = pltpu.make_async_copy(
            ref if len(ref.shape) != 3 or i == 0 else ref.at[0], ups if i == 0 else parts.at[i - 1], loc_sem.at[next(sem)])
        copy.start()
        part_copies.append(copy)
    x_copies = []
    for k, ref in enumerate(gw_refs):
        copy = pltpu.make_async_remote_copy(
            src_ref=ref.at[:, 1 - low], dst_ref=gw_x.at[k], send_sem=x_send.at[k], recv_sem=x_recv.at[k],
            device_id=x_peer, device_id_type=mesh_id)
        copy.start()
        x_copies.append(copy)
        copy = pltpu.make_async_copy(ref.at[:, low], gw_mine.at[k], loc_sem.at[next(sem)])
        copy.start()
        x_copies.append(copy)
    for h in range(heads):
        for r, src in ((0, wT_own), (2, wT_far)):
            rows = src.at[pl.ds(h * part, part), :]
            copy = pltpu.make_async_copy(rows, wall.at[pl.ds((h * n + r) * part, part), :], loc_sem.at[next(sem)])
            copy.start()
            waits.append(copy)
            copy = pltpu.make_async_remote_copy(
                src_ref=rows, dst_ref=wall.at[pl.ds((h * n + r + 1) * part, part), :], send_sem=w_send.at[2 * h + r // 2],
                recv_sem=w_recv.at[2 * h + r // 2], device_id=peer(1), device_id_type=mesh_id)
            copy.start()
            waits.append(copy)
    pieces = [(last_blocks[0], last, 0)]
    pieces += [(early_blocks[h * n + r], h, r) for r in range(n) for h in range(last)]
    for src, h, r in pieces:
        copy = pltpu.make_async_copy(src, blk.at[pl.ds((h * n + r) * part, part), :], loc_sem.at[next(sem)])
        copy.start()
        waits.append(copy)
    rows_here = pl.ds(pl.multiple_of(me * quarter, CHUNK), quarter)
    for src, dst in ((bh_ref, bh), (tok_ref.at[rows_here, :], tok)):
        copy = pltpu.make_async_copy(src, dst, loc_sem.at[next(sem)])
        copy.start()
        waits.append(copy)

    for copy in part_copies:
        copy.wait()
    size = parts.shape[1] // high_count
    total = sum(parts[i].astype(jnp.float32) for i in range(3)).astype(jnp.bfloat16)
    for z in range(high_count):
        big[z] = total[z * size:(z + 1) * size]
    b_copies = []
    for d in range(1, high_count):
        copy = pltpu.make_async_remote_copy(
            src_ref=big.at[(high + d) % high_count], dst_ref=big_z.at[d], send_sem=b_send.at[d], recv_sem=b_recv.at[d],
            device_id={"dp": (dp_me + d * low_count) % dp}, device_id_type=mesh_id)
        copy.start()
        b_copies.append(copy)
    total = sum(ups[z].astype(jnp.float32) for z in range(high_count)).astype(jnp.bfloat16)
    for x in range(low_count):
        up_send[x] = total[x * size:(x + 1) * size]
    up_copy = pltpu.make_async_remote_copy(
        src_ref=up_send.at[1 - low], dst_ref=up_in, send_sem=u_sem.at[0], recv_sem=u_sem.at[1], device_id=x_peer,
        device_id_type=mesh_id)
    up_copy.start()
    rows = []
    zero = lambda k: [jnp.zeros((1, k), jnp.float32)] if k else []
    for k in (0, 2):
        piece = jnp.concatenate([ref[:1, k * HD:(k + 1) * HD] for ref in b_refs], axis=1)
        size = piece.shape[1]
        total = jnp.zeros((1, feat), jnp.float32)
        for i in range(n):
            placed = jnp.concatenate(zero(i * size) + [piece] + zero((n - 1 - i) * size), axis=1)
            total = jnp.where(me == i, placed, total)
        rows.append(total)

    for copy in waits:
        copy.wait()
    first = last * n * part
    for c in range(chunks):
        here = pl.ds(c * CHUNK, CHUNK)
        acc[here, :] = dot(blk[:first, here], wall[:first], 0, 0)
        if c == 0 and chunks > 1:
            ask(1)
    for copy in x_copies:
        copy.wait()
    gw_mine[...] = (gw_mine[...].astype(jnp.float32) + gw_x[...].astype(jnp.float32)).astype(jnp.bfloat16)
    z_copies = []
    for d in range(1, high_count):
        copy = pltpu.make_async_remote_copy(
            src_ref=gw_mine.at[:, (high + d) % high_count], dst_ref=gw_z.at[d], send_sem=p_send.at[d], recv_sem=p_recv.at[d],
            device_id={"dp": (dp_me + d * low_count) % dp}, device_id_type=mesh_id)
        copy.start()
        z_copies.append(copy)

    flag_col = column(mark_ref[1:2, rows_here])
    emb = vec_ref[0:1]
    gain = vec_ref[1:2]
    results = []
    mask_sum = jnp.zeros((1, feat), jnp.float32)
    gain_sum = jnp.zeros((1, feat), jnp.float32)
    bias_sum = jnp.zeros((1, feat), jnp.float32)
    for c in range(chunks):
        here = pl.ds(c * CHUNK, CHUNK)
        flag = flag_col[c * CHUNK:(c + 1) * CHUNK] == 1.0
        for r in (2, 3, 1):
            arrivals[c, r].wait()
        if c + 2 < chunks:
            ask(c + 2)
        back = acc[here, :] + dot(blk[first:, here], wall[first:], 0, 0)
        x = jnp.where(flag, emb, tok[here, :].astype(jnp.float32))
        centred = x - jnp.mean(x, axis=1, keepdims=True)
        scale = lax.rsqrt(jnp.mean(centred * centred, axis=1, keepdims=True) + EPS)
        normed = centred * scale
        gain_sum += jnp.sum(back * normed, axis=0, keepdims=True)
        bias_sum += jnp.sum(back, axis=0, keepdims=True)
        m = back * gain
        back_in = bh[here, :] + scale * (
            m - jnp.mean(m, axis=1, keepdims=True) - normed * jnp.mean(m * normed, axis=1, keepdims=True))
        acc[here, :] = jnp.where(flag, 0.0, back_in)
        copy = pltpu.make_async_copy(acc.at[here, :], grad_ref.at[here, :], r_sem.at[c])
        copy.start()
        results.append(copy)
        mask_sum += jnp.sum(jnp.where(flag, back_in, 0.0), axis=0, keepdims=True)

    l_own[...] = jnp.zeros(l_own.shape, jnp.float32)
    lanes = feat // 128
    for i, row in enumerate((mask_sum, gain_sum, bias_sum, *rows)):
        for j in range(lanes):
            l_own[i * lanes + j:i * lanes + j + 1] = row[:, j * 128:(j + 1) * 128]
    l_copies = []
    for r in range(1, n):
        copy = pltpu.make_async_remote_copy(src_ref=l_own, dst_ref=l_t.at[r], send_sem=ls.at[r], recv_sem=lr.at[r],
                                            device_id=peer(r), device_id_type=mesh_id)
        copy.start()
        l_copies.append(copy)
    total = e_dp[0]
    for d, copy in enumerate(f_copies):
        copy.wait()
        total = total + e_dp[d + 1]
    early_ref[me] = total
    h_copies = []
    for r in range(1, n):
        copy = pltpu.make_async_remote_copy(src_ref=early_ref.at[me], dst_ref=early_ref.at[me], send_sem=hs.at[r],
                                            recv_sem=hr.at[r], device_id=peer(r), device_id_type=mesh_id)
        copy.start()
        h_copies.append(copy)
    total = l_own[...]
    for r, copy in enumerate(l_copies):
        copy.wait()
        total = total + l_t[r + 1]
    l_dp[0] = total
    m_copies = []
    for d in range(1, dp):
        copy = pltpu.make_async_remote_copy(src_ref=l_dp.at[0], dst_ref=l_dp.at[d], send_sem=ms.at[d], recv_sem=mr.at[d],
                                            device_id=dp_peer(d), device_id_type=mesh_id)
        copy.start()
        m_copies.append(copy)
    up_copy.wait()
    up_ref[...] = up_send[low].astype(jnp.float32) + up_in[...].astype(jnp.float32)
    for copies, mine, arrived, out in ((b_copies, big[high], big_z, down_ref), (z_copies, gw_mine[:, high], gw_z, qkv_ref)):
        total = mine.astype(jnp.float32)
        for d, copy in enumerate(copies):
            copy.wait()
            total = total + arrived[d + 1].astype(jnp.float32)
        out[...] = total
    for copy in h_copies:
        copy.wait()
    total = l_dp[0]
    for d, copy in enumerate(m_copies):
        copy.wait()
        total = total + l_dp[d + 1]
    late_ref[...] = total
    for copy in results:
        copy.wait()


def finish(n, dp, early_blocks, last_blocks, gws, biases, sums, wT_own, wT_far, back_hidden, tokens, marks, vectors, early):
    quarter, feat = back_hidden.shape
    part = last_blocks[0].shape[0]
    heads = len(biases)
    chunks = quarter // CHUNK
    vm, any_, vmem = pltpu.VMEM, pl.BlockSpec(memory_space=pl.ANY), pl.BlockSpec(memory_space=pltpu.VMEM)
    bf16, f32 = jnp.bfloat16, jnp.float32
    sem = pltpu.SemaphoreType.DMA
    late_rows = -(-5 * (feat // 128) // 8) * 8
    share = early.shape[0]
    count, size = dp // 2, feat // dp
    half, units = sums[3].shape
    kinds = len(gws)
    wide = gws[0].shape[1]
    gws = [g.reshape(count, 2, size, wide) for g in gws]
    early_blocks = [b for blocks in early_blocks for b in blocks]

    def body(*refs):
        cut = [len(early_blocks), n, kinds, heads, len(sums)]
        groups = []
        for width in cut:
            groups.append(refs[:width])
            refs = refs[width:]
        fin_kernel(*groups, *refs, n=n, dp=dp)

    return pl.pallas_call(
        body,
        name="finish",
        in_specs=[any_] * (len(early_blocks) + n + kinds) + [vmem] * heads + [any_] * (len(sums) + 4) + [vmem] * 3,
        out_specs=[any_] + [vmem] * 5,
        out_shape=[jax.ShapeDtypeStruct((quarter, feat), f32), jax.ShapeDtypeStruct((kinds, size, wide), f32),
                   jax.ShapeDtypeStruct((size, units), f32), jax.ShapeDtypeStruct((size, units), f32), jax.ShapeDtypeStruct((n, share, feat), f32),
                   jax.ShapeDtypeStruct((late_rows, 128), f32)],
        scratch_shapes=[
            vm((heads * n * part, feat), bf16), vm((heads * n * part, quarter), bf16),
            vm((quarter, feat), f32), vm((quarter, feat), bf16), vm((quarter, feat), f32),
            vm((kinds, count, size, wide), bf16), vm((kinds, count, size, wide), bf16), vm((count, kinds, size, wide), bf16),
            vm((count, 2 * size, units), bf16), vm((2, size, units), bf16), vm((size, units), bf16),
            vm((3, half, units), bf16), vm((count, size, units), bf16), vm((count, size, units), bf16),
            vm((dp, share, feat), f32),
            vm((late_rows, 128), f32), vm((n, late_rows, 128), f32), vm((dp, late_rows, 128), f32),
            sem((dp + 40,)), sem((2 * heads,)), sem((2 * heads,)), sem((chunks * n,)), sem((chunks * n,)),
            sem((dp,)), sem((dp,)), sem((dp,)), sem((dp,)), sem((dp,)), sem((dp,)), sem((2,)), sem((dp,)), sem((dp,)), sem((n,)), sem((n,)),
            sem((n,)), sem((n,)), sem((dp,)), sem((dp,)), sem((chunks,)),
        ],
        cost_estimate=pl.CostEstimate(flops=8 * 10**9, bytes_accessed=25 * 2**20, transcendentals=0),
        compiler_params=pltpu.CompilerParams(vmem_limit_bytes=60 * 2**20, collective_id=1, has_side_effects=True),
    )(*early_blocks, *last_blocks, *gws, *biases, *sums, wT_own, wT_far, back_hidden, tokens, marks, vectors, early)


def pack_kernel(early_ref, late_ref, qkv_ref, up_ref, down_ref, q_out, k_out, v_out, up_out, down_out, out_out, *vec_refs):
    heads = q_out.shape[1] // HD
    part = 3 * HD
    places = [(0, 0), (0, part), (1, part)]
    for n, out in enumerate((q_out, k_out, v_out)):
        for h in range(heads):
            out[:, h * HD:(h + 1) * HD] = qkv_ref[places[h][0], :, places[h][1] + n * HD:places[h][1] + (n + 1) * HD]
    units = up_out.shape[1]
    up_out[...] = up_ref[...]
    down_out[...] = down_ref[...]
    out_out[...] = jnp.transpose(qkv_ref[1, :, :part])
    feat = early_ref.shape[2]
    lanes = feat // 128
    for i in range(5):
        for j in range(lanes):
            vec_refs[i][j * 128:(j + 1) * 128] = late_ref[i * lanes + j, :]
    n = vec_refs[9].shape[0] // units
    share = -(-(4 + n) // n)
    row = lambda i: early_ref[i // share, i % share, :]
    for i in range(4):
        vec_refs[5 + i][...] = row(i)
    for i in range(n):
        vec_refs[9][i * units:(i + 1) * units] = row(4 + i)


def pack(early, late, qkv, up, down, up_units):
    kinds, rows, width = qkv.shape
    width //= 2
    feat = early.shape[2]
    vmem = pl.BlockSpec(memory_space=pltpu.VMEM)
    shape = lambda *s: jax.ShapeDtypeStruct(s, jnp.float32)
    return pl.pallas_call(
        pack_kernel,
        name="pack",
        in_specs=[vmem] * 5,
        out_specs=[vmem] * 16,
        out_shape=[shape(rows, width)] * 3 + [shape(*up.shape), shape(*down.shape), shape(width, rows)]
        + [shape(feat)] * 9 + [shape(up_units)],
        compiler_params=pltpu.CompilerParams(vmem_limit_bytes=VMEM_LIMIT),
    )(early, late, qkv, up, down)


def swap(array, axis, distance):
    return lax.ppermute(array, axis, [(i, i ^ distance) for i in range(lax.axis_size(axis))])


def per_device(
    tokens,
    token_mask,
    masked_flags,
    doc_lengths,
    mask_embedding,
    ln1_gain,
    ln1_bias,
    w_query,
    query_bias,
    w_key,
    w_value,
    value_bias,
    w_out,
    out_bias,
    ln2_gain,
    ln2_bias,
    w_up,
    up_bias,
    w_down,
    down_bias,
    cotangent,
):
    n = lax.axis_size("tensor")
    dp_size = lax.axis_size("dp")
    hidden_units = w_up.shape[1]

    own = (w_out, w_up, w_down)
    dp_me = lax.axis_index("dp")
    odd = (dp_me % 2 + dp_me // 2) % 2 == 1
    far = swap(jnp.where(odd, w_down, w_up), "tensor", 2)
    out_far = swap(w_out, "tensor", 2)
    first_norm, query_pair, key_wide, head_rows, wT, vectors, marks = project(
        doc_lengths, tokens, token_mask, masked_flags,
        (mask_embedding, ln1_gain, ln1_bias, out_bias, ln2_gain, ln2_bias, down_bias, up_bias), (query_bias, value_bias),
        w_query.T, w_key.T, w_value.T,
    )
    wT_far = swap(wT, "tensor", 2)
    context, log_totals = attend(doc_lengths, marks, key_wide, head_rows)
    context, wT_far = lax.optimization_barrier((context, wT_far))
    layer_output, back_hidden, back_context, up_k, up_s, down_k, down_s, early, out_grad, out_send = middle(
        n, dp_size, tokens, context, cotangent, own, out_far, far, marks, vectors
    )

    low_count = 2
    high_count = dp_size // low_count
    along_z = [[z * low_count + x for z in range(high_count)] for x in range(low_count)]

    def back(head, do, join=(), held=()):
        outs = attend_back(
            head, n, doc_lengths, marks, query_pair, key_wide, head_rows, context, log_totals, do, first_norm, join, held
        )
        return outs[:n], *outs[n:]

    def exchange(parts):
        return [parts[0]] + [swap(parts[r], "tensor", r) for r in range(1, n)]

    up_in = swap(up_s, "tensor", 2)
    down_in = swap(down_s, "dp", 1)
    parts, bias0, gw = back(0, back_context)
    parts, out_send = lax.optimization_barrier((parts, out_send))
    out_in = swap(out_send, "tensor", 2)
    blocks0 = exchange(parts)
    parts, bias1, gw01, up, down_s = back(1, back_context, (gw,), (up_k, up_in, down_k, down_in))
    do, blocks0, out_in, parts, up, down_s = lax.optimization_barrier((back_context, blocks0, out_in, parts, up, down_s))
    up = lax.all_to_all(up.reshape(high_count, -1, hidden_units), "dp", 0, 0, axis_index_groups=along_z)
    down_in2 = swap(down_s, "tensor", 2)
    blocks1 = exchange(parts)
    last, bias2, gw2 = back(2, do, (out_grad, out_in))
    input_grad, qkv, up, down, early, late = finish(
        n, dp_size, (blocks0, blocks1), last, (gw01, gw2), (bias0, bias1, bias2),
        (up, down_k, down_in, down_in2), wT, wT_far, back_hidden, tokens, marks, vectors, early,
    )
    (gq, gk, gv, grad_up, grad_down, grad_out, mask_sum, gain1, bias1, q_bias, v_bias, gain2, bias2, o_bias, d_bias,
     u_bias) = pack(early, late, qkv, up, down, n * hidden_units)
    return (layer_output, input_grad, mask_sum, gain1, bias1, gq, q_bias, gk, gv, v_bias, grad_out, o_bias, gain2, bias2,
            grad_up, u_bias, grad_down.T, d_bias)


def solution(mesh):
    in_specs = (
        P("dp", None),
        P("dp"),
        P("dp"),
        P("dp"),
        P(),
        P(),
        P(),
        P(None, "tensor"),
        P("tensor"),
        P(None, "tensor"),
        P(None, "tensor"),
        P("tensor"),
        P("tensor", None),
        P(),
        P(),
        P(),
        P(None, "tensor"),
        P("tensor"),
        P("tensor", None),
        P(),
        P(("dp", "tensor"), None),
    )
    out_specs = (
        P(("dp", "tensor"), None),
        P(("dp", "tensor"), None),
        P(),
        P(),
        P(),
        P("dp", "tensor"),
        P(),
        P("dp", "tensor"),
        P("dp", "tensor"),
        P(),
        P("tensor", "dp"),
        P(),
        P(),
        P(),
        P("dp", "tensor"),
        P(),
        P("tensor", "dp"),
        P(),
    )
    return jax.shard_map(
        per_device, mesh=mesh, in_specs=in_specs, out_specs=out_specs, check_vma=False
    )
```
